512 devices in a mesh: gen: 64 (over y, z), mp: 8 (over x, core).
Axes of the slice: x: 4, y: 4, z: 16, core: 2. Of those that a mesh axis runs over, the one named last changes fastest.
Arguments:
- pre_x: bfloat16 [64, 512, 4096], P('gen', None, 'mp'), may hold values from -6 to 6
- pre_z: bfloat16 [64, 512, 4096], P('gen', None, 'mp'), may hold values from -6 to 6
- pre_bc: bfloat16 [64, 2, 512, 512], P('gen', None, None, 'mp'), may hold values from -2 to 2
- pre_raw: bfloat16 [64, 512, 64], P('gen', None, 'mp'), may hold values from -6 to 6
- prompt_len: int32 [64], P('gen'), may hold values from 1 to 512, as said below
- live_state: bfloat16 [2048, 64, 64, 64], P('gen', 'mp'), may hold values from -6 to 6
- live_conv: bfloat16 [2048, 3, 4096], P('gen', None, 'mp'), may hold values from -6 to 6
- source: int32 [2048], P('gen'), may hold values from 0 to 2047, as said below
- reader: int32 [1024], P('gen'), may hold values from 0 to 63, as said below
- step_xz: bfloat16 [4, 2, 3072, 4096], P(None, None, 'gen', 'mp'), may hold values from -6 to 6
- step_bc: bfloat16 [4, 2, 3072, 512], P(None, None, 'gen', 'mp'), may hold values from -2 to 2
- step_raw: bfloat16 [4, 3072, 64], P(None, 'gen', 'mp'), may hold values from -6 to 6
- decay: float32 [64], P('mp'), may hold values from 0.02 to 2
- dt_bias: float32 [64], P('mp'), may hold values from -4 to 0
- conv_weight: bfloat16 [4, 4096], P(None, 'mp'), may hold values from -3 to 3
- conv_bias: float32 [4096], P('mp'), may hold values from -3 to 3
- skip: float32 [64], P('mp'), may hold values from 0.5 to 1.5
- norm_gain: float32 [4096], P('mp'), may hold values from 0.5 to 1.5
Outputs:
- prefill_out: bfloat16 [64, 512, 4096], P('gen', None, 'mp')
- decode_out: bfloat16 [4, 3072, 4096], P(None, 'gen', 'mp')
The draws below stay inside these ranges and needn't reach their ends.
Inputs may be any that keep to these rules, and one draw needn't show every extreme that they name: source is a permutation; new row i*32 + k takes an old row of slot k, the 32 new rows of one gen index come from 32 different gen indices, so at most one old row of one gen index goes to any one gen index. `reader`: each prompt is continued by exactly 16 rows, on 16 different gen indices; the 16 rows of one gen index continue 16 different prompts. `prompt_len`: one prompt has exactly 512 tokens.
All inputs are finite; a program needn't handle non-finite values.
Results may differ from the reference program's by a relative error of at most 0.006.
Values may be sent and summed in bfloat16 or wider, within the bound.
No kernel may reach another device: no remote copies, remote signals or barrier semaphores. Data moves between devices by JAX's collectives and lax.ppermute only.
A program may use at most 128 MiB of HBM per device.

```python
import math
import jax
import jax.numpy as jnp
from jax import lax

HEADS = 64
HDIM = 64
STATE = 64
NGROUP = 8
CONV = 4
SPAN = 512
GROUP = 16
STEPS = 4
LIVE_DEV = 32
PROMPTS = 64
LIVE = 2048
NEW = 1024
ROWS = 3072
N_GEN = 64


def latin(key, count, width):
    first, second, third = jax.random.split(key, 3)
    outer = jax.random.permutation(first, count)
    inner = jax.random.permutation(second, count)
    offsets = jax.random.permutation(third, count)[:width]
    return (outer, inner, offsets)


def draw_source(key, part):
    key = jax.random.fold_in(key, 11)
    count = LIVE // LIVE_DEV
    outer, inner, offsets = latin(key, count, LIVE_DEV)
    outer_back = jnp.argsort(outer)
    inner_back = jnp.argsort(inner)
    gens = jnp.arange(count)
    slots = jnp.arange(LIVE_DEV)
    anchor = inner_back[(outer_back[gens][:, None] - offsets[None, :]) % count]
    return (anchor * LIVE_DEV + slots[None, :]).reshape(LIVE).astype(jnp.int32)


def draw_reader(key, part):
    key = jax.random.fold_in(key, 23)
    count = NEW // GROUP
    outer, inner, offsets = latin(key, count, GROUP)
    gens = jnp.arange(count)
    prompt = outer[(inner[gens][:, None] + offsets[None, :]) % count]
    return prompt.reshape(NEW).astype(jnp.int32)


def draw_prompt_len(key, part):
    key = jax.random.fold_in(key, 37)
    first, second = jax.random.split(key)
    lengths = jax.random.randint(first, (PROMPTS,), 1, SPAN + 1)
    longest = jax.random.randint(second, (), 0, PROMPTS)
    return lengths.at[longest].set(SPAN).astype(jnp.int32)


def level_of(stream_key, extent, pieces, low, top_value):
    factor_of = 1.0
    for axis_at, shards_of in pieces:
        draws = jax.random.uniform(jax.random.fold_in(jax.random.fold_in(stream_key, 6), axis_at), (shards_of,), jnp.float32, low / len(pieces), top_value / len(pieces))
        factor_of = factor_of * jnp.repeat(jnp.exp(draws), extent[axis_at] // shards_of).reshape((-1,) + (1,) * (len(extent) - 1 - axis_at))
    return factor_of


def normal_values(own_key, dims, deviation, limit, cuts=(), kind=jnp.bfloat16):
    result = deviation * jax.random.normal(own_key, dims, jnp.float32)
    if cuts:
        result = result * level_of(own_key, dims, cuts, -0.22, 0.18)
    return jnp.clip(result, -limit, limit).astype(kind)


def setup_inputs(seed: int = 0) -> dict:
    splits = jax.random.split(jax.random.key(seed), 19)
    return {
        "pre_x": normal_values(splits[0], (PROMPTS, SPAN, HEADS * HDIM), 1.0, 6.0, ((0, 64), (2, 8))),
        "pre_z": normal_values(splits[1], (PROMPTS, SPAN, HEADS * HDIM), 1.0, 6.0, ((0, 64), (2, 8))),
        "pre_bc": normal_values(splits[2], (PROMPTS, 2, SPAN, NGROUP * STATE), 0.35, 2.0, ((0, 64), (3, 8))),
        "pre_raw": normal_values(splits[3], (PROMPTS, SPAN, HEADS), 1.0, 6.0, ((0, 64), (2, 8))),
        "prompt_len": draw_prompt_len(jax.random.fold_in(splits[18], 71), 0),
        "live_state": normal_values(splits[5], (LIVE, HEADS, HDIM, STATE), 1.0, 6.0, ((0, 64), (1, 8))),
        "live_conv": normal_values(splits[6], (LIVE, CONV - 1, HEADS * HDIM), 1.0, 6.0, ((0, 64), (2, 8))),
        "source": draw_source(jax.random.fold_in(splits[18], 71), 0),
        "reader": draw_reader(jax.random.fold_in(splits[18], 71), 0),
        "step_xz": normal_values(splits[9], (STEPS, 2, ROWS, HEADS * HDIM), 1.0, 6.0, ((2, 64), (3, 8))),
        "step_bc": normal_values(splits[10], (STEPS, 2, ROWS, NGROUP * STATE), 0.35, 2.0, ((2, 64), (3, 8))),
        "step_raw": normal_values(splits[11], (STEPS, ROWS, HEADS), 1.0, 6.0, ((1, 64), (2, 8))),
        "decay": jnp.clip(jnp.exp(math.log(2.0) - 4.6051702 * jax.random.uniform(splits[12], (HEADS,), jnp.float32) ** level_of(splits[12], (HEADS,), ((0, 8),), -0.2, 0.2)), 0.02, 2.0),
        "dt_bias": jnp.clip(-4.0 + 4.0 * jax.random.uniform(splits[13], (HEADS,), jnp.float32) ** level_of(splits[13], (HEADS,), ((0, 8),), -0.2, 0.2), -4.0, 0.0),
        "conv_weight": normal_values(splits[14], (CONV, HEADS * HDIM), CONV ** -0.5, 3.0, ((1, 8),)),
        "conv_bias": normal_values(splits[15], (HEADS * HDIM,), 0.5, 3.0, ((0, 8),), jnp.float32),
        "skip": jnp.clip(0.5 + 1.0 * jax.random.uniform(splits[16], (HEADS,), jnp.float32) ** level_of(splits[16], (HEADS,), ((0, 8),), -0.2, 0.2), 0.5, 1.5),
        "norm_gain": jnp.clip(1.0 + 0.1 * jax.random.normal(splits[17], (HEADS * HDIM,), jnp.float32), 0.5, 1.5),
    }


EPS = 1e-05

def gated(y, gate_in, norm_gain):
    g = y * jax.nn.silu(gate_in.astype(jnp.float32))
    power = lax.optimization_barrier(jnp.mean(g * g, axis=-1, keepdims=True))
    return (g * lax.rsqrt(power + EPS) * norm_gain).astype(jnp.bfloat16)

def prefill_prompt(xin, zin, bcin, rawin, length, decay, dt_bias, conv_weight, conv_bias, skip, norm_gain):
    width = HEADS * HDIM
    per_group = HEADS // NGROUP
    padded = jnp.concatenate([jnp.zeros((CONV - 1, width), jnp.bfloat16), xin], 0)
    acc = conv_bias
    for offset in range(CONV):
        acc = acc + padded[offset:offset + SPAN].astype(jnp.float32) * conv_weight[offset].astype(jnp.float32)
    xconv = jax.nn.silu(acc).astype(jnp.bfloat16)
    spots = jnp.arange(SPAN, dtype=jnp.int32)
    dt = jnp.where((spots < length)[:, None], jax.nn.softplus(rawin.astype(jnp.float32) + dt_bias), 0.0)
    cum = jnp.cumsum(dt * -decay, axis=0)
    causal = spots[:, None] >= spots[None, :]
    heads_x = xconv.reshape(SPAN, HEADS, HDIM)
    bmats = bcin[0].reshape(SPAN, NGROUP, STATE)
    cmats = bcin[1].reshape(SPAN, NGROUP, STATE)

    def one_head(head):
        grp = head // per_group
        bmat = lax.dynamic_index_in_dim(bmats, grp, 1, False)
        cmat = lax.dynamic_index_in_dim(cmats, grp, 1, False)
        scores = jnp.dot(cmat, bmat.T, preferred_element_type=jnp.float32)
        rate = lax.dynamic_index_in_dim(cum, head, 1, False)
        stride = lax.dynamic_index_in_dim(dt, head, 1, False)
        gap = jnp.where(causal, rate[:, None] - rate[None, :], -jnp.inf)
        weights = (scores * jnp.exp(gap) * stride[None, :]).astype(jnp.bfloat16)
        xhead = lax.dynamic_index_in_dim(heads_x, head, 1, False)
        yhead = jnp.dot(weights, xhead, preferred_element_type=jnp.float32) + skip[head] * xhead.astype(jnp.float32)
        tail = jnp.exp(rate[-1] - rate) * stride
        state = jnp.dot(xhead.astype(jnp.float32).T, bmat.astype(jnp.float32) * tail[:, None], precision=lax.Precision.HIGHEST)
        return (yhead, state.astype(jnp.bfloat16))
    ys, states = lax.map(one_head, jnp.arange(HEADS, dtype=jnp.int32))
    y = jnp.transpose(ys, (1, 0, 2)).reshape(SPAN, width)
    out = gated(y, zin, norm_gain)
    tail_rows = lax.dynamic_slice_in_dim(padded, length.astype(jnp.int32), CONV - 1, 0)
    return (out, states, tail_rows)

def decode_block(state, conv, xz, bc, raw, decay, dt_bias, conv_weight, conv_bias, skip, norm_gain):
    rows = state.shape[0]
    per_group = HEADS // NGROUP
    results = []
    for step in range(STEPS):
        window = jnp.concatenate([conv, xz[step, 0][:, None]], 1)
        acc = conv_bias
        for offset in range(CONV):
            acc = acc + window[:, offset].astype(jnp.float32) * conv_weight[offset].astype(jnp.float32)
        xconv = jax.nn.silu(acc).astype(jnp.bfloat16)
        conv = window[:, 1:]
        dt = jax.nn.softplus(raw[step].astype(jnp.float32) + dt_bias)
        bexp = jnp.repeat(bc[step, 0].reshape(rows, NGROUP, STATE).astype(jnp.float32), per_group, axis=1)
        cexp = jnp.repeat(bc[step, 1].reshape(rows, NGROUP, STATE).astype(jnp.float32), per_group, axis=1)
        xhead = xconv.reshape(rows, HEADS, HDIM).astype(jnp.float32)
        state = jnp.exp(-dt * decay)[:, :, None, None] * state + (dt[:, :, None] * xhead)[:, :, :, None] * bexp[:, :, None, :]
        y = jnp.einsum('rhpn,rhn->rhp', state, cexp, precision=lax.Precision.HIGHEST) + skip[None, :, None] * xhead
        results.append(gated(y.reshape(rows, HEADS * HDIM), xz[step, 1], norm_gain))
    return jnp.stack(results)

def reference(pre_x, pre_z, pre_bc, pre_raw, prompt_len, live_state, live_conv, source, reader, step_xz, step_bc, step_raw, decay, dt_bias, conv_weight, conv_bias, skip, norm_gain):

    def run_prompt(item):
        xin, zin, bcin, rawin, length = item
        return prefill_prompt(xin, zin, bcin, rawin, length, decay, dt_bias, conv_weight, conv_bias, skip, norm_gain)
    prefill_out, prefix_state, prefix_tail = lax.map(run_prompt, (pre_x, pre_z, pre_bc, pre_raw, prompt_len))
    rows_dev = LIVE_DEV + GROUP
    width = HEADS * HDIM
    xz_blocks = jnp.transpose(step_xz.reshape(STEPS, 2, N_GEN, rows_dev, width), (2, 0, 1, 3, 4))
    bc_blocks = jnp.transpose(step_bc.reshape(STEPS, 2, N_GEN, rows_dev, NGROUP * STATE), (2, 0, 1, 3, 4))
    raw_blocks = jnp.transpose(step_raw.reshape(STEPS, N_GEN, rows_dev, HEADS), (1, 0, 2, 3))

    def run_block(item):
        block, xz, bc, raw = item
        picked = lax.dynamic_slice_in_dim(source, block * LIVE_DEV, LIVE_DEV, 0)
        readers = lax.dynamic_slice_in_dim(reader, block * GROUP, GROUP, 0)
        state = jnp.concatenate([live_state[picked], prefix_state[readers]], 0).astype(jnp.float32)
        conv = jnp.concatenate([live_conv[picked], prefix_tail[readers]], 0)
        return decode_block(state, conv, xz, bc, raw, decay, dt_bias, conv_weight, conv_bias, skip, norm_gain)
    decoded = lax.map(run_block, (jnp.arange(N_GEN, dtype=jnp.int32), xz_blocks, bc_blocks, raw_blocks))
    decode_out = jnp.transpose(decoded, (1, 0, 2, 3)).reshape(STEPS, ROWS, width)
    return (prefill_out, decode_out)
```

```python
import jax
import jax.numpy as jnp
from jax import lax
from jax.experimental import pallas as pl
from jax.experimental.pallas import tpu as pltpu
from jax.sharding import PartitionSpec as P

STATE = 64
EPS = 1e-05
SUB = 8
F32 = jnp.float32
BF16 = jnp.bfloat16
NT = (((1,), (1,)), ((), ()))
TN = (((0,), (0,)), ((), ()))


def iota(shape, dim):
    return lax.broadcasted_iota(jnp.int32, shape, dim)


def mm(a, b):
    return jnp.dot(a, b, preferred_element_type=F32)


def mm_nt(a, b):
    return lax.dot_general(a, b, NT, preferred_element_type=F32)


def onehot(mask):
    return jnp.where(mask, 1.0, 0.0).astype(BF16)


def split2(x):
    hi = x.astype(BF16)
    return hi, (x - hi.astype(F32)).astype(BF16)


def split3(x):
    hi = x.astype(BF16)
    rest = x - hi.astype(F32)
    mid = rest.astype(BF16)
    return hi, mid, (rest - mid.astype(F32)).astype(BF16)


def silu(x):
    return x / (1.0 + jnp.exp(-x))


def softplus(x):
    return jnp.maximum(x, 0.0) + jnp.log1p(jnp.exp(-jnp.abs(x)))


def expander(heads, width):
    return onehot(iota((heads, width), 1) // (width // heads) == iota((heads, width), 0))


def spread(x, expand):
    hi, lo = split2(x)
    return mm(hi, expand) + mm(lo, expand)


def ask_kernel(live_dev, readers, bc_ref, tgt_l_ref, tgt_r_ref, out_ref):
    steps = bc_ref.shape[0]
    slots = out_ref.shape[0]
    zeros_l = jnp.zeros((live_dev, STATE), F32)
    place = (iota((live_dev, STATE), 0) + 1).astype(F32)
    parts = [bc_ref[t, 1, 0:live_dev, :].astype(F32) for t in range(steps)]
    parts += [place] + [zeros_l] * (SUB - steps - 1)
    data_l = jnp.concatenate(parts, 0)
    data_l = jnp.concatenate([data_l, jnp.zeros_like(data_l)], 1).astype(BF16)
    parts = [
        bc_ref[t % steps, 1, live_dev : live_dev + readers, :].astype(F32) for t in range(SUB)
    ]
    data_r = jnp.concatenate(parts, 0)
    data_r = jnp.concatenate([jnp.zeros_like(data_r), data_r], 1).astype(BF16)
    pick_l = onehot(iota((slots, SUB * live_dev), 0) == tgt_l_ref[...])
    pick_r = onehot(iota((slots, SUB * readers), 0) == tgt_r_ref[...])
    out_ref[...] = (mm(pick_l, data_l) + mm(pick_r, data_r)).astype(BF16)


def state_kernel(
    len_ref,
    x_ref,
    bc_ref,
    raw_ref,
    rawt_ref,
    decay_ref,
    bias_ref,
    decayt_ref,
    biast_ref,
    cw_ref,
    cb_ref,
    xc_ref,
    cum_ref,
    cumt_ref,
    dtt_ref,
    st_ref,
    xf,
):
    span, width = x_ref.shape
    heads = raw_ref.shape[1]
    taps = cw_ref.shape[0]
    length = len_ref[0]
    xf[0:SUB, :] = jnp.zeros((SUB, width), F32)
    xf[SUB : SUB + span, :] = x_ref[...].astype(F32)
    dt = softplus(raw_ref[...].astype(F32) + bias_ref[...])
    dt = jnp.where(iota((span, heads), 0) < length, dt, 0.0)
    dtt = softplus(rawt_ref[...].astype(F32) + biast_ref[...])
    dtt = jnp.where(iota((heads, span), 1) < length, dtt, 0.0)
    dtt_ref[...] = dtt
    tri = onehot(iota((span, span), 0) >= iota((span, span), 1))
    pieces = split3(dtt * -decayt_ref[...])
    cum = mm_nt(tri, pieces[0]) + mm_nt(tri, pieces[1]) + mm_nt(tri, pieces[2])
    cumt = mm_nt(pieces[0], tri) + mm_nt(pieces[1], tri) + mm_nt(pieces[2], tri)
    cum_ref[...] = cum
    cumt_ref[...] = cumt
    weight = jnp.exp(cum[span - 1 : span, :] - cum) * dt
    expand = expander(heads, width)
    block = 128
    total = jnp.zeros((STATE, width), F32)
    for start in range(0, span, block):
        acc = cb_ref[...]
        for k in range(taps):
            first = SUB - taps + 1 + k + start
            acc = acc + xf[first : first + block, :] * cw_ref[k : k + 1, :]
        xc = silu(acc).astype(BF16)
        xc_ref[start : start + block, :] = xc
        weighted = xc.astype(F32) * spread(weight[start : start + block, :], expand)
        total = total + lax.dot_general(
            bc_ref[0, start : start + block, :],
            weighted.astype(BF16),
            TN,
            preferred_element_type=F32,
        )
    st_ref[0:STATE, :] = jnp.zeros((STATE, width), BF16)
    st_ref[STATE : 2 * STATE, :] = total.astype(BF16)


def prompt_kernel(
    xc_ref, z_ref, bc_ref, cum_ref, cumt_ref, dtt_ref, skip_ref, g_ref, ss_ref, scores
):
    span, width = xc_ref.shape
    heads = cum_ref.shape[1]
    block = 128
    ones = jnp.ones((SUB, block), BF16)
    lanes = iota((block, block), 1)
    causal = iota((block, block), 0) >= lanes
    for start in range(0, span, block):
        stop = start + block
        cmat = bc_ref[1, start:stop, :]
        scores[:, 0:stop] = mm_nt(cmat, bc_ref[0, 0:stop, :])
        square = jnp.zeros((block, block), F32)
        for lane in range(0, width, block):
            halves = []
            for half in range(2):
                head = lane * heads // width + half
                at = cum_ref[start:stop, head : head + 1]
                gap = jnp.where(causal, at - cumt_ref[head : head + 1, start:stop], -jnp.inf)
                near = scores[:, start:stop] * jnp.exp(gap) * dtt_ref[head : head + 1, start:stop]
                yhead = mm(near.astype(BF16), xc_ref[start:stop, lane : lane + block])
                if start:
                    gap = at - cumt_ref[head : head + 1, 0:start]
                    far = scores[:, 0:start] * jnp.exp(gap) * dtt_ref[head : head + 1, 0:start]
                    yhead = yhead + mm(far.astype(BF16), xc_ref[0:start, lane : lane + block])
                halves.append(yhead)
            y = jnp.where(lanes < block // 2, halves[0], halves[1])
            xin = xc_ref[start:stop, lane : lane + block].astype(F32)
            y = y + skip_ref[:, lane : lane + block] * xin
            gate = y * silu(z_ref[start:stop, lane : lane + block].astype(F32))
            g_ref[start:stop, lane : lane + block] = gate
            square = square + gate * gate
        hi, lo = split2(square)
        ss_ref[:, start:stop] = mm_nt(ones, hi) + mm_nt(ones, lo)


def answer_kernel(
    ask_ref, state_ref, conv_ref, prefix_ref, tail_a_ref, tail_b_ref, out_ref, cs, ys
):
    slots = ask_ref.shape[0]
    block = state_ref.shape[0]
    count = ys.shape[0]
    width = prefix_ref.shape[1]
    step = pl.program_id(0)
    ask = ask_ref[...]

    def places():
        row, col = iota((slots, slots), 0), iota((slots, slots), 1)
        return mm(onehot(col == (row // SUB) * SUB + 4), ask)

    @pl.when(step == 0)
    def _():
        place = places().astype(BF16)
        lane0 = onehot(iota((SUB, 2 * STATE), 1) == 0)
        across = mm_nt(lane0, place)[0:1, :].astype(jnp.int32)
        row, col = iota((count, slots), 0), iota((count, slots), 1)
        back = onehot(row + SUB - col % SUB == across * SUB)
        got = mm(back, ask)
        cs[...] = jnp.where(iota(got.shape, 0) % SUB < 4, got, 0.0)

    for k in range(block):
        first = pl.multiple_of((step * block + k) * SUB, SUB)
        cmat = cs[pl.ds(first, SUB), 0:STATE].astype(BF16)
        ys[pl.ds(first, SUB), :] = mm_nt(cmat, state_ref[k]) + conv_ref[k].astype(F32)

    @pl.when(step == pl.num_programs(0) - 1)
    def _():
        place = places()[:, 0:1].astype(jnp.int32)
        row, col = iota((slots, count), 0), iota((slots, count), 1)
        there = onehot(col + SUB - row % SUB == place * SUB)
        live = mm(there, ys[...].astype(BF16)).reshape(slots // SUB, SUB, width)
        live = live + tail_a_ref[...].astype(F32)[None]
        out_ref[:, 0:width] = live.reshape(slots, width).astype(BF16)
        new = mm(ask, prefix_ref[...])
        half = width // 2
        first = iota((slots, half), 0) % SUB < SUB // 2
        new = jnp.where(first, new[:, 0:half], new[:, half:width])
        out_ref[:, width : width + half] = new.astype(BF16)
        tail = jnp.broadcast_to(
            tail_b_ref[...].astype(F32)[None], (slots // SUB,) + tail_b_ref.shape
        )
        out_ref[:, width + half :] = tail.reshape(slots, tail_b_ref.shape[1]).astype(BF16)


def decode_kernel(
    live_dev,
    readers,
    got_ref,
    tgt_l_ref,
    tgt_r_ref,
    xz_ref,
    bc_ref,
    raw_ref,
    decay_ref,
    bias_ref,
    skip_ref,
    cw_ref,
    cb_ref,
    pre_ss_ref,
    g_ref,
    ss_ref,
):
    slots = got_ref.shape[0]
    steps, _, rows, width = xz_ref.shape
    heads = raw_ref.shape[1]
    span = pre_ss_ref.shape[1]
    taps = cw_ref.shape[0]
    half = width // 2
    part = width // 4
    pick_l = onehot(iota((SUB * live_dev, slots), 1) == tgt_l_ref[...])
    pick_r = onehot(iota((SUB * readers, slots), 1) == tgt_r_ref[...])
    live = mm(pick_l, got_ref[:, 0:width])
    new = mm(pick_r, got_ref[:, width:])
    old = mm(pick_r[(SUB - 1) * readers :, :], got_ref[:, 0:width])

    def live_row(r):
        return live[r * live_dev : (r + 1) * live_dev, :]

    def new_row(r, first, last):
        return new[r * readers : (r + 1) * readers, first:last]

    def tail_row(r):
        return jnp.concatenate(
            [new_row(r + i, half, half + part) for i in range(4)], 1
        )

    first = []
    for t in range(steps):
        wide = jnp.concatenate([new_row(t, 0, half), new_row(t + 4, 0, half)], 1)
        first.append(jnp.concatenate([live_row(t), wide], 0))
    inputs = [
        jnp.concatenate([live_row(4), old], 0),
        jnp.concatenate([live_row(5), tail_row(0)], 0),
        jnp.concatenate([live_row(6), tail_row(4)], 0),
    ]
    inputs += [xz_ref[t, 0].astype(F32) for t in range(steps)]
    expand = expander(heads, width)
    weights = [cw_ref[k : k + 1, :].astype(F32) for k in range(taps)]
    dts, logs, bmats, cmats, xcs, gates = [], [], [], [], [], []
    for t in range(steps):
        acc = cb_ref[...]
        for k in range(taps):
            acc = acc + inputs[t + k] * weights[k]
        xcs.append(silu(acc).astype(BF16).astype(F32))
        dt = softplus(raw_ref[t * rows : (t + 1) * rows, :].astype(F32) + bias_ref[...])
        dts.append(dt)
        decayed = -dt * decay_ref[...]
        logs.append(decayed if t == 0 else logs[-1] + decayed)
        bmats.append(bc_ref[t, 0].astype(F32))
        cmats.append(bc_ref[t, 1].astype(F32))
        y = spread(jnp.exp(logs[t]), expand) * first[t]
        for s in range(t + 1):
            score = jnp.sum(bmats[s] * cmats[t], axis=1, keepdims=True)
            factor = dts[s] * score
            if s < t:
                factor = jnp.exp(logs[t] - logs[s]) * factor
            else:
                factor = factor + skip_ref[...]
            y = y + spread(factor, expand) * xcs[s]
        gate = y * silu(xz_ref[t, 1].astype(F32))
        g_ref[t * rows : (t + 1) * rows, :] = gate
        gates.append(gate * gate)
    square = jnp.concatenate(gates, 0)
    hi, lo = split2(square)
    ones = jnp.ones((SUB, width), BF16)
    sums = mm_nt(ones, hi) + mm_nt(ones, lo)
    pad = ss_ref.shape[2] - span - sums.shape[1]
    sums = jnp.concatenate([sums, jnp.zeros((SUB, pad), F32)], 1)
    for i in range(ss_ref.shape[0]):
        ss_ref[i, :, 0:span] = pre_ss_ref[...]
        ss_ref[i, :, span:] = sums


def finish_kernel(width_all, ss_ref, pre_ref, step_ref, gain_ref, pre_out_ref, step_out_ref):
    total = ss_ref[0]
    for i in range(1, ss_ref.shape[0]):
        total = total + ss_ref[i]
    scale = lax.rsqrt(total[0:1, :] / width_all + EPS)
    gain = gain_ref[...]
    span = pre_ref.shape[0]
    block = 128

    def column(first, rows):
        row = jnp.broadcast_to(scale[:, first : first + block], (rows, block))
        diag = iota((rows, block), 0) == iota((rows, block), 1)
        return jnp.sum(jnp.where(diag, row, 0.0), axis=1, keepdims=True)

    for start in range(0, span, block):
        part = slice(start, start + block)
        pre_out_ref[part, :] = (pre_ref[part, :] * column(start, block) * gain).astype(BF16)
    count = step_ref.shape[0]
    for start in range(0, count, block):
        rows = min(block, count - start)
        part = slice(start, start + rows)
        step_out_ref[part, :] = (step_ref[part, :] * column(span + start, rows) * gain).astype(
            BF16
        )


def params(**more):
    return pltpu.CompilerParams(vmem_limit_bytes=40 * 1024 * 1024, **more)


def cost(flops, moved, special=0):
    return pl.CostEstimate(flops=flops, bytes_accessed=moved, transcendentals=special)


def vmem():
    return pl.BlockSpec(memory_space=pltpu.VMEM)


def shape(dims, kind):
    return jax.ShapeDtypeStruct(dims, kind)


def per_device(
    pre_x,
    pre_z,
    pre_bc,
    pre_raw,
    prompt_len,
    live_state,
    live_conv,
    source,
    reader,
    step_xz,
    step_bc,
    step_raw,
    decay,
    dt_bias,
    conv_weight,
    conv_bias,
    skip,
    norm_gain,
):
    _, span, width = pre_x.shape
    mp = lax.axis_size("mp")
    gens = lax.axis_size("gen")
    width_all = width * mp
    live_dev = source.shape[0]
    readers = reader.shape[0]
    heads = pre_raw.shape[2]
    steps, _, rows, _ = step_xz.shape
    slots = gens * SUB
    offset = jnp.arange(SUB, dtype=jnp.int32)[:, None]
    tgt_l = SUB * (source // live_dev)[None, :] + offset
    tgt_r = SUB * reader[None, :] + offset

    ask = pl.pallas_call(
        lambda *refs: ask_kernel(live_dev, readers, *refs),
        out_shape=shape((slots, 2 * STATE), BF16),
        in_specs=[vmem()] * 3,
        out_specs=vmem(),
        compiler_params=params(),
        cost_estimate=cost(2 * slots * 384 * 128, 400000),
        name="ask",
    )(step_bc, tgt_l.reshape(1, -1), tgt_r.reshape(1, -1))
    asked = lax.all_to_all(
        ask.reshape(gens, SUB, 2 * STATE), "gen", split_axis=0, concat_axis=0, tiled=True
    ).reshape(slots, 2 * STATE)

    length = prompt_len[0]
    raw = pre_raw[0]
    xconv, cum, cumt, dtt, prefix = pl.pallas_call(
        state_kernel,
        out_shape=(
            shape((span, width), BF16),
            shape((span, heads), F32),
            shape((heads, span), F32),
            shape((heads, span), F32),
            shape((2 * STATE, width), BF16),
        ),
        in_specs=[pl.BlockSpec(memory_space=pltpu.SMEM)] + [vmem()] * 10,
        out_specs=(vmem(),) * 5,
        scratch_shapes=[pltpu.VMEM((span + SUB, width), F32)],
        compiler_params=params(),
        cost_estimate=cost(2 * 10 * span * span * 64, 2 * span * width * 2, span * width * 2),
        name="state",
    )(
        prompt_len,
        pre_x[0],
        pre_bc[0],
        raw,
        raw.T,
        decay[None],
        dt_bias[None],
        decay[:, None],
        dt_bias[:, None],
        conv_weight.astype(F32),
        conv_bias[None],
    )
    taps = conv_weight.shape[0]
    spots = length - (taps - 1) + jnp.arange(taps - 1, dtype=jnp.int32)
    tails = jnp.where(
        (spots >= 0)[:, None], pre_x[0][jnp.maximum(spots, 0)], jnp.zeros((), BF16)
    )
    tail_a = jnp.concatenate([jnp.zeros((SUB - 1, width), BF16), tails[0:1]], 0)
    tail_b = tails[1:].reshape(SUB, width // 4)
    conv = jnp.pad(live_conv, ((0, 0), (steps, SUB - steps - (taps - 1)), (0, 0)))

    block = 8
    answer = pl.pallas_call(
        answer_kernel,
        grid=(live_dev // block,),
        out_shape=shape((slots, width + width // 2 + width // 4), BF16),
        in_specs=[
            pl.BlockSpec((slots, 2 * STATE), lambda i: (0, 0)),
            pl.BlockSpec((block, width, STATE), lambda i: (i, 0, 0)),
            pl.BlockSpec((block, SUB, width), lambda i: (i, 0, 0)),
            pl.BlockSpec((2 * STATE, width), lambda i: (0, 0)),
            pl.BlockSpec((SUB, width), lambda i: (0, 0)),
            pl.BlockSpec((SUB, width // 4), lambda i: (0, 0)),
        ],
        out_specs=pl.BlockSpec((slots, width + width // 2 + width // 4), lambda i: (0, 0)),
        scratch_shapes=[
            pltpu.VMEM((live_dev * SUB, 2 * STATE), F32),
            pltpu.VMEM((live_dev * SUB, width), F32),
        ],
        compiler_params=params(dimension_semantics=("arbitrary",)),
        cost_estimate=cost(2 * slots * 512 * 1024, 6000000),
        name="answer",
    )(asked, live_state.reshape(live_dev, width, STATE), conv, prefix, tail_a, tail_b)
    lanes = answer.shape[1]
    got = lax.all_to_all(
        answer.reshape(gens, SUB, lanes), "gen", split_axis=0, concat_axis=0, tiled=True
    ).reshape(slots, lanes)

    pre_gate, pre_ss = pl.pallas_call(
        prompt_kernel,
        out_shape=(shape((span, width), F32), shape((SUB, span), F32)),
        in_specs=[vmem()] * 7,
        out_specs=(vmem(), vmem()),
        scratch_shapes=[pltpu.VMEM((128, span), F32)],
        compiler_params=params(),
        cost_estimate=cost(2 * heads * span * span * 128, 2500000, heads * span * span),
        name="prompt",
    )(xconv, pre_z[0], pre_bc[0], cum, cumt, dtt, jnp.repeat(skip, width // heads)[None])

    count = steps * rows
    padded = -(-(span + count) // 128) * 128
    step_gate, sums = pl.pallas_call(
        lambda *refs: decode_kernel(live_dev, readers, *refs),
        out_shape=(shape((count, width), F32), shape((mp, SUB, padded), F32)),
        in_specs=[vmem()] * 12,
        out_specs=(vmem(), vmem()),
        compiler_params=params(),
        cost_estimate=cost(2 * 384 * 512 * 512, 2500000),
        name="decode",
    )(
        got,
        tgt_l.reshape(-1, 1),
        tgt_r.reshape(-1, 1),
        step_xz,
        step_bc,
        step_raw.reshape(count, heads),
        decay[None],
        dt_bias[None],
        skip[None],
        conv_weight,
        conv_bias[None],
        pre_ss,
    )
    sums = lax.all_to_all(sums, "mp", split_axis=0, concat_axis=0, tiled=True)

    prefill_out, decoded = pl.pallas_call(
        lambda *refs: finish_kernel(width_all, *refs),
        out_shape=(shape((span, width), BF16), shape((count, width), BF16)),
        in_specs=[vmem()] * 4,
        out_specs=(vmem(), vmem()),
        compiler_params=params(),
        cost_estimate=cost(1000000, 2500000),
        name="finish",
    )(sums, pre_gate, step_gate, norm_gain[None])
    return (prefill_out[None], decoded.reshape(steps, rows, width))


def solution(mesh):
    placed = (
        P("gen", None, "mp"),
        P("gen", None, "mp"),
        P("gen", None, None, "mp"),
        P("gen", None, "mp"),
        P("gen"),
        P("gen", "mp", None, None),
        P("gen", None, "mp"),
        P("gen"),
        P("gen"),
        P(None, None, "gen", "mp"),
        P(None, None, "gen", "mp"),
        P(None, "gen", "mp"),
        P("mp"),
        P("mp"),
        P(None, "mp"),
        P("mp"),
        P("mp"),
        P("mp"),
    )
    return jax.shard_map(
        per_device,
        mesh=mesh,
        in_specs=placed,
        out_specs=(P("gen", None, "mp"), P(None, "gen", "mp")),
        check_vma=False,
    )
```

```python
import jax
import jax.numpy as jnp
from jax import lax
from jax.experimental import pallas as pl
from jax.experimental.pallas import tpu as pltpu
from jax.sharding import PartitionSpec as P

STATE = 64
EPS = 1e-05
SUB = 8
F32 = jnp.float32
BF16 = jnp.bfloat16
NT = (((1,), (1,)), ((), ()))
TN = (((0,), (0,)), ((), ()))


def iota(shape, dim):
    return lax.broadcasted_iota(jnp.int32, shape, dim)


def mm(a, b):
    return jnp.dot(a, b, preferred_element_type=F32)


def mm_nt(a, b):
    return lax.dot_general(a, b, NT, preferred_element_type=F32)


def onehot(mask):
    return jnp.where(mask, 1.0, 0.0).astype(BF16)


def split2(x):
    hi = x.astype(BF16)
    return hi, (x - hi.astype(F32)).astype(BF16)


def split3(x):
    hi = x.astype(BF16)
    rest = x - hi.astype(F32)
    mid = rest.astype(BF16)
    return hi, mid, (rest - mid.astype(F32)).astype(BF16)


def silu(x):
    return x / (1.0 + jnp.exp(-x))


def softplus(x):
    return jnp.maximum(x, 0.0) + jnp.log1p(jnp.exp(-jnp.abs(x)))


def expander(heads, width):
    return onehot(iota((heads, width), 1) // (width // heads) == iota((heads, width), 0))


def spread(x, expand):
    hi, lo = split2(x)
    return mm(hi, expand) + mm(lo, expand)


def fetch(sources, targets, sems):
    copies = [
        pltpu.make_async_copy(source, target, sems.at[i])
        for i, (source, target) in enumerate(zip(sources, targets))
    ]
    for copy in copies:
        copy.start()
    return copies


def ask_kernel(*refs):
    sources, out_ref, targets, sems = refs[:5], refs[5], refs[6:11], refs[11]
    for copy in fetch(sources, targets, sems):
        copy.wait()
    bc_ref, source_ref, reader_ref, len_ref, x_ref = targets
    steps = bc_ref.shape[0]
    slots = out_ref.shape[0]
    live_dev = source_ref.shape[1]
    readers = reader_ref.shape[1]
    span, width = x_ref.shape
    part = width // 4
    zeros_l = jnp.zeros((live_dev, STATE), F32)
    place = (iota((live_dev, STATE), 0) + 1).astype(F32)
    parts = [bc_ref[t, 1, 0:live_dev, :].astype(F32) for t in range(steps)]
    parts += [place] + [zeros_l] * (SUB - steps - 1)
    data_l = jnp.concatenate(parts, 0)
    data_l = jnp.concatenate([data_l, jnp.zeros_like(data_l)], 1).astype(BF16)
    parts = [
        bc_ref[t % steps, 1, live_dev : live_dev + readers, :].astype(F32) for t in range(SUB)
    ]
    data_r = jnp.concatenate(parts, 0)
    data_r = jnp.concatenate([jnp.zeros_like(data_r), data_r], 1).astype(BF16)
    first_l = lax.div(source_ref[...], live_dev) * SUB
    first_r = reader_ref[...] * SUB
    tgt_l = jnp.concatenate([first_l + r for r in range(SUB)], 1)
    tgt_r = jnp.concatenate([first_r + r for r in range(SUB)], 1)
    pick_l = onehot(iota((slots, SUB * live_dev), 0) == tgt_l)
    pick_r = onehot(iota((slots, SUB * readers), 0) == tgt_r)
    out_ref[:, 0 : 2 * STATE] = (mm(pick_l, data_l) + mm(pick_r, data_r)).astype(BF16)
    row, col = iota((2 * SUB, span), 0), iota((2 * SUB, span), 1)
    last = onehot(col == len_ref[...] - 2 + row // SUB)
    both = mm(last, x_ref[...])
    lane_part = iota((SUB, part), 0) % 4
    tail = jnp.zeros((SUB, part), F32)
    for i in range(4):
        lanes = slice(i * part, (i + 1) * part)
        piece = jnp.where(iota((SUB, part), 0) < 4, both[0:SUB, lanes], both[SUB:, lanes])
        tail = jnp.where(lane_part == i, piece, tail)
    tail = jnp.broadcast_to(tail[None], (slots // SUB, SUB, part))
    out_ref[:, 2 * STATE :] = tail.reshape(slots, part).astype(BF16)


def state_kernel(*refs):
    sources, outs, targets = refs[:10], refs[10:18], refs[18:26]
    sems, xf = refs[26], refs[27]
    xc_ref, cum_ref, cumt_ref, dtt_ref, st_ref, tail_ref, live_ref, conv_ref = outs
    copies = fetch(sources, targets + (live_ref, conv_ref), sems)
    for copy in copies[:8]:
        copy.wait()
    len_ref, rawt_ref, decay_ref, bias_ref, cw_ref, cb_ref, bct_ref, x_ref = targets
    span, width = x_ref.shape
    heads = rawt_ref.shape[0]
    taps = cw_ref.shape[0]
    length = len_ref[...]
    xf[0:SUB, :] = jnp.zeros((SUB, width), F32)
    xf[SUB : SUB + span, :] = x_ref[...].astype(F32)
    square = iota((heads, heads), 0) == iota((heads, heads), 1)

    def column(row):
        return jnp.sum(jnp.where(square, row, 0.0), axis=1, keepdims=True)

    dtt = softplus(rawt_ref[...].astype(F32) + column(bias_ref[...]))
    dtt = jnp.where(iota((heads, span), 1) < length, dtt, 0.0)
    dtt_ref[...] = dtt
    tri = onehot(iota((span, span), 0) >= iota((span, span), 1))
    pieces = split3(dtt * -column(decay_ref[...]))
    cum_ref[...] = mm_nt(tri, pieces[0]) + mm_nt(tri, pieces[1]) + mm_nt(tri, pieces[2])
    cumt = mm_nt(pieces[0], tri) + mm_nt(pieces[1], tri) + mm_nt(pieces[2], tri)
    cumt_ref[...] = cumt
    weight = jnp.exp(cumt[:, span - 1 : span] - cumt) * dtt
    weight_hi, weight_lo = split2(weight)
    expand = expander(heads, width)
    weights = [cw_ref[k : k + 1, :].astype(F32) for k in range(taps)]
    block = 128
    total = jnp.zeros((STATE, width), F32)
    for start in range(0, span, block):
        part = slice(start, start + block)
        acc = cb_ref[...]
        for k in range(taps):
            first = SUB - taps + 1 + k + start
            acc = acc + xf[first : first + block, :] * weights[k]
        xc = silu(acc).astype(BF16)
        xc_ref[part, :] = xc
        wide = lax.dot_general(weight_hi[:, part], expand, TN, preferred_element_type=F32)
        wide = wide + lax.dot_general(
            weight_lo[:, part], expand, TN, preferred_element_type=F32
        )
        weighted = (xc.astype(F32) * wide).astype(BF16)
        total = total + mm(bct_ref[0, :, part], weighted)
    st_ref[0:STATE, :] = jnp.zeros((STATE, width), BF16)
    st_ref[STATE : 2 * STATE, :] = total.astype(BF16)
    row, col = iota((SUB, span), 0), iota((SUB, span), 1)
    tail = onehot((col == length - (taps - 1)) & (row == SUB - 1))
    tail_ref[...] = mm(tail, x_ref[...]).astype(BF16)
    for copy in copies[8:]:
        copy.wait()


def prompt_kernel(
    xc_ref, z_ref, bct_ref, cum_ref, cumt_ref, dtt_ref, skip_ref, g_ref, ss_ref, scores
):
    span, width = xc_ref.shape
    heads = cum_ref.shape[1]
    block = 128
    ones = jnp.ones((SUB, block), BF16)
    lanes = iota((block, block), 1)
    causal = iota((block, block), 0) >= lanes
    for start in range(0, span, block):
        stop = start + block
        scores[:, 0:stop] = lax.dot_general(
            bct_ref[1, :, start:stop], bct_ref[0, :, 0:stop], TN, preferred_element_type=F32
        )
        square = jnp.zeros((block, block), F32)
        for lane in range(0, width, block):
            halves = []
            for half in range(2):
                head = lane * heads // width + half
                at = cum_ref[start:stop, head : head + 1]
                gap = jnp.where(causal, at - cumt_ref[head : head + 1, start:stop], -jnp.inf)
                near = scores[:, start:stop] * jnp.exp(gap) * dtt_ref[head : head + 1, start:stop]
                yhead = mm(near.astype(BF16), xc_ref[start:stop, lane : lane + block])
                if start:
                    gap = at - cumt_ref[head : head + 1, 0:start]
                    far = scores[:, 0:start] * jnp.exp(gap) * dtt_ref[head : head + 1, 0:start]
                    yhead = yhead + mm(far.astype(BF16), xc_ref[0:start, lane : lane + block])
                halves.append(yhead)
            y = jnp.where(lanes < block // 2, halves[0], halves[1])
            xin = xc_ref[start:stop, lane : lane + block].astype(F32)
            y = y + skip_ref[:, lane : lane + block] * xin
            gate = y * silu(z_ref[start:stop, lane : lane + block].astype(F32))
            g_ref[start:stop, lane : lane + block] = gate
            square = square + gate * gate
        hi, lo = split2(square)
        ss_ref[:, start:stop] = mm_nt(ones, hi) + mm_nt(ones, lo)


def answer_kernel(ask_ref, state_ref, conv_ref, prefix_ref, tail_ref, out_ref, cs, ys):
    slots = ask_ref.shape[0]
    live_dev = state_ref.shape[0]
    count = ys.shape[0]
    width = prefix_ref.shape[1]
    half = width // 2
    ask = ask_ref[:, 0 : 2 * STATE]
    row, col = iota((slots, slots), 0), iota((slots, slots), 1)
    place = mm(onehot(col == (row // SUB) * SUB + 4), ask)
    lane0 = onehot(iota((SUB, 2 * STATE), 1) == 0)
    across = mm_nt(lane0, place.astype(BF16))[0:1, :].astype(jnp.int32)
    row, col = iota((count, slots), 0), iota((count, slots), 1)
    back = onehot(row + SUB - col % SUB == across * SUB)
    got = mm(back, ask)
    cs[...] = jnp.where(iota(got.shape, 0) % SUB < 4, got, 0.0)
    for k in range(live_dev):
        rows = slice(k * SUB, (k + 1) * SUB)
        ys[rows, :] = mm_nt(cs[rows, 0:STATE].astype(BF16), state_ref[k])
    place = place[:, 0:1].astype(jnp.int32)
    row, col = iota((slots, count), 0), iota((slots, count), 1)
    there = onehot(col + SUB - row % SUB == place * SUB)
    live = mm(there, ys[...].astype(BF16))
    kept = conv_ref.shape[0]
    row, col = iota((slots, kept), 0), iota((slots, kept), 1)
    there = onehot(
        (lax.div(col, live_dev) + 4 == row % SUB) & (col % live_dev + 1 == place)
    )
    live = (live + mm(there, conv_ref[...])).reshape(slots // SUB, SUB, width)
    live = live + tail_ref[...].astype(F32)[None]
    out_ref[:, 0:width] = live.reshape(slots, width).astype(BF16)
    new = mm(ask, prefix_ref[...])
    first = iota((slots, half), 0) % SUB < SUB // 2
    new = jnp.where(first, new[:, 0:half], new[:, half:width])
    out_ref[:, width : width + half] = new.astype(BF16)


def decode_kernel(
    live_dev,
    readers,
    got_ref,
    ask_ref,
    tgt_l_ref,
    tgt_r_ref,
    xz_ref,
    bc_ref,
    raw_ref,
    decay_ref,
    bias_ref,
    skip_ref,
    cw_ref,
    cb_ref,
    pre_ss_ref,
    g_ref,
    ss_ref,
):
    slots = got_ref.shape[0]
    steps, _, rows, width = xz_ref.shape
    heads = raw_ref.shape[1]
    span = pre_ss_ref.shape[1]
    taps = cw_ref.shape[0]
    half = width // 2
    pick_l = onehot(iota((SUB * live_dev, slots), 1) == tgt_l_ref[...])
    pick_r = onehot(iota((SUB * readers, slots), 1) == tgt_r_ref[...])
    live = mm(pick_l, got_ref[:, 0:width])
    new = mm(pick_r, got_ref[:, width:])
    old = mm(pick_r[(SUB - 1) * readers :, :], got_ref[:, 0:width])
    late = mm(pick_r, ask_ref[:, 2 * STATE :])

    def live_row(r):
        return live[r * live_dev : (r + 1) * live_dev, :]

    def new_row(r, first, last):
        return new[r * readers : (r + 1) * readers, first:last]

    def tail_row(r):
        return jnp.concatenate(
            [late[(r + i) * readers : (r + i + 1) * readers, :] for i in range(4)], 1
        )

    first = []
    for t in range(steps):
        wide = jnp.concatenate([new_row(t, 0, half), new_row(t + 4, 0, half)], 1)
        first.append(jnp.concatenate([live_row(t), wide], 0))
    inputs = [
        jnp.concatenate([live_row(4), old], 0),
        jnp.concatenate([live_row(5), tail_row(0)], 0),
        jnp.concatenate([live_row(6), tail_row(4)], 0),
    ]
    inputs += [xz_ref[t, 0].astype(F32) for t in range(steps)]
    expand = expander(heads, width)
    weights = [cw_ref[k : k + 1, :].astype(F32) for k in range(taps)]
    dts, logs, bmats, cmats, xcs, gates = [], [], [], [], [], []
    for t in range(steps):
        acc = cb_ref[...]
        for k in range(taps):
            acc = acc + inputs[t + k] * weights[k]
        xcs.append(silu(acc).astype(BF16).astype(F32))
        dt = softplus(raw_ref[t * rows : (t + 1) * rows, :].astype(F32) + bias_ref[...])
        dts.append(dt)
        decayed = -dt * decay_ref[...]
        logs.append(decayed if t == 0 else logs[-1] + decayed)
        bmats.append(bc_ref[t, 0].astype(F32))
        cmats.append(bc_ref[t, 1].astype(F32))
        y = spread(jnp.exp(logs[t]), expand) * first[t]
        for s in range(t + 1):
            score = jnp.sum(bmats[s] * cmats[t], axis=1, keepdims=True)
            factor = dts[s] * score
            if s < t:
                factor = jnp.exp(logs[t] - logs[s]) * factor
            else:
                factor = factor + skip_ref[...]
            y = y + spread(factor, expand) * xcs[s]
        gate = y * silu(xz_ref[t, 1].astype(F32))
        g_ref[t * rows : (t + 1) * rows, :] = gate
        gates.append(gate * gate)
    square = jnp.concatenate(gates, 0)
    hi, lo = split2(square)
    ones = jnp.ones((SUB, width), BF16)
    sums = mm_nt(ones, hi) + mm_nt(ones, lo)
    pad = ss_ref.shape[2] - span - sums.shape[1]
    sums = jnp.concatenate([sums, jnp.zeros((SUB, pad), F32)], 1)
    for i in range(ss_ref.shape[0]):
        ss_ref[i, :, 0:span] = pre_ss_ref[...]
        ss_ref[i, :, span:] = sums


def finish_kernel(width_all, ss_ref, pre_ref, step_ref, gain_ref, pre_out_ref, step_out_ref):
    total = ss_ref[0]
    for i in range(1, ss_ref.shape[0]):
        total = total + ss_ref[i]
    scale = lax.rsqrt(total[0:1, :] / width_all + EPS)
    gain = gain_ref[...]
    span = pre_ref.shape[0]
    block = 128

    def column(first, rows):
        row = jnp.broadcast_to(scale[:, first : first + block], (rows, block))
        diag = iota((rows, block), 0) == iota((rows, block), 1)
        return jnp.sum(jnp.where(diag, row, 0.0), axis=1, keepdims=True)

    for start in range(0, span, block):
        part = slice(start, start + block)
        pre_out_ref[part, :] = (pre_ref[part, :] * column(start, block) * gain).astype(BF16)
    count = step_ref.shape[0]
    for start in range(0, count, block):
        rows = min(block, count - start)
        part = slice(start, start + rows)
        step_out_ref[part, :] = (step_ref[part, :] * column(span + start, rows) * gain).astype(
            BF16
        )


def params(**more):
    return pltpu.CompilerParams(vmem_limit_bytes=24 * 1024 * 1024, **more)


def cost(flops, moved, special=0):
    return pl.CostEstimate(flops=flops, bytes_accessed=moved, transcendentals=special)


def vmem():
    return pl.BlockSpec(memory_space=pltpu.VMEM)


def hbm():
    return pl.BlockSpec(memory_space=pltpu.HBM)


def shape(dims, kind):
    return jax.ShapeDtypeStruct(dims, kind)


def per_device(
    pre_x,
    pre_z,
    pre_bc,
    pre_raw,
    prompt_len,
    live_state,
    live_conv,
    source,
    reader,
    step_xz,
    step_bc,
    step_raw,
    decay,
    dt_bias,
    conv_weight,
    conv_bias,
    skip,
    norm_gain,
):
    _, span, width = pre_x.shape
    mp = lax.axis_size("mp")
    gens = lax.axis_size("gen")
    width_all = width * mp
    live_dev = source.shape[0]
    readers = reader.shape[0]
    heads = pre_raw.shape[2]
    steps, _, rows, _ = step_xz.shape
    slots = gens * SUB
    offset = jnp.arange(SUB, dtype=jnp.int32)[:, None]
    tgt_l = SUB * (source // live_dev)[None, :] + offset
    tgt_r = SUB * reader[None, :] + offset

    length = prompt_len.reshape(1, 1)
    conv_rows = jnp.transpose(live_conv, (1, 0, 2)).reshape(-1, width)
    bct = jnp.swapaxes(pre_bc[0], 1, 2)
    dma = pltpu.SemaphoreType.DMA

    def staged(*arrays):
        return [pltpu.VMEM(array.shape, array.dtype) for array in arrays]

    operands = (step_bc, source[None], reader[None], length, pre_x[0])
    ask = pl.pallas_call(
        ask_kernel,
        out_shape=shape((slots, 2 * STATE + width // 4), BF16),
        in_specs=[hbm()] * len(operands),
        out_specs=vmem(),
        scratch_shapes=staged(*operands) + [dma((len(operands),))],
        compiler_params=params(),
        cost_estimate=cost(2 * slots * 384 * 128, 800000),
        name="ask",
    )(*operands)
    lanes = ask.shape[1]
    asked = lax.all_to_all(
        ask.reshape(gens, SUB, lanes), "gen", split_axis=0, concat_axis=0, tiled=True
    ).reshape(slots, lanes)

    live = live_state.reshape(live_dev, width, STATE)
    operands = (
        length,
        pre_raw[0].T,
        decay[None],
        dt_bias[None],
        conv_weight,
        conv_bias[None],
        bct,
        pre_x[0],
    )
    xconv, cum, cumt, dtt, prefix, tail, live_near, conv_near = pl.pallas_call(
        state_kernel,
        out_shape=(
            shape((span, width), BF16),
            shape((span, heads), F32),
            shape((heads, span), F32),
            shape((heads, span), F32),
            shape((2 * STATE, width), BF16),
            shape((SUB, width), BF16),
            shape(live.shape, BF16),
            shape(conv_rows.shape, BF16),
        ),
        in_specs=[hbm()] * (len(operands) + 2),
        out_specs=(vmem(),) * 8,
        scratch_shapes=staged(*operands)
        + [dma((len(operands) + 2,)), pltpu.VMEM((span + SUB, width), F32)],
        compiler_params=params(),
        cost_estimate=cost(2 * 10 * span * span * 64, 6000000, span * width * 2),
        name="state",
    )(*operands, live, conv_rows)

    answer = pl.pallas_call(
        answer_kernel,
        out_shape=shape((slots, width + width // 2), BF16),
        in_specs=[vmem()] * 5,
        out_specs=vmem(),
        scratch_shapes=[
            pltpu.VMEM((live_dev * SUB, 2 * STATE), F32),
            pltpu.VMEM((live_dev * SUB, width), F32),
        ],
        compiler_params=params(),
        cost_estimate=cost(2 * slots * 512 * 1024, 2000000),
        name="answer",
    )(asked, live_near, conv_near, prefix, tail)
    lanes = answer.shape[1]
    got = lax.all_to_all(
        answer.reshape(gens, SUB, lanes), "gen", split_axis=0, concat_axis=0, tiled=True
    ).reshape(slots, lanes)

    pre_gate, pre_ss = pl.pallas_call(
        prompt_kernel,
        out_shape=(shape((span, width), F32), shape((SUB, span), F32)),
        in_specs=[vmem()] * 7,
        out_specs=(vmem(), vmem()),
        scratch_shapes=[pltpu.VMEM((128, span), F32)],
        compiler_params=params(),
        cost_estimate=cost(2 * heads * span * span * 128, 2500000, heads * span * span),
        name="prompt",
    )(xconv, pre_z[0], bct, cum, cumt, dtt, jnp.repeat(skip, width // heads)[None])

    count = steps * rows
    padded = -(-(span + count) // 128) * 128
    step_gate, sums = pl.pallas_call(
        lambda *refs: decode_kernel(live_dev, readers, *refs),
        out_shape=(shape((count, width), F32), shape((mp, SUB, padded), F32)),
        in_specs=[vmem()] * 13,
        out_specs=(vmem(), vmem()),
        compiler_params=params(),
        cost_estimate=cost(2 * 384 * 512 * 512, 2500000),
        name="decode",
    )(
        got,
        asked,
        tgt_l.reshape(-1, 1),
        tgt_r.reshape(-1, 1),
        step_xz,
        step_bc,
        step_raw.reshape(count, heads),
        decay[None],
        dt_bias[None],
        skip[None],
        conv_weight,
        conv_bias[None],
        pre_ss,
    )
    sums = lax.all_to_all(sums, "mp", split_axis=0, concat_axis=0, tiled=True)

    prefill_out, decoded = pl.pallas_call(
        lambda *refs: finish_kernel(width_all, *refs),
        out_shape=(shape((span, width), BF16), shape((count, width), BF16)),
        in_specs=[vmem()] * 4,
        out_specs=(vmem(), vmem()),
        compiler_params=params(),
        cost_estimate=cost(1000000, 2500000),
        name="finish",
    )(sums, pre_gate, step_gate, norm_gain[None])
    return (prefill_out[None], decoded.reshape(steps, rows, width))


def solution(mesh):
    placed = (
        P("gen", None, "mp"),
        P("gen", None, "mp"),
        P("gen", None, None, "mp"),
        P("gen", None, "mp"),
        P("gen"),
        P("gen", "mp", None, None),
        P("gen", None, "mp"),
        P("gen"),
        P("gen"),
        P(None, None, "gen", "mp"),
        P(None, None, "gen", "mp"),
        P(None, "gen", "mp"),
        P("mp"),
        P("mp"),
        P(None, "mp"),
        P("mp"),
        P("mp"),
        P("mp"),
    )
    return jax.shard_map(
        per_device,
        mesh=mesh,
        in_specs=placed,
        out_specs=(P("gen", None, "mp"), P(None, "gen", "mp")),
        check_vma=False,
    )
```

```python
import jax
import jax.numpy as jnp
from jax import lax
from jax.experimental import pallas as pl
from jax.experimental.pallas import tpu as pltpu
from jax.sharding import PartitionSpec as P

STATE = 64
EPS = 1e-05
SUB = 8
RING = 16
CHUNKS = 4
WHOLE = 60 * 1024 * 1024
F32 = jnp.float32
BF16 = jnp.bfloat16
NT = (((1,), (1,)), ((), ()))
TN = (((0,), (0,)), ((), ()))


def iota(shape, dim):
    return lax.broadcasted_iota(jnp.int32, shape, dim)


def mm(a, b):
    return jnp.dot(a, b, preferred_element_type=F32)


def mm_nt(a, b):
    return lax.dot_general(a, b, NT, preferred_element_type=F32)


def onehot(mask):
    return jnp.where(mask, 1.0, 0.0).astype(BF16)


def split2(x):
    hi = x.astype(BF16)
    return hi, (x - hi.astype(F32)).astype(BF16)


def split3(x):
    hi = x.astype(BF16)
    rest = x - hi.astype(F32)
    mid = rest.astype(BF16)
    return hi, mid, (rest - mid.astype(F32)).astype(BF16)


def silu(x):
    return x / (1.0 + jnp.exp(-x))


def softplus(x):
    return jnp.maximum(x, 0.0) + jnp.log1p(jnp.exp(-jnp.abs(x)))


def expander(heads, width):
    return onehot(iota((heads, width), 1) // (width // heads) == iota((heads, width), 0))


def spread(x, expand):
    hi, lo = split2(x)
    return mm(hi, expand) + mm(lo, expand)


def fetch(sources, targets, sems):
    copies = [
        pltpu.make_async_copy(source, target, sems.at[i])
        for i, (source, target) in enumerate(zip(sources, targets))
    ]
    for copy in copies:
        copy.start()
    return copies


def ask_kernel(ring, *refs):
    sources, out_ref, targets, sems = refs[:5], refs[5], refs[6:11], refs[11]
    for copy in fetch(sources, targets, sems):
        copy.wait()
    bc_ref, source_ref, reader_ref, len_ref, x_ref = targets
    steps = bc_ref.shape[0]
    slots = out_ref.shape[0]
    live_dev = source_ref.shape[1]
    readers = reader_ref.shape[1]
    span, width = x_ref.shape
    part = width // 4
    zeros_l = jnp.zeros((live_dev, STATE), F32)
    place = (iota((live_dev, STATE), 0) + 1).astype(F32)
    parts = [bc_ref[t, 1, 0:live_dev, :].astype(F32) for t in range(steps)]
    parts += [place] + [zeros_l] * (SUB - steps - 1)
    data_l = jnp.concatenate(parts, 0)
    data_l = jnp.concatenate([data_l, jnp.zeros_like(data_l)], 1).astype(BF16)
    parts = [
        bc_ref[t % steps, 1, live_dev : live_dev + readers, :].astype(F32) for t in range(SUB)
    ]
    data_r = jnp.concatenate(parts, 0)
    data_r = jnp.concatenate([jnp.zeros_like(data_r), data_r], 1).astype(BF16)

    def slot(gen):
        return (lax.rem(gen, ring) * (slots // SUB // ring) + lax.div(gen, ring)) * SUB

    first_l = slot(lax.div(source_ref[...], live_dev))
    first_r = slot(reader_ref[...])
    tgt_l = jnp.concatenate([first_l + r for r in range(SUB)], 1)
    tgt_r = jnp.concatenate([first_r + r for r in range(SUB)], 1)
    pick_l = onehot(iota((slots, SUB * live_dev), 0) == tgt_l)
    pick_r = onehot(iota((slots, SUB * readers), 0) == tgt_r)
    out_ref[:, 0 : 2 * STATE] = (mm(pick_l, data_l) + mm(pick_r, data_r)).astype(BF16)
    row, col = iota((2 * SUB, span), 0), iota((2 * SUB, span), 1)
    last = onehot(col == len_ref[...] - 2 + row // SUB)
    both = mm(last, x_ref[...])
    lane_part = iota((SUB, part), 0) % 4
    tail = jnp.zeros((SUB, part), F32)
    for i in range(4):
        lanes = slice(i * part, (i + 1) * part)
        piece = jnp.where(iota((SUB, part), 0) < 4, both[0:SUB, lanes], both[SUB:, lanes])
        tail = jnp.where(lane_part == i, piece, tail)
    tail = jnp.broadcast_to(tail[None], (slots // SUB, SUB, part))
    out_ref[:, 2 * STATE :] = tail.reshape(slots, part).astype(BF16)


def state_kernel(*refs):
    sources, outs, targets = refs[:8], refs[8:14], refs[14:22]
    sems, xf = refs[22], refs[23]
    xc_ref, cum_ref, cumt_ref, dtt_ref, st_ref, tail_ref = outs
    for copy in fetch(sources, targets, sems):
        copy.wait()
    len_ref, rawt_ref, decay_ref, bias_ref, cw_ref, cb_ref, bct_ref, x_ref = targets
    span, width = x_ref.shape
    heads = rawt_ref.shape[0]
    taps = cw_ref.shape[0]
    length = len_ref[...]
    xf[0:SUB, :] = jnp.zeros((SUB, width), F32)
    xf[SUB : SUB + span, :] = x_ref[...].astype(F32)
    square = iota((heads, heads), 0) == iota((heads, heads), 1)

    def column(row):
        return jnp.sum(jnp.where(square, row, 0.0), axis=1, keepdims=True)

    dtt = softplus(rawt_ref[...].astype(F32) + column(bias_ref[...]))
    dtt = jnp.where(iota((heads, span), 1) < length, dtt, 0.0)
    dtt_ref[...] = dtt
    tri = onehot(iota((span, span), 0) >= iota((span, span), 1))
    pieces = split3(dtt * -column(decay_ref[...]))
    cum_ref[...] = mm_nt(tri, pieces[0]) + mm_nt(tri, pieces[1]) + mm_nt(tri, pieces[2])
    cumt = mm_nt(pieces[0], tri) + mm_nt(pieces[1], tri) + mm_nt(pieces[2], tri)
    cumt_ref[...] = cumt
    weight = jnp.exp(cumt[:, span - 1 : span] - cumt) * dtt
    weight_hi, weight_lo = split2(weight)
    expand = expander(heads, width)
    weights = [cw_ref[k : k + 1, :].astype(F32) for k in range(taps)]
    block = 128
    total = jnp.zeros((STATE, width), F32)
    for start in range(0, span, block):
        part = slice(start, start + block)
        acc = cb_ref[...]
        for k in range(taps):
            first = SUB - taps + 1 + k + start
            acc = acc + xf[first : first + block, :] * weights[k]
        xc = silu(acc).astype(BF16)
        xc_ref[part, :] = xc
        wide = lax.dot_general(weight_hi[:, part], expand, TN, preferred_element_type=F32)
        wide = wide + lax.dot_general(
            weight_lo[:, part], expand, TN, preferred_element_type=F32
        )
        weighted = (xc.astype(F32) * wide).astype(BF16)
        total = total + mm(bct_ref[0, :, part], weighted)
    st_ref[0:STATE, :] = jnp.zeros((STATE, width), BF16)
    st_ref[STATE : 2 * STATE, :] = total.astype(BF16)
    row, col = iota((SUB, span), 0), iota((SUB, span), 1)
    tail = onehot((col == length - (taps - 1)) & (row == SUB - 1))
    tail_ref[...] = mm(tail, x_ref[...]).astype(BF16)


def prompt_kernel(
    xc_ref, z_ref, bct_ref, cum_ref, cumt_ref, dtt_ref, skip_ref, g_ref, ss_ref, scores
):
    span, width = xc_ref.shape
    heads = cum_ref.shape[1]
    block = 128
    ones = jnp.ones((SUB, block), BF16)
    lanes = iota((block, block), 1)
    causal = iota((block, block), 0) >= lanes
    for start in range(0, span, block):
        stop = start + block
        scores[:, 0:stop] = lax.dot_general(
            bct_ref[1, :, start:stop], bct_ref[0, :, 0:stop], TN, preferred_element_type=F32
        )
        square = jnp.zeros((block, block), F32)
        for lane in range(0, width, block):
            halves = []
            for half in range(2):
                head = lane * heads // width + half
                at = cum_ref[start:stop, head : head + 1]
                gap = jnp.where(causal, at - cumt_ref[head : head + 1, start:stop], -jnp.inf)
                near = scores[:, start:stop] * jnp.exp(gap) * dtt_ref[head : head + 1, start:stop]
                yhead = mm(near.astype(BF16), xc_ref[start:stop, lane : lane + block])
                if start:
                    gap = at - cumt_ref[head : head + 1, 0:start]
                    far = scores[:, 0:start] * jnp.exp(gap) * dtt_ref[head : head + 1, 0:start]
                    yhead = yhead + mm(far.astype(BF16), xc_ref[0:start, lane : lane + block])
                halves.append(yhead)
            y = jnp.where(lanes < block // 2, halves[0], halves[1])
            xin = xc_ref[start:stop, lane : lane + block].astype(F32)
            y = y + skip_ref[:, lane : lane + block] * xin
            gate = y * silu(z_ref[start:stop, lane : lane + block].astype(F32))
            g_ref[start:stop, lane : lane + block] = gate
            square = square + gate * gate
        hi, lo = split2(square)
        ss_ref[:, start:stop] = mm_nt(ones, hi) + mm_nt(ones, lo)


def answer_kernel(*refs):
    sources, live_hbm, out_ref, targets = refs[:4], refs[4], refs[5], refs[6:10]
    state_ref, sems, cs, ys = refs[10:]
    chunk = state_ref.shape[0] // CHUNKS
    chunks = [slice(i * chunk, (i + 1) * chunk) for i in range(CHUNKS)]
    copies = fetch(
        sources + tuple(live_hbm.at[part] for part in chunks),
        targets + tuple(state_ref.at[part] for part in chunks),
        sems,
    )
    for copy in copies[:4]:
        copy.wait()
    ask_ref, conv_ref, prefix_ref, tail_ref = targets
    slots = ask_ref.shape[0]
    live_dev = state_ref.shape[0]
    count = ys.shape[0]
    width = prefix_ref.shape[1]
    half = width // 2
    ask = ask_ref[:, 0 : 2 * STATE]
    row, col = iota((slots, slots), 0), iota((slots, slots), 1)
    place = mm(onehot(col == (row // SUB) * SUB + 4), ask)
    lane0 = onehot(iota((SUB, 2 * STATE), 1) == 0)
    across = mm_nt(lane0, place.astype(BF16))[0:1, :].astype(jnp.int32)
    row, col = iota((count, slots), 0), iota((count, slots), 1)
    back = onehot(row + SUB - col % SUB == across * SUB)
    got = mm(back, ask)
    cs[...] = jnp.where(iota(got.shape, 0) % SUB < 4, got, 0.0)
    for k in range(live_dev):
        if k % chunk == 0:
            copies[4 + k // chunk].wait()
        rows = slice(k * SUB, (k + 1) * SUB)
        ys[rows, :] = mm_nt(cs[rows, 0:STATE].astype(BF16), state_ref[k])
    place = place[:, 0:1].astype(jnp.int32)
    row, col = iota((slots, count), 0), iota((slots, count), 1)
    there = onehot(col + SUB - row % SUB == place * SUB)
    live = mm(there, ys[...].astype(BF16))
    kept = conv_ref.shape[0]
    row, col = iota((slots, kept), 0), iota((slots, kept), 1)
    there = onehot(
        (lax.div(col, live_dev) + 4 == row % SUB) & (col % live_dev + 1 == place)
    )
    live = (live + mm(there, conv_ref[...])).reshape(slots // SUB, SUB, width)
    live = live + tail_ref[...].astype(F32)[None]
    out_ref[:, 0:width] = live.reshape(slots, width).astype(BF16)
    new = mm(ask, prefix_ref[...])
    first = iota((slots, half), 0) % SUB < SUB // 2
    new = jnp.where(first, new[:, 0:half], new[:, half:width])
    out_ref[:, width : width + half] = new.astype(BF16)


def decode_kernel(
    live_dev,
    readers,
    got_ref,
    ask_ref,
    tgt_l_ref,
    tgt_r_ref,
    xz_ref,
    bc_ref,
    raw_ref,
    decay_ref,
    bias_ref,
    skip_ref,
    cw_ref,
    cb_ref,
    pre_ss_ref,
    g_ref,
    ss_ref,
):
    slots = got_ref.shape[0]
    steps, _, rows, width = xz_ref.shape
    heads = raw_ref.shape[1]
    span = pre_ss_ref.shape[1]
    taps = cw_ref.shape[0]
    half = width // 2
    pick_l = onehot(iota((SUB * live_dev, slots), 1) == tgt_l_ref[...])
    pick_r = onehot(iota((SUB * readers, slots), 1) == tgt_r_ref[...])
    live = mm(pick_l, got_ref[:, 0:width])
    new = mm(pick_r, got_ref[:, width:])
    old = mm(pick_r[(SUB - 1) * readers :, :], got_ref[:, 0:width])
    late = mm(pick_r, ask_ref[:, 2 * STATE :])

    def live_row(r):
        return live[r * live_dev : (r + 1) * live_dev, :]

    def new_row(r, first, last):
        return new[r * readers : (r + 1) * readers, first:last]

    def tail_row(r):
        return jnp.concatenate(
            [late[(r + i) * readers : (r + i + 1) * readers, :] for i in range(4)], 1
        )

    first = []
    for t in range(steps):
        wide = jnp.concatenate([new_row(t, 0, half), new_row(t + 4, 0, half)], 1)
        first.append(jnp.concatenate([live_row(t), wide], 0))
    inputs = [
        jnp.concatenate([live_row(4), old], 0),
        jnp.concatenate([live_row(5), tail_row(0)], 0),
        jnp.concatenate([live_row(6), tail_row(4)], 0),
    ]
    inputs += [xz_ref[t, 0].astype(F32) for t in range(steps)]
    expand = expander(heads, width)
    weights = [cw_ref[k : k + 1, :].astype(F32) for k in range(taps)]
    dts, logs, bmats, cmats, xcs, gates = [], [], [], [], [], []
    for t in range(steps):
        acc = cb_ref[...]
        for k in range(taps):
            acc = acc + inputs[t + k] * weights[k]
        xcs.append(silu(acc).astype(BF16).astype(F32))
        dt = softplus(raw_ref[t * rows : (t + 1) * rows, :].astype(F32) + bias_ref[...])
        dts.append(dt)
        decayed = -dt * decay_ref[...]
        logs.append(decayed if t == 0 else logs[-1] + decayed)
        bmats.append(bc_ref[t, 0].astype(F32))
        cmats.append(bc_ref[t, 1].astype(F32))
        y = spread(jnp.exp(logs[t]), expand) * first[t]
        for s in range(t + 1):
            score = jnp.sum(bmats[s] * cmats[t], axis=1, keepdims=True)
            factor = dts[s] * score
            if s < t:
                factor = jnp.exp(logs[t] - logs[s]) * factor
            else:
                factor = factor + skip_ref[...]
            y = y + spread(factor, expand) * xcs[s]
        gate = y * silu(xz_ref[t, 1].astype(F32))
        g_ref[t * rows : (t + 1) * rows, :] = gate
        gates.append(gate * gate)
    square = jnp.concatenate(gates, 0)
    hi, lo = split2(square)
    ones = jnp.ones((SUB, width), BF16)
    sums = mm_nt(ones, hi) + mm_nt(ones, lo)
    lanes = ss_ref.shape[2]
    pad = -sums.shape[1] % lanes
    sums = jnp.concatenate([pre_ss_ref[...], sums, jnp.zeros((SUB, pad), F32)], 1)
    parts = [sums[0:1, i : i + lanes] for i in range(0, sums.shape[1], lanes)]
    parts += [jnp.zeros((SUB - len(parts), lanes), F32)]
    ss_ref[...] = jnp.broadcast_to(jnp.concatenate(parts, 0)[None], ss_ref.shape)


def finish_kernel(width_all, ss_ref, pre_ref, step_ref, gain_ref, pre_out_ref, step_out_ref):
    total = ss_ref[0]
    for i in range(1, ss_ref.shape[0]):
        total = total + ss_ref[i]
    scale = lax.rsqrt(total / width_all + EPS)
    gain = gain_ref[...]
    span = pre_ref.shape[0]
    block = 128

    def column(first, rows):
        row = scale[first // block : first // block + 1, :]
        diag = iota((rows, block), 0) == iota((rows, block), 1)
        return jnp.sum(jnp.where(diag, row, 0.0), axis=1, keepdims=True)

    for start in range(0, span, block):
        part = slice(start, start + block)
        pre_out_ref[part, :] = (pre_ref[part, :] * column(start, block) * gain).astype(BF16)
    count = step_ref.shape[0]
    for start in range(0, count, block):
        rows = min(block, count - start)
        part = slice(start, start + rows)
        step_out_ref[part, :] = (step_ref[part, :] * column(span + start, rows) * gain).astype(
            BF16
        )


def params(limit=24 * 1024 * 1024, **more):
    return pltpu.CompilerParams(vmem_limit_bytes=limit, **more)


def cost(flops, moved, special=0):
    return pl.CostEstimate(flops=flops, bytes_accessed=moved, transcendentals=special)


def vmem():
    return pl.BlockSpec(memory_space=pltpu.VMEM)


def hbm():
    return pl.BlockSpec(memory_space=pltpu.HBM)


def shape(dims, kind):
    return jax.ShapeDtypeStruct(dims, kind)


def per_device(
    pre_x,
    pre_z,
    pre_bc,
    pre_raw,
    prompt_len,
    live_state,
    live_conv,
    source,
    reader,
    step_xz,
    step_bc,
    step_raw,
    decay,
    dt_bias,
    conv_weight,
    conv_bias,
    skip,
    norm_gain,
):
    _, span, width = pre_x.shape
    mp = lax.axis_size("mp")
    gens = lax.axis_size("gen")
    width_all = width * mp
    live_dev = source.shape[0]
    readers = reader.shape[0]
    heads = pre_raw.shape[2]
    steps, _, rows, _ = step_xz.shape
    slots = gens * SUB
    offset = jnp.arange(SUB, dtype=jnp.int32)[:, None]
    tgt_l = SUB * (source // live_dev)[None, :] + offset
    tgt_r = SUB * reader[None, :] + offset

    length = prompt_len.reshape(1, 1)
    conv_rows = jnp.transpose(live_conv, (1, 0, 2)).reshape(-1, width)
    bct = jnp.swapaxes(pre_bc[0], 1, 2)
    dma = pltpu.SemaphoreType.DMA

    def staged(*arrays):
        return [pltpu.VMEM(array.shape, array.dtype) for array in arrays]

    operands = (step_bc, source[None], reader[None], length, pre_x[0])
    ask = pl.pallas_call(
        lambda *refs: ask_kernel(RING, *refs),
        out_shape=shape((slots, 2 * STATE + width // 4), BF16),
        in_specs=[hbm()] * len(operands),
        out_specs=vmem(),
        scratch_shapes=staged(*operands) + [dma((len(operands),))],
        compiler_params=params(WHOLE),
        cost_estimate=cost(2 * slots * 384 * 128, 800000),
        name="ask",
    )(*operands)
    lanes = ask.shape[1]
    outer = gens // RING
    along_z = [[y * RING + z for z in range(RING)] for y in range(outer)]
    along_y = [[y * RING + z for y in range(outer)] for z in range(RING)]
    asked = lax.all_to_all(
        ask.reshape(gens, SUB, lanes), "gen", 0, 0, axis_index_groups=along_z, tiled=True
    )
    asked = jnp.swapaxes(asked.reshape(RING, outer, SUB, lanes), 0, 1)
    asked = lax.all_to_all(
        asked.reshape(gens, SUB, lanes), "gen", 0, 0, axis_index_groups=along_y, tiled=True
    ).reshape(slots, lanes)

    live = live_state.reshape(live_dev, width, STATE)
    operands = (
        length,
        pre_raw[0].T,
        decay[None],
        dt_bias[None],
        conv_weight,
        conv_bias[None],
        bct,
        pre_x[0],
    )
    xconv, cum, cumt, dtt, prefix, tail = pl.pallas_call(
        state_kernel,
        out_shape=(
            shape((span, width), BF16),
            shape((span, heads), F32),
            shape((heads, span), F32),
            shape((heads, span), F32),
            shape((2 * STATE, width), BF16),
            shape((SUB, width), BF16),
        ),
        in_specs=[hbm()] * len(operands),
        out_specs=(vmem(),) * 6,
        scratch_shapes=staged(*operands)
        + [dma((len(operands),)), pltpu.VMEM((span + SUB, width), F32)],
        compiler_params=params(WHOLE),
        cost_estimate=cost(2 * 10 * span * span * 64, 2000000, span * width * 2),
        name="state",
    )(*operands)

    operands = (asked, conv_rows, prefix, tail)
    answer = pl.pallas_call(
        answer_kernel,
        out_shape=shape((slots, width + width // 2), BF16),
        in_specs=[hbm()] * (len(operands) + 1),
        out_specs=vmem(),
        scratch_shapes=staged(*operands, live)
        + [
            dma((len(operands) + CHUNKS,)),
            pltpu.VMEM((live_dev * SUB, 2 * STATE), F32),
            pltpu.VMEM((live_dev * SUB, width), F32),
        ],
        compiler_params=params(WHOLE),
        cost_estimate=cost(2 * slots * 512 * 1024, 6000000),
        name="answer",
    )(*operands, live)
    lanes = answer.shape[1]
    got = lax.all_to_all(
        answer.reshape(gens, SUB, lanes), "gen", split_axis=0, concat_axis=0, tiled=True
    ).reshape(slots, lanes)

    pre_gate, pre_ss = pl.pallas_call(
        prompt_kernel,
        out_shape=(shape((span, width), F32), shape((SUB, span), F32)),
        in_specs=[vmem()] * 7,
        out_specs=(vmem(), vmem()),
        scratch_shapes=[pltpu.VMEM((128, span), F32)],
        compiler_params=params(),
        cost_estimate=cost(2 * heads * span * span * 128, 2500000, heads * span * span),
        name="prompt",
    )(xconv, pre_z[0], bct, cum, cumt, dtt, jnp.repeat(skip, width // heads)[None])

    count = steps * rows
    step_gate, sums = pl.pallas_call(
        lambda *refs: decode_kernel(live_dev, readers, *refs),
        out_shape=(shape((count, width), F32), shape((mp, SUB, 128), F32)),
        in_specs=[vmem()] * 13,
        out_specs=(vmem(), vmem()),
        compiler_params=params(),
        cost_estimate=cost(2 * 384 * 512 * 512, 2500000),
        name="decode",
    )(
        got,
        asked,
        tgt_l.reshape(-1, 1),
        tgt_r.reshape(-1, 1),
        step_xz,
        step_bc,
        step_raw.reshape(count, heads),
        decay[None],
        dt_bias[None],
        skip[None],
        conv_weight,
        conv_bias[None],
        pre_ss,
    )
    sums = lax.all_to_all(sums, "mp", split_axis=0, concat_axis=0, tiled=True)

    prefill_out, decoded = pl.pallas_call(
        lambda *refs: finish_kernel(width_all, *refs),
        out_shape=(shape((span, width), BF16), shape((count, width), BF16)),
        in_specs=[vmem()] * 4,
        out_specs=(vmem(), vmem()),
        compiler_params=params(),
        cost_estimate=cost(1000000, 2500000),
        name="finish",
    )(sums, pre_gate, step_gate, norm_gain[None])
    return (prefill_out[None], decoded.reshape(steps, rows, width))


def solution(mesh):
    placed = (
        P("gen", None, "mp"),
        P("gen", None, "mp"),
        P("gen", None, None, "mp"),
        P("gen", None, "mp"),
        P("gen"),
        P("gen", "mp", None, None),
        P("gen", None, "mp"),
        P("gen"),
        P("gen"),
        P(None, None, "gen", "mp"),
        P(None, None, "gen", "mp"),
        P(None, "gen", "mp"),
        P("mp"),
        P("mp"),
        P(None, "mp"),
        P("mp"),
        P("mp"),
        P("mp"),
    )
    return jax.shard_map(
        per_device,
        mesh=mesh,
        in_specs=placed,
        out_specs=(P("gen", None, "mp"), P(None, "gen", "mp")),
        check_vma=False,
    )
```

```python
import jax
import jax.numpy as jnp
from jax import lax
from jax.experimental import pallas as pl
from jax.experimental.pallas import tpu as pltpu
from jax.sharding import PartitionSpec as P

STATE = 64
EPS = 1e-05
SUB = 8
CHUNKS = 4
WHOLE = 60 * 1024 * 1024
F32 = jnp.float32
BF16 = jnp.bfloat16
NT = (((1,), (1,)), ((), ()))
TN = (((0,), (0,)), ((), ()))


def iota(shape, dim):
    return lax.broadcasted_iota(jnp.int32, shape, dim)


def mm(a, b):
    return jnp.dot(a, b, preferred_element_type=F32)


def mm_nt(a, b):
    return lax.dot_general(a, b, NT, preferred_element_type=F32)


def onehot(mask):
    return jnp.where(mask, 1.0, 0.0).astype(BF16)


def split2(x):
    hi = x.astype(BF16)
    return hi, (x - hi.astype(F32)).astype(BF16)


def split3(x):
    hi = x.astype(BF16)
    rest = x - hi.astype(F32)
    mid = rest.astype(BF16)
    return hi, mid, (rest - mid.astype(F32)).astype(BF16)


def silu(x):
    return x / (1.0 + jnp.exp(-x))


def softplus(x):
    return jnp.maximum(x, 0.0) + jnp.log1p(jnp.exp(-jnp.abs(x)))


def expander(heads, width):
    return onehot(iota((heads, width), 1) // (width // heads) == iota((heads, width), 0))


def spread(x, expand):
    hi, lo = split2(x)
    return mm(hi, expand) + mm(lo, expand)


def fetch(sources, targets, sems):
    copies = [
        pltpu.make_async_copy(source, target, sems.at[i])
        for i, (source, target) in enumerate(zip(sources, targets))
    ]
    for copy in copies:
        copy.start()
    return copies


def ask_kernel(*refs):
    sources, out_ref, targets, sems = refs[:5], refs[5], refs[6:11], refs[11]
    for copy in fetch(sources, targets, sems):
        copy.wait()
    bc_ref, source_ref, reader_ref, len_ref, x_ref = targets
    steps = bc_ref.shape[0]
    slots = out_ref.shape[0]
    live_dev = source_ref.shape[1]
    readers = reader_ref.shape[1]
    span, width = x_ref.shape
    part = width // 4
    zeros_l = jnp.zeros((live_dev, STATE), F32)
    place = (iota((live_dev, STATE), 0) + 1).astype(F32)
    parts = [bc_ref[t, 1, 0:live_dev, :].astype(F32) for t in range(steps)]
    parts += [place] + [zeros_l] * (SUB - steps - 1)
    data_l = jnp.concatenate(parts, 0)
    data_l = jnp.concatenate([data_l, jnp.zeros_like(data_l)], 1).astype(BF16)
    parts = [
        bc_ref[t % steps, 1, live_dev : live_dev + readers, :].astype(F32) for t in range(SUB)
    ]
    data_r = jnp.concatenate(parts, 0)
    data_r = jnp.concatenate([jnp.zeros_like(data_r), data_r], 1).astype(BF16)
    first_l = lax.div(source_ref[...], live_dev) * SUB
    first_r = reader_ref[...] * SUB
    tgt_l = jnp.concatenate([first_l + r for r in range(SUB)], 1)
    tgt_r = jnp.concatenate([first_r + r for r in range(SUB)], 1)
    pick_l = onehot(iota((slots, SUB * live_dev), 0) == tgt_l)
    pick_r = onehot(iota((slots, SUB * readers), 0) == tgt_r)
    out_ref[:, 0 : 2 * STATE] = (mm(pick_l, data_l) + mm(pick_r, data_r)).astype(BF16)
    row, col = iota((2 * SUB, span), 0), iota((2 * SUB, span), 1)
    last = onehot(col == len_ref[...] - 2 + row // SUB)
    both = mm(last, x_ref[...])
    lane_part = iota((SUB, part), 0) % 4
    tail = jnp.zeros((SUB, part), F32)
    for i in range(4):
        lanes = slice(i * part, (i + 1) * part)
        piece = jnp.where(iota((SUB, part), 0) < 4, both[0:SUB, lanes], both[SUB:, lanes])
        tail = jnp.where(lane_part == i, piece, tail)
    tail = jnp.broadcast_to(tail[None], (slots // SUB, SUB, part))
    out_ref[:, 2 * STATE :] = tail.reshape(slots, part).astype(BF16)


def state_kernel(*refs):
    sources, outs, targets = refs[:8], refs[8:14], refs[14:22]
    sems, xf = refs[22], refs[23]
    xc_ref, cum_ref, cumt_ref, dtt_ref, st_ref, tail_ref = outs
    for copy in fetch(sources, targets, sems):
        copy.wait()
    len_ref, rawt_ref, decay_ref, bias_ref, cw_ref, cb_ref, bct_ref, x_ref = targets
    span, width = x_ref.shape
    heads = rawt_ref.shape[0]
    taps = cw_ref.shape[0]
    length = len_ref[...]
    xf[0:SUB, :] = jnp.zeros((SUB, width), F32)
    xf[SUB : SUB + span, :] = x_ref[...].astype(F32)
    square = iota((heads, heads), 0) == iota((heads, heads), 1)

    def column(row):
        return jnp.sum(jnp.where(square, row, 0.0), axis=1, keepdims=True)

    dtt = softplus(rawt_ref[...].astype(F32) + column(bias_ref[...]))
    dtt = jnp.where(iota((heads, span), 1) < length, dtt, 0.0)
    dtt_ref[...] = dtt
    tri = onehot(iota((span, span), 0) >= iota((span, span), 1))
    pieces = split3(dtt * -column(decay_ref[...]))
    cum_ref[...] = mm_nt(tri, pieces[0]) + mm_nt(tri, pieces[1]) + mm_nt(tri, pieces[2])
    cumt = mm_nt(pieces[0], tri) + mm_nt(pieces[1], tri) + mm_nt(pieces[2], tri)
    cumt_ref[...] = cumt
    weight = jnp.exp(cumt[:, span - 1 : span] - cumt) * dtt
    weight_hi, weight_lo = split2(weight)
    expand = expander(heads, width)
    weights = [cw_ref[k : k + 1, :].astype(F32) for k in range(taps)]
    block = 128
    total = jnp.zeros((STATE, width), F32)
    for start in range(0, span, block):
        part = slice(start, start + block)
        acc = cb_ref[...]
        for k in range(taps):
            first = SUB - taps + 1 + k + start
            acc = acc + xf[first : first + block, :] * weights[k]
        xc = silu(acc).astype(BF16)
        xc_ref[part, :] = xc
        wide = lax.dot_general(weight_hi[:, part], expand, TN, preferred_element_type=F32)
        wide = wide + lax.dot_general(
            weight_lo[:, part], expand, TN, preferred_element_type=F32
        )
        weighted = (xc.astype(F32) * wide).astype(BF16)
        total = total + mm(bct_ref[0, :, part], weighted)
    st_ref[0:STATE, :] = jnp.zeros((STATE, width), BF16)
    st_ref[STATE : 2 * STATE, :] = total.astype(BF16)
    row, col = iota((SUB, span), 0), iota((SUB, span), 1)
    tail = onehot((col == length - (taps - 1)) & (row == SUB - 1))
    tail_ref[...] = mm(tail, x_ref[...]).astype(BF16)


def prompt_kernel(
    xc_ref,
    z_ref,
    bct_ref,
    cum_ref,
    cumt_ref,
    dtt_ref,
    skip_ref,
    ask_ref,
    tgt_r_ref,
    g_ref,
    ss_ref,
    late_ref,
    scores,
):
    readers = late_ref.shape[0] // 2
    part = ask_ref.shape[1] - 2 * STATE
    pick_r = onehot(iota((SUB * readers, ask_ref.shape[0]), 1) == tgt_r_ref[...])
    late = mm(pick_r, ask_ref[:, 2 * STATE :])
    for r in range(SUB):
        rows = slice(r // 4 * readers, (r // 4 + 1) * readers)
        late_ref[rows, r % 4 * part : (r % 4 + 1) * part] = late[
            r * readers : (r + 1) * readers, :
        ]
    span, width = xc_ref.shape
    heads = cum_ref.shape[1]
    block = 128
    ones = jnp.ones((SUB, block), BF16)
    lanes = iota((block, block), 1)
    causal = iota((block, block), 0) >= lanes
    for start in range(0, span, block):
        stop = start + block
        scores[:, 0:stop] = lax.dot_general(
            bct_ref[1, :, start:stop], bct_ref[0, :, 0:stop], TN, preferred_element_type=F32
        )
        square = jnp.zeros((block, block), F32)
        for lane in range(0, width, block):
            halves = []
            for half in range(2):
                head = lane * heads // width + half
                at = cum_ref[start:stop, head : head + 1]
                gap = jnp.where(causal, at - cumt_ref[head : head + 1, start:stop], -jnp.inf)
                near = scores[:, start:stop] * jnp.exp(gap) * dtt_ref[head : head + 1, start:stop]
                yhead = mm(near.astype(BF16), xc_ref[start:stop, lane : lane + block])
                if start:
                    gap = at - cumt_ref[head : head + 1, 0:start]
                    far = scores[:, 0:start] * jnp.exp(gap) * dtt_ref[head : head + 1, 0:start]
                    yhead = yhead + mm(far.astype(BF16), xc_ref[0:start, lane : lane + block])
                halves.append(yhead)
            y = jnp.where(lanes < block // 2, halves[0], halves[1])
            xin = xc_ref[start:stop, lane : lane + block].astype(F32)
            y = y + skip_ref[:, lane : lane + block] * xin
            gate = y * silu(z_ref[start:stop, lane : lane + block].astype(F32))
            g_ref[start:stop, lane : lane + block] = gate
            square = square + gate * gate
        hi, lo = split2(square)
        ss_ref[:, start:stop] = mm_nt(ones, hi) + mm_nt(ones, lo)


def answer_kernel(*refs):
    sources, live_hbm, out_ref, targets = refs[:4], refs[4], refs[5], refs[6:10]
    state_ref, sems, cs, ys = refs[10:]
    chunk = state_ref.shape[0] // CHUNKS
    chunks = [slice(i * chunk, (i + 1) * chunk) for i in range(CHUNKS)]
    copies = fetch(
        sources + tuple(live_hbm.at[part] for part in chunks),
        targets + tuple(state_ref.at[part] for part in chunks),
        sems,
    )
    for copy in copies[:4]:
        copy.wait()
    ask_ref, conv_ref, prefix_ref, tail_ref = targets
    slots = ask_ref.shape[0]
    live_dev = state_ref.shape[0]
    count = ys.shape[0]
    width = prefix_ref.shape[1]
    half = width // 2
    ask = ask_ref[:, 0 : 2 * STATE]
    row, col = iota((slots, slots), 0), iota((slots, slots), 1)
    place = mm(onehot(col == (row // SUB) * SUB + 4), ask)
    lane0 = onehot(iota((SUB, 2 * STATE), 1) == 0)
    across = mm_nt(lane0, place.astype(BF16))[0:1, :].astype(jnp.int32)
    row, col = iota((count, slots), 0), iota((count, slots), 1)
    back = onehot(row + SUB - col % SUB == across * SUB)
    got = mm(back, ask)
    cs[...] = jnp.where(iota(got.shape, 0) % SUB < 4, got, 0.0)
    for k in range(live_dev):
        if k % chunk == 0:
            copies[4 + k // chunk].wait()
        rows = slice(k * SUB, (k + 1) * SUB)
        ys[rows, :] = mm_nt(cs[rows, 0:STATE].astype(BF16), state_ref[k])
    place = place[:, 0:1].astype(jnp.int32)
    row, col = iota((slots, count), 0), iota((slots, count), 1)
    there = onehot(col + SUB - row % SUB == place * SUB)
    live = mm(there, ys[...].astype(BF16))
    kept = conv_ref.shape[0]
    row, col = iota((slots, kept), 0), iota((slots, kept), 1)
    there = onehot(
        (lax.div(col, live_dev) + 4 == row % SUB) & (col % live_dev + 1 == place)
    )
    live = (live + mm(there, conv_ref[...])).reshape(slots // SUB, SUB, width)
    live = live + tail_ref[...].astype(F32)[None]
    out_ref[:, 0:width] = live.reshape(slots, width).astype(BF16)
    new = mm(ask, prefix_ref[...])
    first = iota((slots, half), 0) % SUB < SUB // 2
    new = jnp.where(first, new[:, 0:half], new[:, half:width])
    out_ref[:, width : width + half] = new.astype(BF16)


def decode_kernel(
    live_dev,
    readers,
    got_ref,
    late_ref,
    tgt_l_ref,
    tgt_r_ref,
    xz_ref,
    bc_ref,
    raw_ref,
    decay_ref,
    bias_ref,
    skip_ref,
    cw_ref,
    cb_ref,
    pre_ss_ref,
    g_ref,
    ss_ref,
):
    slots = got_ref.shape[0]
    steps, _, rows, width = xz_ref.shape
    heads = raw_ref.shape[1]
    span = pre_ss_ref.shape[1]
    taps = cw_ref.shape[0]
    half = width // 2
    pick_l = onehot(iota((SUB * live_dev, slots), 1) == tgt_l_ref[...])
    pick_r = onehot(iota((SUB * readers, slots), 1) == tgt_r_ref[...])
    live = mm(pick_l, got_ref[:, 0:width])
    new = mm(pick_r, got_ref[:, width:])
    old = mm(pick_r[(SUB - 1) * readers :, :], got_ref[:, 0:width])

    def live_row(r):
        return live[r * live_dev : (r + 1) * live_dev, :]

    def new_row(r, first, last):
        return new[r * readers : (r + 1) * readers, first:last]

    first = []
    for t in range(steps):
        wide = jnp.concatenate([new_row(t, 0, half), new_row(t + 4, 0, half)], 1)
        first.append(jnp.concatenate([live_row(t), wide], 0))
    inputs = [
        jnp.concatenate([live_row(4), old], 0),
        jnp.concatenate([live_row(5), late_ref[0:readers, :]], 0),
        jnp.concatenate([live_row(6), late_ref[readers:, :]], 0),
    ]
    inputs += [xz_ref[t, 0].astype(F32) for t in range(steps)]
    expand = expander(heads, width)
    weights = [cw_ref[k : k + 1, :].astype(F32) for k in range(taps)]
    dts, logs, bmats, cmats, xcs, gates = [], [], [], [], [], []
    for t in range(steps):
        acc = cb_ref[...]
        for k in range(taps):
            acc = acc + inputs[t + k] * weights[k]
        xcs.append(silu(acc).astype(BF16).astype(F32))
        dt = softplus(raw_ref[t * rows : (t + 1) * rows, :].astype(F32) + bias_ref[...])
        dts.append(dt)
        decayed = -dt * decay_ref[...]
        logs.append(decayed if t == 0 else logs[-1] + decayed)
        bmats.append(bc_ref[t, 0].astype(F32))
        cmats.append(bc_ref[t, 1].astype(F32))
        y = spread(jnp.exp(logs[t]), expand) * first[t]
        for s in range(t + 1):
            score = jnp.sum(bmats[s] * cmats[t], axis=1, keepdims=True)
            factor = dts[s] * score
            if s < t:
                factor = jnp.exp(logs[t] - logs[s]) * factor
            else:
                factor = factor + skip_ref[...]
            y = y + spread(factor, expand) * xcs[s]
        gate = y * silu(xz_ref[t, 1].astype(F32))
        g_ref[t * rows : (t + 1) * rows, :] = gate
        gates.append(gate * gate)
    square = jnp.concatenate(gates, 0)
    hi, lo = split2(square)
    ones = jnp.ones((SUB, width), BF16)
    sums = mm_nt(ones, hi) + mm_nt(ones, lo)
    lanes = ss_ref.shape[1]
    pad = -sums.shape[1] % lanes
    sums = jnp.concatenate([pre_ss_ref[...], sums, jnp.zeros((SUB, pad), F32)], 1)
    parts = [sums[0:1, i : i + lanes] for i in range(0, sums.shape[1], lanes)]
    parts += [jnp.zeros((SUB - len(parts), lanes), F32)]
    ss_ref[...] = jnp.concatenate(parts, 0)


def finish_kernel(width_all, *refs):
    sums, (pre_ref, step_ref, gain_ref, pre_out_ref, step_out_ref) = refs[:-5], refs[-5:]
    total = sums[0][...]
    for part in sums[1:]:
        total = total + part[...]
    scale = lax.rsqrt(total / width_all + EPS)
    gain = gain_ref[...]
    span = pre_ref.shape[0]
    block = 128

    def column(first, rows):
        row = scale[first // block : first // block + 1, :]
        diag = iota((rows, block), 0) == iota((rows, block), 1)
        return jnp.sum(jnp.where(diag, row, 0.0), axis=1, keepdims=True)

    for start in range(0, span, block):
        part = slice(start, start + block)
        pre_out_ref[part, :] = (pre_ref[part, :] * column(start, block) * gain).astype(BF16)
    count = step_ref.shape[0]
    for start in range(0, count, block):
        rows = min(block, count - start)
        part = slice(start, start + rows)
        step_out_ref[part, :] = (step_ref[part, :] * column(span + start, rows) * gain).astype(
            BF16
        )


def params(limit=24 * 1024 * 1024, **more):
    return pltpu.CompilerParams(vmem_limit_bytes=limit, **more)


def cost(flops, moved, special=0):
    return pl.CostEstimate(flops=flops, bytes_accessed=moved, transcendentals=special)


def vmem():
    return pl.BlockSpec(memory_space=pltpu.VMEM)


def hbm():
    return pl.BlockSpec(memory_space=pltpu.HBM)


def shape(dims, kind):
    return jax.ShapeDtypeStruct(dims, kind)


def per_device(
    pre_x,
    pre_z,
    pre_bc,
    pre_raw,
    prompt_len,
    live_state,
    live_conv,
    source,
    reader,
    step_xz,
    step_bc,
    step_raw,
    decay,
    dt_bias,
    conv_weight,
    conv_bias,
    skip,
    norm_gain,
):
    _, span, width = pre_x.shape
    mp = lax.axis_size("mp")
    gens = lax.axis_size("gen")
    width_all = width * mp
    live_dev = source.shape[0]
    readers = reader.shape[0]
    heads = pre_raw.shape[2]
    steps, _, rows, _ = step_xz.shape
    slots = gens * SUB
    offset = jnp.arange(SUB, dtype=jnp.int32)[:, None]
    tgt_l = SUB * (source // live_dev)[None, :] + offset
    tgt_r = SUB * reader[None, :] + offset

    length = prompt_len.reshape(1, 1)
    conv_rows = jnp.transpose(live_conv, (1, 0, 2)).reshape(-1, width)
    bct = jnp.swapaxes(pre_bc[0], 1, 2)
    dma = pltpu.SemaphoreType.DMA

    def staged(*arrays):
        return [pltpu.VMEM(array.shape, array.dtype) for array in arrays]

    operands = (step_bc, source[None], reader[None], length, pre_x[0])
    ask = pl.pallas_call(
        ask_kernel,
        out_shape=shape((slots, 2 * STATE + width // 4), BF16),
        in_specs=[hbm()] * len(operands),
        out_specs=vmem(),
        scratch_shapes=staged(*operands) + [dma((len(operands),))],
        compiler_params=params(WHOLE),
        cost_estimate=cost(2 * slots * 384 * 128, 800000),
        name="ask",
    )(*operands)
    lanes = ask.shape[1]
    asked = lax.all_to_all(
        ask.reshape(gens, SUB, lanes), "gen", split_axis=0, concat_axis=0, tiled=True
    ).reshape(slots, lanes)

    live = live_state.reshape(live_dev, width, STATE)
    operands = (
        length,
        pre_raw[0].T,
        decay[None],
        dt_bias[None],
        conv_weight,
        conv_bias[None],
        bct,
        pre_x[0],
    )
    xconv, cum, cumt, dtt, prefix, tail = pl.pallas_call(
        state_kernel,
        out_shape=(
            shape((span, width), BF16),
            shape((span, heads), F32),
            shape((heads, span), F32),
            shape((heads, span), F32),
            shape((2 * STATE, width), BF16),
            shape((SUB, width), BF16),
        ),
        in_specs=[hbm()] * len(operands),
        out_specs=(vmem(),) * 6,
        scratch_shapes=staged(*operands)
        + [dma((len(operands),)), pltpu.VMEM((span + SUB, width), F32)],
        compiler_params=params(WHOLE),
        cost_estimate=cost(2 * 10 * span * span * 64, 2000000, span * width * 2),
        name="state",
    )(*operands)

    operands = (asked, conv_rows, prefix, tail)
    answer = pl.pallas_call(
        answer_kernel,
        out_shape=shape((slots, width + width // 2), BF16),
        in_specs=[hbm()] * (len(operands) + 1),
        out_specs=vmem(),
        scratch_shapes=staged(*operands, live)
        + [
            dma((len(operands) + CHUNKS,)),
            pltpu.VMEM((live_dev * SUB, 2 * STATE), F32),
            pltpu.VMEM((live_dev * SUB, width), F32),
        ],
        compiler_params=params(WHOLE),
        cost_estimate=cost(2 * slots * 512 * 1024, 6000000),
        name="answer",
    )(*operands, live)
    lanes = answer.shape[1]
    got = lax.all_to_all(
        answer.reshape(gens, SUB, lanes), "gen", split_axis=0, concat_axis=0, tiled=True
    ).reshape(slots, lanes)

    pre_gate, pre_ss, late = pl.pallas_call(
        prompt_kernel,
        out_shape=(
            shape((span, width), F32),
            shape((SUB, span), F32),
            shape((2 * readers, width), F32),
        ),
        in_specs=[vmem()] * 9,
        out_specs=(vmem(),) * 3,
        scratch_shapes=[pltpu.VMEM((128, span), F32)],
        compiler_params=params(WHOLE),
        cost_estimate=cost(2 * heads * span * span * 128, 2500000, heads * span * span),
        name="prompt",
    )(xconv, pre_z[0], bct, cum, cumt, dtt, jnp.repeat(skip, width // heads)[None], asked, tgt_r.reshape(-1, 1))

    count = steps * rows
    step_gate, sums = pl.pallas_call(
        lambda *refs: decode_kernel(live_dev, readers, *refs),
        out_shape=(shape((count, width), F32), shape((SUB, 128), F32)),
        in_specs=[vmem()] * 13,
        out_specs=(vmem(), vmem()),
        compiler_params=params(),
        cost_estimate=cost(2 * 384 * 512 * 512, 2500000),
        name="decode",
    )(
        got,
        late,
        tgt_l.reshape(-1, 1),
        tgt_r.reshape(-1, 1),
        step_xz,
        step_bc,
        step_raw.reshape(count, heads),
        decay[None],
        dt_bias[None],
        skip[None],
        conv_weight,
        conv_bias[None],
        pre_ss,
    )
    sums = [sums] + [
        lax.ppermute(sums, "mp", [(i, (i + shift) % mp) for i in range(mp)])
        for shift in range(1, mp)
    ]

    prefill_out, decoded = pl.pallas_call(
        lambda *refs: finish_kernel(width_all, *refs),
        out_shape=(shape((span, width), BF16), shape((count, width), BF16)),
        in_specs=[vmem()] * (mp + 3),
        out_specs=(vmem(), vmem()),
        compiler_params=params(),
        cost_estimate=cost(1000000, 2500000),
        name="finish",
    )(*sums, pre_gate, step_gate, norm_gain[None])
    return (prefill_out[None], decoded.reshape(steps, rows, width))


def solution(mesh):
    placed = (
        P("gen", None, "mp"),
        P("gen", None, "mp"),
        P("gen", None, None, "mp"),
        P("gen", None, "mp"),
        P("gen"),
        P("gen", "mp", None, None),
        P("gen", None, "mp"),
        P("gen"),
        P("gen"),
        P(None, None, "gen", "mp"),
        P(None, None, "gen", "mp"),
        P(None, "gen", "mp"),
        P("mp"),
        P("mp"),
        P(None, "mp"),
        P("mp"),
        P("mp"),
        P("mp"),
    )
    return jax.shard_map(
        per_device,
        mesh=mesh,
        in_specs=placed,
        out_specs=(P("gen", None, "mp"), P(None, "gen", "mp")),
        check_vma=False,
    )
```

```python
import jax
import jax.numpy as jnp
from jax import lax
from jax.experimental import pallas as pl
from jax.experimental.pallas import tpu as pltpu
from jax.sharding import PartitionSpec as P

STATE = 64
EPS = 1e-05
SUB = 8
CHUNKS = 4
WHOLE = 60 * 1024 * 1024
F32 = jnp.float32
BF16 = jnp.bfloat16
NT = (((1,), (1,)), ((), ()))
TN = (((0,), (0,)), ((), ()))


def iota(shape, dim):
    return lax.broadcasted_iota(jnp.int32, shape, dim)


def mm(a, b):
    return jnp.dot(a, b, preferred_element_type=F32)


def mm_nt(a, b):
    return lax.dot_general(a, b, NT, preferred_element_type=F32)


def onehot(mask):
    return jnp.where(mask, 1.0, 0.0).astype(BF16)


def split2(x):
    hi = x.astype(BF16)
    return hi, (x - hi.astype(F32)).astype(BF16)


def split3(x):
    hi = x.astype(BF16)
    rest = x - hi.astype(F32)
    mid = rest.astype(BF16)
    return hi, mid, (rest - mid.astype(F32)).astype(BF16)


def silu(x):
    return x / (1.0 + jnp.exp(-x))


def softplus(x):
    return jnp.maximum(x, 0.0) + jnp.log1p(jnp.exp(-jnp.abs(x)))


def expander(heads, width):
    return onehot(iota((heads, width), 1) // (width // heads) == iota((heads, width), 0))


def spread(x, expand):
    hi, lo = split2(x)
    return mm(hi, expand) + mm(lo, expand)


def fetch(sources, targets, sems):
    copies = [
        pltpu.make_async_copy(source, target, sems.at[i])
        for i, (source, target) in enumerate(zip(sources, targets))
    ]
    for copy in copies:
        copy.start()
    return copies


def ask_kernel(*refs):
    sources, out_ref, targets, sems = refs[:5], refs[5], refs[6:11], refs[11]
    for copy in fetch(sources, targets, sems):
        copy.wait()
    bc_ref, source_ref, reader_ref, len_ref, x_ref = targets
    steps = bc_ref.shape[0]
    slots = out_ref.shape[0]
    live_dev = source_ref.shape[1]
    readers = reader_ref.shape[1]
    span, width = x_ref.shape
    part = width // 4
    zeros_l = jnp.zeros((live_dev, STATE), F32)
    place = (iota((live_dev, STATE), 0) + 1).astype(F32)
    parts = [bc_ref[t, 1, 0:live_dev, :].astype(F32) for t in range(steps)]
    parts += [place] + [zeros_l] * (SUB - steps - 1)
    data_l = jnp.concatenate(parts, 0)
    data_l = jnp.concatenate([data_l, jnp.zeros_like(data_l)], 1).astype(BF16)
    parts = [
        bc_ref[t % steps, 1, live_dev : live_dev + readers, :].astype(F32) for t in range(SUB)
    ]
    data_r = jnp.concatenate(parts, 0)
    data_r = jnp.concatenate([jnp.zeros_like(data_r), data_r], 1).astype(BF16)
    first_l = lax.div(source_ref[...], live_dev) * SUB
    first_r = reader_ref[...] * SUB
    tgt_l = jnp.concatenate([first_l + r for r in range(SUB)], 1)
    tgt_r = jnp.concatenate([first_r + r for r in range(SUB)], 1)
    pick_l = onehot(iota((slots, SUB * live_dev), 0) == tgt_l)
    pick_r = onehot(iota((slots, SUB * readers), 0) == tgt_r)
    out_ref[:, 0 : 2 * STATE] = (mm(pick_l, data_l) + mm(pick_r, data_r)).astype(BF16)
    row, col = iota((2 * SUB, span), 0), iota((2 * SUB, span), 1)
    last = onehot(col == len_ref[...] - 2 + row // SUB)
    both = mm(last, x_ref[...])
    lane_part = iota((SUB, part), 0) % 4
    tail = jnp.zeros((SUB, part), F32)
    for i in range(4):
        lanes = slice(i * part, (i + 1) * part)
        piece = jnp.where(iota((SUB, part), 0) < 4, both[0:SUB, lanes], both[SUB:, lanes])
        tail = jnp.where(lane_part == i, piece, tail)
    tail = jnp.broadcast_to(tail[None], (slots // SUB, SUB, part))
    out_ref[:, 2 * STATE :] = tail.reshape(slots, part).astype(BF16)


def state_kernel(*refs):
    sources, outs, targets = refs[:8], refs[8:14], refs[14:22]
    sems, xf = refs[22], refs[23]
    xc_ref, cum_ref, cumt_ref, dtt_ref, st_ref, tail_ref = outs
    for copy in fetch(sources, targets, sems):
        copy.wait()
    len_ref, rawt_ref, decay_ref, bias_ref, cw_ref, cb_ref, bct_ref, x_ref = targets
    span, width = x_ref.shape
    heads = rawt_ref.shape[0]
    taps = cw_ref.shape[0]
    length = len_ref[...]
    xf[0:SUB, :] = jnp.zeros((SUB, width), F32)
    xf[SUB : SUB + span, :] = x_ref[...].astype(F32)
    square = iota((heads, heads), 0) == iota((heads, heads), 1)

    def column(row):
        return jnp.sum(jnp.where(square, row, 0.0), axis=1, keepdims=True)

    dtt = softplus(rawt_ref[...].astype(F32) + column(bias_ref[...]))
    dtt = jnp.where(iota((heads, span), 1) < length, dtt, 0.0)
    dtt_ref[...] = dtt
    tri = onehot(iota((span, span), 0) >= iota((span, span), 1))
    pieces = split3(dtt * -column(decay_ref[...]))
    cum_ref[...] = mm_nt(tri, pieces[0]) + mm_nt(tri, pieces[1]) + mm_nt(tri, pieces[2])
    cumt = mm_nt(pieces[0], tri) + mm_nt(pieces[1], tri) + mm_nt(pieces[2], tri)
    cumt_ref[...] = cumt
    weight = jnp.exp(cumt[:, span - 1 : span] - cumt) * dtt
    weight_hi, weight_lo = split2(weight)
    expand = expander(heads, width)
    weights = [cw_ref[k : k + 1, :].astype(F32) for k in range(taps)]
    block = 128
    total = jnp.zeros((STATE, width), F32)
    for start in range(0, span, block):
        part = slice(start, start + block)
        acc = cb_ref[...]
        for k in range(taps):
            first = SUB - taps + 1 + k + start
            acc = acc + xf[first : first + block, :] * weights[k]
        xc = silu(acc).astype(BF16)
        xc_ref[part, :] = xc
        wide = lax.dot_general(weight_hi[:, part], expand, TN, preferred_element_type=F32)
        wide = wide + lax.dot_general(
            weight_lo[:, part], expand, TN, preferred_element_type=F32
        )
        weighted = (xc.astype(F32) * wide).astype(BF16)
        total = total + mm(bct_ref[0, :, part], weighted)
    st_ref[0:STATE, :] = jnp.zeros((STATE, width), BF16)
    st_ref[STATE : 2 * STATE, :] = total.astype(BF16)
    row, col = iota((SUB, span), 0), iota((SUB, span), 1)
    tail = onehot((col == length - (taps - 1)) & (row == SUB - 1))
    tail_ref[...] = mm(tail, x_ref[...]).astype(BF16)


def prompt_kernel(
    xc_ref,
    z_ref,
    bct_ref,
    cum_ref,
    cumt_ref,
    dtt_ref,
    skip_ref,
    ask_ref,
    tgt_r_ref,
    g_ref,
    ss_ref,
    late_ref,
    scores,
):
    readers = late_ref.shape[0] // 2
    part = ask_ref.shape[1] - 2 * STATE
    pick_r = onehot(iota((SUB * readers, ask_ref.shape[0]), 1) == tgt_r_ref[...])
    late = mm(pick_r, ask_ref[:, 2 * STATE :])
    for r in range(SUB):
        rows = slice(r // 4 * readers, (r // 4 + 1) * readers)
        late_ref[rows, r % 4 * part : (r % 4 + 1) * part] = late[
            r * readers : (r + 1) * readers, :
        ]
    span, width = xc_ref.shape
    heads = cum_ref.shape[1]
    block = 128
    ones = jnp.ones((SUB, block), BF16)
    lanes = iota((block, block), 1)
    causal = iota((block, block), 0) >= lanes
    for start in range(0, span, block):
        stop = start + block
        scores[:, 0:stop] = lax.dot_general(
            bct_ref[1, :, start:stop], bct_ref[0, :, 0:stop], TN, preferred_element_type=F32
        )
        square = jnp.zeros((block, block), F32)
        for lane in range(0, width, block):
            halves = []
            for half in range(2):
                head = lane * heads // width + half
                at = cum_ref[start:stop, head : head + 1]
                gap = jnp.where(causal, at - cumt_ref[head : head + 1, start:stop], -jnp.inf)
                near = scores[:, start:stop] * jnp.exp(gap) * dtt_ref[head : head + 1, start:stop]
                yhead = mm(near.astype(BF16), xc_ref[start:stop, lane : lane + block])
                if start:
                    gap = at - cumt_ref[head : head + 1, 0:start]
                    far = scores[:, 0:start] * jnp.exp(gap) * dtt_ref[head : head + 1, 0:start]
                    yhead = yhead + mm(far.astype(BF16), xc_ref[0:start, lane : lane + block])
                halves.append(yhead)
            y = jnp.where(lanes < block // 2, halves[0], halves[1])
            xin = xc_ref[start:stop, lane : lane + block].astype(F32)
            y = y + skip_ref[:, lane : lane + block] * xin
            gate = y * silu(z_ref[start:stop, lane : lane + block].astype(F32))
            g_ref[start:stop, lane : lane + block] = gate
            square = square + gate * gate
        hi, lo = split2(square)
        ss_ref[:, start:stop] = mm_nt(ones, hi) + mm_nt(ones, lo)


def answer_kernel(*refs):
    sources, live_hbm, out_ref, targets = refs[:4], refs[4], refs[5], refs[6:10]
    state_ref, sems, cs, ys = refs[10:]
    chunk = state_ref.shape[0] // CHUNKS
    chunks = [slice(i * chunk, (i + 1) * chunk) for i in range(CHUNKS)]
    copies = fetch(
        sources + tuple(live_hbm.at[part] for part in chunks),
        targets + tuple(state_ref.at[part] for part in chunks),
        sems,
    )
    for copy in copies[:4]:
        copy.wait()
    ask_ref, conv_ref, prefix_ref, tail_ref = targets
    slots = ask_ref.shape[0]
    live_dev = state_ref.shape[0]
    count = ys.shape[0]
    width = prefix_ref.shape[1]
    half = width // 2
    ask = ask_ref[:, 0 : 2 * STATE]
    down, lane = iota((slots, 1), 0), iota((1, slots), 1)
    in_slot = jnp.bitwise_and(down, SUB - 1)
    place = mm(onehot(lane == down - in_slot + 4), ask)
    lane0 = onehot(iota((SUB, 2 * STATE), 1) == 0)
    across = mm_nt(lane0, place.astype(BF16))[0:1, :].astype(jnp.int32)
    back = (across - 1) * SUB + jnp.bitwise_and(lane, SUB - 1)
    got = mm(onehot(iota((count, 1), 0) == back), ask)
    first = jnp.bitwise_and(iota((count, 1), 0), SUB - 1) < 4
    cs[...] = jnp.where(first, got, 0.0)
    for k in range(live_dev):
        if k % chunk == 0:
            copies[4 + k // chunk].wait()
        rows = slice(k * SUB, (k + 1) * SUB)
        ys[rows, :] = mm_nt(cs[rows, 0:STATE].astype(BF16), state_ref[k])
    place = place[:, 0:1].astype(jnp.int32)
    there = onehot(iota((1, count), 1) == (place - 1) * SUB + in_slot)
    live = mm(there, ys[...].astype(BF16))
    kept = conv_ref.shape[0]
    conv_row = (in_slot - 4) * live_dev + place - 1
    conv_row = jnp.where((place > 0) & (in_slot >= 4), conv_row, -1)
    there = onehot(iota((1, kept), 1) == conv_row)
    live = (live + mm(there, conv_ref[...])).reshape(slots // SUB, SUB, width)
    live = live + tail_ref[...].astype(F32)[None]
    out_ref[:, 0:width] = live.reshape(slots, width).astype(BF16)
    new = mm(ask, prefix_ref[...])
    new = jnp.where(in_slot < SUB // 2, new[:, 0:half], new[:, half:width])
    out_ref[:, width : width + half] = new.astype(BF16)


def decode_kernel(
    live_dev,
    readers,
    got_ref,
    late_ref,
    tgt_l_ref,
    tgt_r_ref,
    xz_ref,
    bc_ref,
    raw_ref,
    decay_ref,
    bias_ref,
    skip_ref,
    cw_ref,
    cb_ref,
    pre_ss_ref,
    g_ref,
    ss_ref,
):
    slots = got_ref.shape[0]
    steps, _, rows, width = xz_ref.shape
    heads = raw_ref.shape[0] // steps
    raws = raw_ref[...].astype(F32).T
    span = pre_ss_ref.shape[1]
    taps = cw_ref.shape[0]
    half = width // 2
    pick_l = onehot(iota((SUB * live_dev, slots), 1) == tgt_l_ref[...])
    pick_r = onehot(iota((SUB * readers, slots), 1) == tgt_r_ref[...])
    live = mm(pick_l, got_ref[:, 0:width])
    new = mm(pick_r, got_ref[:, width:])
    old = mm(pick_r[(SUB - 1) * readers :, :], got_ref[:, 0:width])

    def live_row(r):
        return live[r * live_dev : (r + 1) * live_dev, :]

    def new_row(r, first, last):
        return new[r * readers : (r + 1) * readers, first:last]

    first = []
    for t in range(steps):
        wide = jnp.concatenate([new_row(t, 0, half), new_row(t + 4, 0, half)], 1)
        first.append(jnp.concatenate([live_row(t), wide], 0))
    inputs = [
        jnp.concatenate([live_row(4), old], 0),
        jnp.concatenate([live_row(5), late_ref[0:readers, :]], 0),
        jnp.concatenate([live_row(6), late_ref[readers:, :]], 0),
    ]
    inputs += [xz_ref[t, 0].astype(F32) for t in range(steps)]
    expand = expander(heads, width)
    weights = [cw_ref[k : k + 1, :].astype(F32) for k in range(taps)]
    dts, logs, bmats, cmats, xcs, gates = [], [], [], [], [], []
    for t in range(steps):
        acc = cb_ref[...]
        for k in range(taps):
            acc = acc + inputs[t + k] * weights[k]
        xcs.append(silu(acc).astype(BF16).astype(F32))
        dt = softplus(raws[:, t * heads : (t + 1) * heads] + bias_ref[...])
        dts.append(dt)
        decayed = -dt * decay_ref[...]
        logs.append(decayed if t == 0 else logs[-1] + decayed)
        bmats.append(bc_ref[t, 0].astype(F32))
        cmats.append(bc_ref[t, 1].astype(F32))
        y = spread(jnp.exp(logs[t]), expand) * first[t]
        for s in range(t + 1):
            score = jnp.sum(bmats[s] * cmats[t], axis=1, keepdims=True)
            factor = dts[s] * score
            if s < t:
                factor = jnp.exp(logs[t] - logs[s]) * factor
            else:
                factor = factor + skip_ref[...]
            y = y + spread(factor, expand) * xcs[s]
        gate = y * silu(xz_ref[t, 1].astype(F32))
        g_ref[t * rows : (t + 1) * rows, :] = gate
        gates.append(gate * gate)
    square = jnp.concatenate(gates, 0)
    hi, lo = split2(square)
    ones = jnp.ones((SUB, width), BF16)
    sums = mm_nt(ones, hi) + mm_nt(ones, lo)
    lanes = ss_ref.shape[2]
    pad = -sums.shape[1] % lanes
    sums = jnp.concatenate([pre_ss_ref[...], sums, jnp.zeros((SUB, pad), F32)], 1)
    parts = [sums[0:1, i : i + lanes] for i in range(0, sums.shape[1], lanes)]
    parts += [jnp.zeros((SUB - len(parts), lanes), F32)]
    ss_ref[...] = jnp.broadcast_to(jnp.concatenate(parts, 0)[None], ss_ref.shape)


def finish_kernel(width_all, ss_ref, pre_ref, step_ref, gain_ref, pre_out_ref, step_out_ref):
    total = ss_ref[0]
    for i in range(1, ss_ref.shape[0]):
        total = total + ss_ref[i]
    scale = lax.rsqrt(total / width_all + EPS)
    gain = gain_ref[...]
    span = pre_ref.shape[0]
    block = 128

    def column(first, rows):
        row = scale[first // block : first // block + 1, :]
        diag = iota((rows, block), 0) == iota((rows, block), 1)
        return jnp.sum(jnp.where(diag, row, 0.0), axis=1, keepdims=True)

    for start in range(0, span, block):
        part = slice(start, start + block)
        pre_out_ref[part, :] = (pre_ref[part, :] * column(start, block) * gain).astype(BF16)
    count = step_ref.shape[0]
    for start in range(0, count, block):
        rows = min(block, count - start)
        part = slice(start, start + rows)
        step_out_ref[part, :] = (step_ref[part, :] * column(span + start, rows) * gain).astype(
            BF16
        )


def params(limit=24 * 1024 * 1024, **more):
    return pltpu.CompilerParams(vmem_limit_bytes=limit, **more)


def cost(flops, moved, special=0):
    return pl.CostEstimate(flops=flops, bytes_accessed=moved, transcendentals=special)


def vmem():
    return pl.BlockSpec(memory_space=pltpu.VMEM)


def hbm():
    return pl.BlockSpec(memory_space=pltpu.HBM)


def shape(dims, kind):
    return jax.ShapeDtypeStruct(dims, kind)


def per_device(
    pre_x,
    pre_z,
    pre_bc,
    pre_raw,
    prompt_len,
    live_state,
    live_conv,
    source,
    reader,
    step_xz,
    step_bc,
    step_raw,
    decay,
    dt_bias,
    conv_weight,
    conv_bias,
    skip,
    norm_gain,
):
    _, span, width = pre_x.shape
    mp = lax.axis_size("mp")
    gens = lax.axis_size("gen")
    width_all = width * mp
    live_dev = source.shape[0]
    readers = reader.shape[0]
    heads = pre_raw.shape[2]
    steps, _, rows, _ = step_xz.shape
    slots = gens * SUB
    offset = jnp.arange(SUB, dtype=jnp.int32)[:, None]
    tgt_l = SUB * (source // live_dev)[None, :] + offset
    tgt_r = SUB * reader[None, :] + offset

    length = prompt_len.reshape(1, 1)
    conv_rows = jnp.transpose(live_conv, (1, 0, 2)).reshape(-1, width)
    bct = jnp.swapaxes(pre_bc[0], 1, 2)
    dma = pltpu.SemaphoreType.DMA

    def staged(*arrays):
        return [pltpu.VMEM(array.shape, array.dtype) for array in arrays]

    operands = (step_bc, source[None], reader[None], length, pre_x[0])
    ask = pl.pallas_call(
        ask_kernel,
        out_shape=shape((slots, 2 * STATE + width // 4), BF16),
        in_specs=[hbm()] * len(operands),
        out_specs=vmem(),
        scratch_shapes=staged(*operands) + [dma((len(operands),))],
        compiler_params=params(WHOLE),
        cost_estimate=cost(2 * slots * 384 * 128, 800000),
        name="ask",
    )(*operands)
    lanes = ask.shape[1]
    asked = lax.all_to_all(
        ask.reshape(gens, SUB, lanes), "gen", split_axis=0, concat_axis=0, tiled=True
    ).reshape(slots, lanes)

    live = live_state.reshape(live_dev, width, STATE)
    operands = (
        length,
        pre_raw[0].T,
        decay[None],
        dt_bias[None],
        conv_weight,
        conv_bias[None],
        bct,
        pre_x[0],
    )
    xconv, cum, cumt, dtt, prefix, tail = pl.pallas_call(
        state_kernel,
        out_shape=(
            shape((span, width), BF16),
            shape((span, heads), F32),
            shape((heads, span), F32),
            shape((heads, span), F32),
            shape((2 * STATE, width), BF16),
            shape((SUB, width), BF16),
        ),
        in_specs=[hbm()] * len(operands),
        out_specs=(vmem(),) * 6,
        scratch_shapes=staged(*operands)
        + [dma((len(operands),)), pltpu.VMEM((span + SUB, width), F32)],
        compiler_params=params(WHOLE),
        cost_estimate=cost(2 * 10 * span * span * 64, 2000000, span * width * 2),
        name="state",
    )(*operands)

    operands = (asked, conv_rows, prefix, tail)
    answer = pl.pallas_call(
        answer_kernel,
        out_shape=shape((slots, width + width // 2), BF16),
        in_specs=[hbm()] * (len(operands) + 1),
        out_specs=vmem(),
        scratch_shapes=staged(*operands, live)
        + [
            dma((len(operands) + CHUNKS,)),
            pltpu.VMEM((live_dev * SUB, 2 * STATE), F32),
            pltpu.VMEM((live_dev * SUB, width), F32),
        ],
        compiler_params=params(WHOLE),
        cost_estimate=cost(2 * slots * 512 * 1024, 6000000),
        name="answer",
    )(*operands, live)
    lanes = answer.shape[1]
    got = lax.all_to_all(
        answer.reshape(gens, SUB, lanes), "gen", split_axis=0, concat_axis=0, tiled=True
    ).reshape(slots, lanes)

    pre_gate, pre_ss, late = pl.pallas_call(
        prompt_kernel,
        out_shape=(
            shape((span, width), F32),
            shape((SUB, span), F32),
            shape((2 * readers, width), F32),
        ),
        in_specs=[vmem()] * 9,
        out_specs=(vmem(),) * 3,
        scratch_shapes=[pltpu.VMEM((128, span), F32)],
        compiler_params=params(),
        cost_estimate=cost(2 * heads * span * span * 128, 2500000, heads * span * span),
        name="prompt",
    )(xconv, pre_z[0], bct, cum, cumt, dtt, jnp.repeat(skip, width // heads)[None], asked, tgt_r.reshape(-1, 1))

    count = steps * rows
    step_gate, sums = pl.pallas_call(
        lambda *refs: decode_kernel(live_dev, readers, *refs),
        out_shape=(shape((count, width), F32), shape((mp, SUB, 128), F32)),
        in_specs=[vmem()] * 13,
        out_specs=(vmem(), vmem()),
        compiler_params=params(),
        cost_estimate=cost(2 * 384 * 512 * 512, 2500000),
        name="decode",
    )(
        got,
        late,
        tgt_l.reshape(-1, 1),
        tgt_r.reshape(-1, 1),
        step_xz,
        step_bc,
        jnp.swapaxes(step_raw, 1, 2).reshape(steps * heads, rows),
        decay[None],
        dt_bias[None],
        skip[None],
        conv_weight,
        conv_bias[None],
        pre_ss,
    )
    sums = lax.all_to_all(sums, "mp", split_axis=0, concat_axis=0, tiled=True)

    prefill_out, decoded = pl.pallas_call(
        lambda *refs: finish_kernel(width_all, *refs),
        out_shape=(shape((span, width), BF16), shape((count, width), BF16)),
        in_specs=[vmem()] * 4,
        out_specs=(vmem(), vmem()),
        compiler_params=params(),
        cost_estimate=cost(1000000, 2500000),
        name="finish",
    )(sums, pre_gate, step_gate, norm_gain[None])
    return (prefill_out[None], decoded.reshape(steps, rows, width))


def solution(mesh):
    placed = (
        P("gen", None, "mp"),
        P("gen", None, "mp"),
        P("gen", None, None, "mp"),
        P("gen", None, "mp"),
        P("gen"),
        P("gen", "mp", None, None),
        P("gen", None, "mp"),
        P("gen"),
        P("gen"),
        P(None, None, "gen", "mp"),
        P(None, None, "gen", "mp"),
        P(None, "gen", "mp"),
        P("mp"),
        P("mp"),
        P(None, "mp"),
        P("mp"),
        P("mp"),
        P("mp"),
    )
    return jax.shard_map(
        per_device,
        mesh=mesh,
        in_specs=placed,
        out_specs=(P("gen", None, "mp"), P(None, "gen", "mp")),
        check_vma=False,
    )
```

```python
import jax
import jax.numpy as jnp
from jax import lax
from jax.experimental import pallas as pl
from jax.experimental.pallas import tpu as pltpu
from jax.sharding import PartitionSpec as P

STATE = 64
EPS = 1e-05
SUB = 8
CHUNKS = 4
GROUP_ROWS = 4
WHOLE = 60 * 1024 * 1024
F32 = jnp.float32
BF16 = jnp.bfloat16
NT = (((1,), (1,)), ((), ()))
TN = (((0,), (0,)), ((), ()))


def iota(shape, dim):
    return lax.broadcasted_iota(jnp.int32, shape, dim)


def mm(a, b):
    return jnp.dot(a, b, preferred_element_type=F32)


def mm_nt(a, b):
    return lax.dot_general(a, b, NT, preferred_element_type=F32)


def onehot(mask):
    return jnp.where(mask, 1.0, 0.0).astype(BF16)


def split2(x):
    hi = x.astype(BF16)
    return hi, (x - hi.astype(F32)).astype(BF16)


def split3(x):
    hi = x.astype(BF16)
    rest = x - hi.astype(F32)
    mid = rest.astype(BF16)
    return hi, mid, (rest - mid.astype(F32)).astype(BF16)


def silu(x):
    return x / (1.0 + jnp.exp(-x))


def softplus(x):
    return jnp.maximum(x, 0.0) + jnp.log1p(jnp.exp(-jnp.abs(x)))


def expander(heads, width):
    return onehot(iota((heads, width), 1) // (width // heads) == iota((heads, width), 0))


def spread(x, expand):
    hi, lo = split2(x)
    return mm(hi, expand) + mm(lo, expand)


def fetch(sources, targets, sems):
    copies = [
        pltpu.make_async_copy(source, target, sems.at[i])
        for i, (source, target) in enumerate(zip(sources, targets))
    ]
    for copy in copies:
        copy.start()
    return copies


def ask_kernel(*refs):
    sources, out_ref, targets, sems = refs[:5], refs[5], refs[6:11], refs[11]
    for copy in fetch(sources, targets, sems):
        copy.wait()
    bc_ref, source_ref, reader_ref, len_ref, x_ref = targets
    steps = bc_ref.shape[0]
    slots = out_ref.shape[0]
    live_dev = source_ref.shape[1]
    readers = reader_ref.shape[1]
    span, width = x_ref.shape
    part = width // 4
    zeros_l = jnp.zeros((live_dev, STATE), F32)
    place = (iota((live_dev, STATE), 0) + 1).astype(F32)
    parts = [bc_ref[t, 1, 0:live_dev, :].astype(F32) for t in range(steps)]
    parts += [place] + [zeros_l] * (SUB - steps - 1)
    data_l = jnp.concatenate(parts, 0)
    data_l = jnp.concatenate([data_l, jnp.zeros_like(data_l)], 1).astype(BF16)
    parts = [
        bc_ref[t % steps, 1, live_dev : live_dev + readers, :].astype(F32) for t in range(SUB)
    ]
    data_r = jnp.concatenate(parts, 0)
    data_r = jnp.concatenate([jnp.zeros_like(data_r), data_r], 1).astype(BF16)
    first_l = lax.div(source_ref[...], live_dev) * SUB
    first_r = reader_ref[...] * SUB
    tgt_l = jnp.concatenate([first_l + r for r in range(SUB)], 1)
    tgt_r = jnp.concatenate([first_r + r for r in range(SUB)], 1)
    pick_l = onehot(iota((slots, SUB * live_dev), 0) == tgt_l)
    pick_r = onehot(iota((slots, SUB * readers), 0) == tgt_r)
    out_ref[:, 0 : 2 * STATE] = (mm(pick_l, data_l) + mm(pick_r, data_r)).astype(BF16)
    row, col = iota((2 * SUB, span), 0), iota((2 * SUB, span), 1)
    last = onehot(col == len_ref[...] - 2 + row // SUB)
    both = mm(last, x_ref[...])
    lane_part = iota((SUB, part), 0) % 4
    tail = jnp.zeros((SUB, part), F32)
    for i in range(4):
        lanes = slice(i * part, (i + 1) * part)
        piece = jnp.where(iota((SUB, part), 0) < 4, both[0:SUB, lanes], both[SUB:, lanes])
        tail = jnp.where(lane_part == i, piece, tail)
    tail = jnp.broadcast_to(tail[None], (slots // SUB, SUB, part))
    out_ref[:, 2 * STATE :] = tail.reshape(slots, part).astype(BF16)


def state_kernel(*refs):
    sources, live_hbm, outs, targets = refs[:8], refs[8], refs[9:16], refs[16:24]
    live_ref, sems, xf = refs[24:]
    xc_ref, cum_ref, cumt_ref, dtt_ref, st_ref, tail_ref, turned_ref = outs
    chunk = live_ref.shape[0] // CHUNKS
    chunks = [slice(i * chunk, (i + 1) * chunk) for i in range(CHUNKS)]
    copies = fetch(
        sources + tuple(live_hbm.at[part] for part in chunks),
        targets + tuple(live_ref.at[part] for part in chunks),
        sems,
    )
    for copy in copies[:8]:
        copy.wait()
    len_ref, rawt_ref, decay_ref, bias_ref, cw_ref, cb_ref, bct_ref, x_ref = targets
    span, width = x_ref.shape
    heads = rawt_ref.shape[0]
    taps = cw_ref.shape[0]
    length = len_ref[...]
    xf[0:SUB, :] = jnp.zeros((SUB, width), F32)
    xf[SUB : SUB + span, :] = x_ref[...].astype(F32)
    square = iota((heads, heads), 0) == iota((heads, heads), 1)

    def column(row):
        return jnp.sum(jnp.where(square, row, 0.0), axis=1, keepdims=True)

    dtt = softplus(rawt_ref[...].astype(F32) + column(bias_ref[...]))
    dtt = jnp.where(iota((heads, span), 1) < length, dtt, 0.0)
    dtt_ref[...] = dtt
    tri = onehot(iota((span, span), 0) >= iota((span, span), 1))
    pieces = split3(dtt * -column(decay_ref[...]))
    cum_ref[...] = mm_nt(tri, pieces[0]) + mm_nt(tri, pieces[1]) + mm_nt(tri, pieces[2])
    cumt = mm_nt(pieces[0], tri) + mm_nt(pieces[1], tri) + mm_nt(pieces[2], tri)
    cumt_ref[...] = cumt
    weight = jnp.exp(cumt[:, span - 1 : span] - cumt) * dtt
    weight_hi, weight_lo = split2(weight)
    expand = expander(heads, width)
    weights = [cw_ref[k : k + 1, :].astype(F32) for k in range(taps)]
    block = 128
    total = jnp.zeros((STATE, width), F32)
    for start in range(0, span, block):
        part = slice(start, start + block)
        acc = cb_ref[...]
        for k in range(taps):
            first = SUB - taps + 1 + k + start
            acc = acc + xf[first : first + block, :] * weights[k]
        xc = silu(acc).astype(BF16)
        xc_ref[part, :] = xc
        wide = lax.dot_general(weight_hi[:, part], expand, TN, preferred_element_type=F32)
        wide = wide + lax.dot_general(
            weight_lo[:, part], expand, TN, preferred_element_type=F32
        )
        weighted = (xc.astype(F32) * wide).astype(BF16)
        total = total + mm(bct_ref[0, :, part], weighted)
    st_ref[0:STATE, :] = jnp.zeros((STATE, width), BF16)
    st_ref[STATE : 2 * STATE, :] = total.astype(BF16)
    row, col = iota((SUB, span), 0), iota((SUB, span), 1)
    tail = onehot((col == length - (taps - 1)) & (row == SUB - 1))
    tail_ref[...] = mm(tail, x_ref[...]).astype(BF16)
    unit = onehot(iota((STATE, STATE), 0) == iota((STATE, STATE), 1))
    for k in range(live_ref.shape[0]):
        if k % chunk == 0:
            copies[8 + k // chunk].wait()
        turned_ref[k * STATE : (k + 1) * STATE, :] = mm_nt(unit, live_ref[k]).astype(BF16)


def prompt_kernel(
    xc_ref,
    z_ref,
    bct_ref,
    cum_ref,
    cumt_ref,
    dtt_ref,
    skip_ref,
    ask_ref,
    tgt_r_ref,
    g_ref,
    ss_ref,
    late_ref,
    scores,
):
    readers = late_ref.shape[0] // 2
    part = ask_ref.shape[1] - 2 * STATE
    pick_r = onehot(iota((SUB * readers, ask_ref.shape[0]), 1) == tgt_r_ref[...])
    late = mm(pick_r, ask_ref[:, 2 * STATE :])
    for r in range(SUB):
        rows = slice(r // 4 * readers, (r // 4 + 1) * readers)
        late_ref[rows, r % 4 * part : (r % 4 + 1) * part] = late[
            r * readers : (r + 1) * readers, :
        ]
    span, width = xc_ref.shape
    heads = cum_ref.shape[1]
    block = 128
    ones = jnp.ones((SUB, block), BF16)
    lanes = iota((block, block), 1)
    causal = iota((block, block), 0) >= lanes
    for start in range(0, span, block):
        stop = start + block
        scores[:, 0:stop] = lax.dot_general(
            bct_ref[1, :, start:stop], bct_ref[0, :, 0:stop], TN, preferred_element_type=F32
        )
        square = jnp.zeros((block, block), F32)
        for lane in range(0, width, block):
            halves = []
            for half in range(2):
                head = lane * heads // width + half
                at = cum_ref[start:stop, head : head + 1]
                gap = jnp.where(causal, at - cumt_ref[head : head + 1, start:stop], -jnp.inf)
                near = scores[:, start:stop] * jnp.exp(gap) * dtt_ref[head : head + 1, start:stop]
                yhead = mm(near.astype(BF16), xc_ref[start:stop, lane : lane + block])
                if start:
                    gap = at - cumt_ref[head : head + 1, 0:start]
                    far = scores[:, 0:start] * jnp.exp(gap) * dtt_ref[head : head + 1, 0:start]
                    yhead = yhead + mm(far.astype(BF16), xc_ref[0:start, lane : lane + block])
                halves.append(yhead)
            y = jnp.where(lanes < block // 2, halves[0], halves[1])
            xin = xc_ref[start:stop, lane : lane + block].astype(F32)
            y = y + skip_ref[:, lane : lane + block] * xin
            gate = y * silu(z_ref[start:stop, lane : lane + block].astype(F32))
            g_ref[start:stop, lane : lane + block] = gate
            square = square + gate * gate
        hi, lo = split2(square)
        ss_ref[:, start:stop] = mm_nt(ones, hi) + mm_nt(ones, lo)


def answer_kernel(*refs):
    sources, turned_hbm, out_ref, targets = refs[:4], refs[4], refs[5], refs[6:10]
    state_ref, sems, ys = refs[10:]
    chunk = state_ref.shape[0] // CHUNKS
    chunks = [slice(i * chunk, (i + 1) * chunk) for i in range(CHUNKS)]
    copies = fetch(
        sources + tuple(turned_hbm.at[part] for part in chunks),
        targets + tuple(state_ref.at[part] for part in chunks),
        sems,
    )
    for copy in copies[:4]:
        copy.wait()
    ask_ref, conv_ref, prefix_ref, tail_ref = targets
    slots = ask_ref.shape[0]
    count = ys.shape[0]
    live_dev = count // SUB
    width = prefix_ref.shape[1]
    half = width // 2
    ask = ask_ref[:, 0 : 2 * STATE]
    down, lane = iota((slots, 1), 0), iota((1, slots), 1)
    in_slot = jnp.bitwise_and(down, SUB - 1)
    place = mm(onehot(lane == down - in_slot + 4), ask)
    lane0 = onehot(iota((SUB, 2 * STATE), 1) == 0)
    across = mm_nt(lane0, place.astype(BF16))[0:1, :].astype(jnp.int32)
    back = (across - 1) * SUB + jnp.bitwise_and(lane, SUB - 1)
    got = mm(onehot(iota((count, 1), 0) == back), ask).astype(BF16)
    deep = GROUP_ROWS * STATE
    copy_of = jnp.bitwise_and(iota((1, deep), 1), STATE - 1)
    wide = mm(got, onehot(iota((2 * STATE, 1), 0) == copy_of))
    row, col = iota((count, 1), 0), iota((1, deep), 1)
    wanted = jnp.where(jnp.bitwise_and(row, SUB - 1) < 4, lax.div(row, SUB), -1)
    wanted = jnp.where(wanted >= 0, jnp.bitwise_and(wanted, GROUP_ROWS - 1), -1)
    wide = jnp.where(wanted == lax.div(col, STATE), wide, 0.0).astype(BF16)
    tall = GROUP_ROWS * SUB
    for group in range(live_dev // GROUP_ROWS):
        first = group * deep
        if first % chunk == 0:
            copies[4 + first // chunk].wait()
        rows = slice(group * tall, (group + 1) * tall)
        ys[rows, :] = mm(wide[rows, :], state_ref[first : first + deep, :]).astype(BF16)
    place = place[:, 0:1].astype(jnp.int32)
    there = onehot(iota((1, count), 1) == (place - 1) * SUB + in_slot)
    live = mm(there, ys[...])
    kept = conv_ref.shape[0]
    conv_row = (in_slot - 4) * live_dev + place - 1
    conv_row = jnp.where((place > 0) & (in_slot >= 4), conv_row, -1)
    there = onehot(iota((1, kept), 1) == conv_row)
    live = (live + mm(there, conv_ref[...])).reshape(slots // SUB, SUB, width)
    live = live + tail_ref[...].astype(F32)[None]
    out_ref[:, 0:width] = live.reshape(slots, width).astype(BF16)
    new = mm(ask, prefix_ref[...])
    new = jnp.where(in_slot < SUB // 2, new[:, 0:half], new[:, half:width])
    out_ref[:, width : width + half] = new.astype(BF16)


def decode_kernel(
    live_dev,
    readers,
    got_ref,
    late_ref,
    tgt_l_ref,
    tgt_r_ref,
    xz_ref,
    bc_ref,
    raw_ref,
    decay_ref,
    bias_ref,
    skip_ref,
    cw_ref,
    cb_ref,
    pre_ss_ref,
    g_ref,
    ss_ref,
):
    slots = got_ref.shape[0]
    steps, _, rows, width = xz_ref.shape
    heads = raw_ref.shape[0] // steps
    raws = raw_ref[...].astype(F32).T
    span = pre_ss_ref.shape[1]
    taps = cw_ref.shape[0]
    half = width // 2
    pick_l = onehot(iota((SUB * live_dev, slots), 1) == tgt_l_ref[...])
    pick_r = onehot(iota((SUB * readers, slots), 1) == tgt_r_ref[...])
    live = mm(pick_l, got_ref[:, 0:width])
    new = mm(pick_r, got_ref[:, width:])
    old = mm(pick_r[(SUB - 1) * readers :, :], got_ref[:, 0:width])

    def live_row(r):
        return live[r * live_dev : (r + 1) * live_dev, :]

    def new_row(r, first, last):
        return new[r * readers : (r + 1) * readers, first:last]

    first = []
    for t in range(steps):
        wide = jnp.concatenate([new_row(t, 0, half), new_row(t + 4, 0, half)], 1)
        first.append(jnp.concatenate([live_row(t), wide], 0))
    inputs = [
        jnp.concatenate([live_row(4), old], 0),
        jnp.concatenate([live_row(5), late_ref[0:readers, :]], 0),
        jnp.concatenate([live_row(6), late_ref[readers:, :]], 0),
    ]
    inputs += [xz_ref[t, 0].astype(F32) for t in range(steps)]
    expand = expander(heads, width)
    weights = [cw_ref[k : k + 1, :].astype(F32) for k in range(taps)]
    dts, logs, bmats, cmats, xcs, gates = [], [], [], [], [], []
    for t in range(steps):
        acc = cb_ref[...]
        for k in range(taps):
            acc = acc + inputs[t + k] * weights[k]
        xcs.append(silu(acc).astype(BF16).astype(F32))
        dt = softplus(raws[:, t * heads : (t + 1) * heads] + bias_ref[...])
        dts.append(dt)
        decayed = -dt * decay_ref[...]
        logs.append(decayed if t == 0 else logs[-1] + decayed)
        bmats.append(bc_ref[t, 0].astype(F32))
        cmats.append(bc_ref[t, 1].astype(F32))
        y = spread(jnp.exp(logs[t]), expand) * first[t]
        for s in range(t + 1):
            score = jnp.sum(bmats[s] * cmats[t], axis=1, keepdims=True)
            factor = dts[s] * score
            if s < t:
                factor = jnp.exp(logs[t] - logs[s]) * factor
            else:
                factor = factor + skip_ref[...]
            y = y + spread(factor, expand) * xcs[s]
        gate = y * silu(xz_ref[t, 1].astype(F32))
        g_ref[t * rows : (t + 1) * rows, :] = gate
        gates.append(gate * gate)
    square = jnp.concatenate(gates, 0)
    hi, lo = split2(square)
    ones = jnp.ones((SUB, width), BF16)
    sums = mm_nt(ones, hi) + mm_nt(ones, lo)
    lanes = ss_ref.shape[2]
    pad = -sums.shape[1] % lanes
    sums = jnp.concatenate([pre_ss_ref[...], sums, jnp.zeros((SUB, pad), F32)], 1)
    parts = [sums[0:1, i : i + lanes] for i in range(0, sums.shape[1], lanes)]
    parts += [jnp.zeros((SUB - len(parts), lanes), F32)]
    ss_ref[...] = jnp.broadcast_to(jnp.concatenate(parts, 0)[None], ss_ref.shape)


def finish_kernel(width_all, ss_ref, pre_ref, step_ref, gain_ref, pre_out_ref, step_out_ref):
    total = ss_ref[0]
    for i in range(1, ss_ref.shape[0]):
        total = total + ss_ref[i]
    scale = lax.rsqrt(total / width_all + EPS)
    gain = gain_ref[...]
    span = pre_ref.shape[0]
    block = 128

    def column(first, rows):
        row = scale[first // block : first // block + 1, :]
        diag = iota((rows, block), 0) == iota((rows, block), 1)
        return jnp.sum(jnp.where(diag, row, 0.0), axis=1, keepdims=True)

    for start in range(0, span, block):
        part = slice(start, start + block)
        pre_out_ref[part, :] = (pre_ref[part, :] * column(start, block) * gain).astype(BF16)
    count = step_ref.shape[0]
    for start in range(0, count, block):
        rows = min(block, count - start)
        part = slice(start, start + rows)
        step_out_ref[part, :] = (step_ref[part, :] * column(span + start, rows) * gain).astype(
            BF16
        )


def params(limit=24 * 1024 * 1024, **more):
    return pltpu.CompilerParams(vmem_limit_bytes=limit, **more)


def cost(flops, moved, special=0):
    return pl.CostEstimate(flops=flops, bytes_accessed=moved, transcendentals=special)


def vmem():
    return pl.BlockSpec(memory_space=pltpu.VMEM)


def hbm():
    return pl.BlockSpec(memory_space=pltpu.HBM)


def shape(dims, kind):
    return jax.ShapeDtypeStruct(dims, kind)


def per_device(
    pre_x,
    pre_z,
    pre_bc,
    pre_raw,
    prompt_len,
    live_state,
    live_conv,
    source,
    reader,
    step_xz,
    step_bc,
    step_raw,
    decay,
    dt_bias,
    conv_weight,
    conv_bias,
    skip,
    norm_gain,
):
    _, span, width = pre_x.shape
    mp = lax.axis_size("mp")
    gens = lax.axis_size("gen")
    width_all = width * mp
    live_dev = source.shape[0]
    readers = reader.shape[0]
    heads = pre_raw.shape[2]
    steps, _, rows, _ = step_xz.shape
    slots = gens * SUB
    offset = jnp.arange(SUB, dtype=jnp.int32)[:, None]
    tgt_l = SUB * (source // live_dev)[None, :] + offset
    tgt_r = SUB * reader[None, :] + offset

    length = prompt_len.reshape(1, 1)
    conv_rows = jnp.transpose(live_conv, (1, 0, 2)).reshape(-1, width)
    bct = jnp.swapaxes(pre_bc[0], 1, 2)
    dma = pltpu.SemaphoreType.DMA

    def staged(*arrays):
        return [pltpu.VMEM(array.shape, array.dtype) for array in arrays]

    operands = (step_bc, source[None], reader[None], length, pre_x[0])
    ask = pl.pallas_call(
        ask_kernel,
        out_shape=shape((slots, 2 * STATE + width // 4), BF16),
        in_specs=[hbm()] * len(operands),
        out_specs=vmem(),
        scratch_shapes=staged(*operands) + [dma((len(operands),))],
        compiler_params=params(WHOLE),
        cost_estimate=cost(2 * slots * 384 * 128, 800000),
        name="ask",
    )(*operands)
    lanes = ask.shape[1]
    asked = lax.all_to_all(
        ask.reshape(gens, SUB, lanes), "gen", split_axis=0, concat_axis=0, tiled=True
    ).reshape(slots, lanes)

    live = live_state.reshape(live_dev, width, STATE)
    operands = (
        length,
        pre_raw[0].T,
        decay[None],
        dt_bias[None],
        conv_weight,
        conv_bias[None],
        bct,
        pre_x[0],
    )
    xconv, cum, cumt, dtt, prefix, tail, turned = pl.pallas_call(
        state_kernel,
        out_shape=(
            shape((span, width), BF16),
            shape((span, heads), F32),
            shape((heads, span), F32),
            shape((heads, span), F32),
            shape((2 * STATE, width), BF16),
            shape((SUB, width), BF16),
            shape((live_dev * STATE, width), BF16),
        ),
        in_specs=[hbm()] * (len(operands) + 1),
        out_specs=(vmem(),) * 7,
        scratch_shapes=staged(*operands, live)
        + [dma((len(operands) + CHUNKS,)), pltpu.VMEM((span + SUB, width), F32)],
        compiler_params=params(WHOLE),
        cost_estimate=cost(2 * 10 * span * span * 64, 8000000, span * width * 2),
        name="state",
    )(*operands, live)

    operands = (asked, conv_rows, prefix, tail)
    answer = pl.pallas_call(
        answer_kernel,
        out_shape=shape((slots, width + width // 2), BF16),
        in_specs=[pl.BlockSpec(memory_space=pl.ANY)] + [hbm()] * len(operands),
        out_specs=vmem(),
        scratch_shapes=staged(*operands, turned)
        + [
            dma((len(operands) + CHUNKS,)),
            pltpu.VMEM((live_dev * SUB, width), BF16),
        ],
        compiler_params=params(WHOLE),
        cost_estimate=cost(2 * slots * 512 * 1024, 4000000),
        name="answer",
    )(*operands, turned)
    lanes = answer.shape[1]
    got = lax.all_to_all(
        answer.reshape(gens, SUB, lanes), "gen", split_axis=0, concat_axis=0, tiled=True
    ).reshape(slots, lanes)

    pre_gate, pre_ss, late = pl.pallas_call(
        prompt_kernel,
        out_shape=(
            shape((span, width), F32),
            shape((SUB, span), F32),
            shape((2 * readers, width), F32),
        ),
        in_specs=[vmem()] * 9,
        out_specs=(vmem(),) * 3,
        scratch_shapes=[pltpu.VMEM((128, span), F32)],
        compiler_params=params(),
        cost_estimate=cost(2 * heads * span * span * 128, 2500000, heads * span * span),
        name="prompt",
    )(xconv, pre_z[0], bct, cum, cumt, dtt, jnp.repeat(skip, width // heads)[None], asked, tgt_r.reshape(-1, 1))

    count = steps * rows
    step_gate, sums = pl.pallas_call(
        lambda *refs: decode_kernel(live_dev, readers, *refs),
        out_shape=(shape((count, width), F32), shape((mp, SUB, 128), F32)),
        in_specs=[vmem()] * 13,
        out_specs=(vmem(), vmem()),
        compiler_params=params(),
        cost_estimate=cost(2 * 384 * 512 * 512, 2500000),
        name="decode",
    )(
        got,
        late,
        tgt_l.reshape(-1, 1),
        tgt_r.reshape(-1, 1),
        step_xz,
        step_bc,
        jnp.swapaxes(step_raw, 1, 2).reshape(steps * heads, rows),
        decay[None],
        dt_bias[None],
        skip[None],
        conv_weight,
        conv_bias[None],
        pre_ss,
    )
    sums = lax.all_to_all(sums, "mp", split_axis=0, concat_axis=0, tiled=True)

    prefill_out, decoded = pl.pallas_call(
        lambda *refs: finish_kernel(width_all, *refs),
        out_shape=(shape((span, width), BF16), shape((count, width), BF16)),
        in_specs=[vmem()] * 4,
        out_specs=(vmem(), vmem()),
        compiler_params=params(),
        cost_estimate=cost(1000000, 2500000),
        name="finish",
    )(sums, pre_gate, step_gate, norm_gain[None])
    return (prefill_out[None], decoded.reshape(steps, rows, width))


def solution(mesh):
    placed = (
        P("gen", None, "mp"),
        P("gen", None, "mp"),
        P("gen", None, None, "mp"),
        P("gen", None, "mp"),
        P("gen"),
        P("gen", "mp", None, None),
        P("gen", None, "mp"),
        P("gen"),
        P("gen"),
        P(None, None, "gen", "mp"),
        P(None, None, "gen", "mp"),
        P(None, "gen", "mp"),
        P("mp"),
        P("mp"),
        P(None, "mp"),
        P("mp"),
        P("mp"),
        P("mp"),
    )
    return jax.shard_map(
        per_device,
        mesh=mesh,
        in_specs=placed,
        out_specs=(P("gen", None, "mp"), P(None, "gen", "mp")),
        check_vma=False,
    )
```

```python
import jax
import jax.numpy as jnp
from jax import lax
from jax.experimental import pallas as pl
from jax.experimental.pallas import tpu as pltpu
from jax.sharding import PartitionSpec as P

STATE = 64
EPS = 1e-05
SUB = 8
CHUNKS = 4
GROUP_ROWS = 4
WHOLE = 60 * 1024 * 1024
F32 = jnp.float32
BF16 = jnp.bfloat16
NT = (((1,), (1,)), ((), ()))
TN = (((0,), (0,)), ((), ()))


def iota(shape, dim):
    return lax.broadcasted_iota(jnp.int32, shape, dim)


def mm(a, b):
    return jnp.dot(a, b, preferred_element_type=F32)


def mm_nt(a, b):
    return lax.dot_general(a, b, NT, preferred_element_type=F32)


def onehot(mask):
    return jnp.where(mask, 1.0, 0.0).astype(BF16)


def split2(x):
    hi = x.astype(BF16)
    return hi, (x - hi.astype(F32)).astype(BF16)


def split3(x):
    hi = x.astype(BF16)
    rest = x - hi.astype(F32)
    mid = rest.astype(BF16)
    return hi, mid, (rest - mid.astype(F32)).astype(BF16)


def silu(x):
    return x / (1.0 + jnp.exp(-x))


def softplus(x):
    return jnp.maximum(x, 0.0) + jnp.log1p(jnp.exp(-jnp.abs(x)))


def expander(heads, width):
    return onehot(iota((heads, width), 1) // (width // heads) == iota((heads, width), 0))


def spread(x, expand):
    hi, lo = split2(x)
    return mm(hi, expand) + mm(lo, expand)


def fetch(sources, targets, sems):
    copies = [
        pltpu.make_async_copy(source, target, sems.at[i])
        for i, (source, target) in enumerate(zip(sources, targets))
    ]
    for copy in copies:
        copy.start()
    return copies


def ask_kernel(*refs):
    sources, out_ref, targets, sems = refs[:3], refs[3], refs[4:7], refs[7]
    for copy in fetch(sources, targets, sems):
        copy.wait()
    bc_ref, source_ref, reader_ref = targets
    steps = bc_ref.shape[0]
    slots = out_ref.shape[0]
    live_dev = source_ref.shape[1]
    readers = reader_ref.shape[1]
    zeros_l = jnp.zeros((live_dev, STATE), F32)
    place = (iota((live_dev, STATE), 0) + 1).astype(F32)
    parts = [bc_ref[t, 1, 0:live_dev, :].astype(F32) for t in range(steps)]
    parts += [place] + [zeros_l] * (SUB - steps - 1)
    data_l = jnp.concatenate(parts, 0)
    data_l = jnp.concatenate([data_l, jnp.zeros_like(data_l)], 1).astype(BF16)
    parts = [
        bc_ref[t % steps, 1, live_dev : live_dev + readers, :].astype(F32) for t in range(SUB)
    ]
    data_r = jnp.concatenate(parts, 0)
    data_r = jnp.concatenate([jnp.zeros_like(data_r), data_r], 1).astype(BF16)
    first_l = lax.div(source_ref[...], live_dev) * SUB
    first_r = reader_ref[...] * SUB
    tgt_l = jnp.concatenate([first_l + r for r in range(SUB)], 1)
    tgt_r = jnp.concatenate([first_r + r for r in range(SUB)], 1)
    pick_l = onehot(iota((slots, SUB * live_dev), 0) == tgt_l)
    pick_r = onehot(iota((slots, SUB * readers), 0) == tgt_r)
    out_ref[...] = (mm(pick_l, data_l) + mm(pick_r, data_r)).astype(BF16)


def state_kernel(*refs):
    sources, live_hbm, outs, targets = refs[:8], refs[8], refs[9:17], refs[17:25]
    live_ref, sems, xf = refs[25:]
    xc_ref, cum_ref, cumt_ref, dtt_ref, st_ref, tail_ref, late_ref, turned_ref = outs
    chunk = live_ref.shape[0] // CHUNKS
    chunks = [slice(i * chunk, (i + 1) * chunk) for i in range(CHUNKS)]
    copies = fetch(
        sources + tuple(live_hbm.at[part] for part in chunks),
        targets + tuple(live_ref.at[part] for part in chunks),
        sems,
    )
    for copy in copies[:8]:
        copy.wait()
    len_ref, rawt_ref, decay_ref, bias_ref, cw_ref, cb_ref, bct_ref, x_ref = targets
    span, width = x_ref.shape
    heads = rawt_ref.shape[0]
    taps = cw_ref.shape[0]
    length = len_ref[0]
    xf[0:SUB, :] = jnp.zeros((SUB, width), F32)
    xf[SUB : SUB + span, :] = x_ref[...].astype(F32)
    square = iota((heads, heads), 0) == iota((heads, heads), 1)

    def column(row):
        return jnp.sum(jnp.where(square, row, 0.0), axis=1, keepdims=True)

    dtt = softplus(rawt_ref[...].astype(F32) + column(bias_ref[...]))
    dtt = jnp.where(iota((heads, span), 1) < length, dtt, 0.0)
    dtt_ref[...] = dtt
    tri = onehot(iota((span, span), 0) >= iota((span, span), 1))
    pieces = split3(dtt * -column(decay_ref[...]))
    cum_ref[...] = mm_nt(tri, pieces[0]) + mm_nt(tri, pieces[1]) + mm_nt(tri, pieces[2])
    cumt = mm_nt(pieces[0], tri) + mm_nt(pieces[1], tri) + mm_nt(pieces[2], tri)
    cumt_ref[...] = cumt
    weight = jnp.exp(cumt[:, span - 1 : span] - cumt) * dtt
    weight_hi, weight_lo = split2(weight)
    expand = expander(heads, width)
    weights = [cw_ref[k : k + 1, :].astype(F32) for k in range(taps)]
    block = 128
    total = jnp.zeros((STATE, width), F32)
    for start in range(0, span, block):
        part = slice(start, start + block)
        acc = cb_ref[...]
        for k in range(taps):
            first = SUB - taps + 1 + k + start
            acc = acc + xf[first : first + block, :] * weights[k]
        xc = silu(acc).astype(BF16)
        xc_ref[part, :] = xc
        wide = lax.dot_general(weight_hi[:, part], expand, TN, preferred_element_type=F32)
        wide = wide + lax.dot_general(
            weight_lo[:, part], expand, TN, preferred_element_type=F32
        )
        weighted = (xc.astype(F32) * wide).astype(BF16)
        total = total + mm(bct_ref[0, :, part], weighted)
    st_ref[0:STATE, :] = jnp.zeros((STATE, width), BF16)
    st_ref[STATE : 2 * STATE, :] = total.astype(BF16)
    row, col = iota((SUB, span), 0), iota((SUB, span), 1)
    tail = onehot((col == length - (taps - 1)) & (row == SUB - 1))
    tail_ref[...] = mm(tail, x_ref[...]).astype(BF16)
    row, col = iota((2 * SUB, span), 0), iota((2 * SUB, span), 1)
    both = mm(onehot(col == length - 2 + jnp.where(row < SUB, 0, 1)), x_ref[...])
    part = width // 4
    row = iota((SUB, part), 0)
    late = jnp.zeros((SUB, part), F32)
    for i in range(4):
        lanes = slice(i * part, (i + 1) * part)
        piece = jnp.where(row < 4, both[0:SUB, lanes], both[SUB:, lanes])
        late = jnp.where(jnp.bitwise_and(row, 3) == i, piece, late)
    late_ref[...] = late.astype(BF16)
    unit = onehot(iota((STATE, STATE), 0) == iota((STATE, STATE), 1))
    for k in range(live_ref.shape[0]):
        if k % chunk == 0:
            copies[8 + k // chunk].wait()
        turned_ref[k * STATE : (k + 1) * STATE, :] = mm_nt(unit, live_ref[k]).astype(BF16)


def prompt_kernel(
    xc_ref,
    z_ref,
    bct_ref,
    cum_ref,
    cumt_ref,
    dtt_ref,
    skip_ref,
    g_ref,
    ss_ref,
    scores,
):
    span, width = xc_ref.shape
    heads = cum_ref.shape[1]
    block = 128
    ones = jnp.ones((SUB, block), BF16)
    lanes = iota((block, block), 1)
    causal = iota((block, block), 0) >= lanes
    for start in range(0, span, block):
        stop = start + block
        scores[:, 0:stop] = lax.dot_general(
            bct_ref[1, :, start:stop], bct_ref[0, :, 0:stop], TN, preferred_element_type=F32
        )
        square = jnp.zeros((block, block), F32)
        for lane in range(0, width, block):
            halves = []
            for half in range(2):
                head = lane * heads // width + half
                at = cum_ref[start:stop, head : head + 1]
                gap = jnp.where(causal, at - cumt_ref[head : head + 1, start:stop], -jnp.inf)
                near = scores[:, start:stop] * jnp.exp(gap) * dtt_ref[head : head + 1, start:stop]
                yhead = mm(near.astype(BF16), xc_ref[start:stop, lane : lane + block])
                if start:
                    gap = at - cumt_ref[head : head + 1, 0:start]
                    far = scores[:, 0:start] * jnp.exp(gap) * dtt_ref[head : head + 1, 0:start]
                    yhead = yhead + mm(far.astype(BF16), xc_ref[0:start, lane : lane + block])
                halves.append(yhead)
            y = jnp.where(lanes < block // 2, halves[0], halves[1])
            xin = xc_ref[start:stop, lane : lane + block].astype(F32)
            y = y + skip_ref[:, lane : lane + block] * xin
            gate = y * silu(z_ref[start:stop, lane : lane + block].astype(F32))
            g_ref[start:stop, lane : lane + block] = gate
            square = square + gate * gate
        hi, lo = split2(square)
        ss_ref[:, start:stop] = mm_nt(ones, hi) + mm_nt(ones, lo)


def answer_kernel(*refs):
    sources, turned_hbm, out_ref, targets = refs[:5], refs[5], refs[6], refs[7:12]
    state_ref, sems, ys = refs[12:]
    chunk = state_ref.shape[0] // CHUNKS
    chunks = [slice(i * chunk, (i + 1) * chunk) for i in range(CHUNKS)]
    copies = fetch(
        sources + tuple(turned_hbm.at[part] for part in chunks),
        targets + tuple(state_ref.at[part] for part in chunks),
        sems,
    )
    for copy in copies[:5]:
        copy.wait()
    ask_ref, conv_ref, prefix_ref, tail_ref, late_ref = targets
    slots = ask_ref.shape[0]
    count = ys.shape[0]
    live_dev = count // SUB
    width = prefix_ref.shape[1]
    half = width // 2
    ask = ask_ref[...]
    down, lane = iota((slots, 1), 0), iota((1, slots), 1)
    in_slot = jnp.bitwise_and(down, SUB - 1)
    place = ask.astype(F32).reshape(slots // SUB, SUB, 2 * STATE)
    place = jnp.broadcast_to(place[:, 4:5, :], place.shape).reshape(slots, 2 * STATE)
    lane0 = onehot(iota((SUB, 2 * STATE), 1) == 0)
    across = mm_nt(lane0, place.astype(BF16))[0:1, :].astype(jnp.int32)
    back = (across - 1) * SUB + jnp.bitwise_and(lane, SUB - 1)
    got = mm(onehot(iota((count, 1), 0) == back), ask).astype(BF16)
    deep = GROUP_ROWS * STATE
    copy_of = jnp.bitwise_and(iota((1, deep), 1), STATE - 1)
    wide = mm(got, onehot(iota((2 * STATE, 1), 0) == copy_of))
    row, col = iota((count, 1), 0), iota((1, deep), 1)
    wanted = jnp.where(jnp.bitwise_and(row, SUB - 1) < 4, lax.div(row, SUB), -1)
    wanted = jnp.where(wanted >= 0, jnp.bitwise_and(wanted, GROUP_ROWS - 1), -1)
    wide = jnp.where(wanted == lax.div(col, STATE), wide, 0.0).astype(BF16)
    tall = GROUP_ROWS * SUB
    for group in range(live_dev // GROUP_ROWS):
        first = group * deep
        if first % chunk == 0:
            copies[5 + first // chunk].wait()
        rows = slice(group * tall, (group + 1) * tall)
        ys[rows, :] = mm(wide[rows, :], state_ref[first : first + deep, :]).astype(BF16)
    place = place[:, 0:1].astype(jnp.int32)
    there = onehot(iota((1, count), 1) == (place - 1) * SUB + in_slot)
    live = mm(there, ys[...])
    kept = conv_ref.shape[0]
    conv_row = (in_slot - 4) * live_dev + place - 1
    conv_row = jnp.where((place > 0) & (in_slot >= 4), conv_row, -1)
    there = onehot(iota((1, kept), 1) == conv_row)
    live = (live + mm(there, conv_ref[...])).reshape(slots // SUB, SUB, width)
    live = live + tail_ref[...].astype(F32)[None]
    out_ref[:, 0:width] = live.reshape(slots, width).astype(BF16)
    new = mm(ask, prefix_ref[...])
    new = jnp.where(in_slot < SUB // 2, new[:, 0:half], new[:, half:width])
    out_ref[:, width : width + half] = new.astype(BF16)
    part = late_ref.shape[1]
    late = jnp.broadcast_to(late_ref[...].astype(F32)[None], (slots // SUB, SUB, part))
    out_ref[:, width + half :] = late.reshape(slots, part).astype(BF16)


def decode_kernel(
    live_dev,
    readers,
    got_ref,
    tgt_l_ref,
    tgt_r_ref,
    xz_ref,
    bc_ref,
    raw_ref,
    decay_ref,
    bias_ref,
    skip_ref,
    cw_ref,
    cb_ref,
    pre_ss_ref,
    g_ref,
    ss_ref,
):
    slots = got_ref.shape[0]
    steps, _, rows, width = xz_ref.shape
    heads = raw_ref.shape[0] // steps
    raws = raw_ref[...].astype(F32).T
    span = pre_ss_ref.shape[1]
    taps = cw_ref.shape[0]
    half = width // 2
    pick_l = onehot(iota((SUB * live_dev, slots), 1) == tgt_l_ref[...])
    pick_r = onehot(iota((SUB * readers, slots), 1) == tgt_r_ref[...])
    live = mm(pick_l, got_ref[:, 0:width])
    new = mm(pick_r, got_ref[:, width:])
    old = mm(pick_r[(SUB - 1) * readers :, :], got_ref[:, 0:width])

    def live_row(r):
        return live[r * live_dev : (r + 1) * live_dev, :]

    def new_row(r, first, last):
        return new[r * readers : (r + 1) * readers, first:last]

    def tail_row(r):
        return jnp.concatenate([new_row(r + i, half, half + width // 4) for i in range(4)], 1)

    first = []
    for t in range(steps):
        wide = jnp.concatenate([new_row(t, 0, half), new_row(t + 4, 0, half)], 1)
        first.append(jnp.concatenate([live_row(t), wide], 0))
    inputs = [
        jnp.concatenate([live_row(4), old], 0),
        jnp.concatenate([live_row(5), tail_row(0)], 0),
        jnp.concatenate([live_row(6), tail_row(4)], 0),
    ]
    inputs += [xz_ref[t, 0].astype(F32) for t in range(steps)]
    expand = expander(heads, width)
    weights = [cw_ref[k : k + 1, :].astype(F32) for k in range(taps)]
    dts, logs, bmats, cmats, xcs, gates = [], [], [], [], [], []
    for t in range(steps):
        acc = cb_ref[...]
        for k in range(taps):
            acc = acc + inputs[t + k] * weights[k]
        xcs.append(silu(acc).astype(BF16).astype(F32))
        dt = softplus(raws[:, t * heads : (t + 1) * heads] + bias_ref[...])
        dts.append(dt)
        decayed = -dt * decay_ref[...]
        logs.append(decayed if t == 0 else logs[-1] + decayed)
        bmats.append(bc_ref[t, 0].astype(F32))
        cmats.append(bc_ref[t, 1].astype(F32))
        y = spread(jnp.exp(logs[t]), expand) * first[t]
        for s in range(t + 1):
            score = jnp.sum(bmats[s] * cmats[t], axis=1, keepdims=True)
            factor = dts[s] * score
            if s < t:
                factor = jnp.exp(logs[t] - logs[s]) * factor
            else:
                factor = factor + skip_ref[...]
            y = y + spread(factor, expand) * xcs[s]
        gate = y * silu(xz_ref[t, 1].astype(F32))
        g_ref[t * rows : (t + 1) * rows, :] = gate
        gates.append(gate * gate)
    square = jnp.concatenate(gates, 0)
    hi, lo = split2(square)
    ones = jnp.ones((SUB, width), BF16)
    sums = mm_nt(ones, hi) + mm_nt(ones, lo)
    lanes = ss_ref.shape[2]
    pad = -sums.shape[1] % lanes
    sums = jnp.concatenate([pre_ss_ref[...], sums, jnp.zeros((SUB, pad), F32)], 1)
    parts = [sums[0:1, i : i + lanes] for i in range(0, sums.shape[1], lanes)]
    parts += [jnp.zeros((SUB - len(parts), lanes), F32)]
    ss_ref[...] = jnp.broadcast_to(jnp.concatenate(parts, 0)[None], ss_ref.shape)


def finish_kernel(width_all, ss_ref, pre_ref, step_ref, gain_ref, pre_out_ref, step_out_ref):
    total = ss_ref[0]
    for i in range(1, ss_ref.shape[0]):
        total = total + ss_ref[i]
    scale = lax.rsqrt(total / width_all + EPS)
    gain = gain_ref[...]
    span = pre_ref.shape[0]
    block = 128

    def column(first, rows):
        row = scale[first // block : first // block + 1, :]
        diag = iota((rows, block), 0) == iota((rows, block), 1)
        return jnp.sum(jnp.where(diag, row, 0.0), axis=1, keepdims=True)

    for start in range(0, span, block):
        part = slice(start, start + block)
        pre_out_ref[part, :] = (pre_ref[part, :] * column(start, block) * gain).astype(BF16)
    count = step_ref.shape[0]
    for start in range(0, count, block):
        rows = min(block, count - start)
        part = slice(start, start + rows)
        step_out_ref[part, :] = (step_ref[part, :] * column(span + start, rows) * gain).astype(
            BF16
        )


def params(limit=24 * 1024 * 1024, **more):
    return pltpu.CompilerParams(vmem_limit_bytes=limit, **more)


def cost(flops, moved, special=0):
    return pl.CostEstimate(flops=flops, bytes_accessed=moved, transcendentals=special)


def vmem():
    return pl.BlockSpec(memory_space=pltpu.VMEM)


def hbm():
    return pl.BlockSpec(memory_space=pltpu.HBM)


def shape(dims, kind):
    return jax.ShapeDtypeStruct(dims, kind)


def per_device(
    pre_x,
    pre_z,
    pre_bc,
    pre_raw,
    prompt_len,
    live_state,
    live_conv,
    source,
    reader,
    step_xz,
    step_bc,
    step_raw,
    decay,
    dt_bias,
    conv_weight,
    conv_bias,
    skip,
    norm_gain,
):
    _, span, width = pre_x.shape
    mp = lax.axis_size("mp")
    gens = lax.axis_size("gen")
    width_all = width * mp
    live_dev = source.shape[0]
    readers = reader.shape[0]
    heads = pre_raw.shape[2]
    steps, _, rows, _ = step_xz.shape
    slots = gens * SUB
    offset = jnp.arange(SUB, dtype=jnp.int32)[:, None]
    tgt_l = SUB * (source // live_dev)[None, :] + offset
    tgt_r = SUB * reader[None, :] + offset

    conv_rows = jnp.transpose(live_conv, (1, 0, 2)).reshape(-1, width)
    bct = jnp.swapaxes(pre_bc[0], 1, 2)
    dma = pltpu.SemaphoreType.DMA

    def staged(*arrays):
        return [pltpu.VMEM(array.shape, array.dtype) for array in arrays]

    operands = (step_bc, source[None], reader[None])
    ask = pl.pallas_call(
        ask_kernel,
        out_shape=shape((slots, 2 * STATE), BF16),
        in_specs=[hbm()] * len(operands),
        out_specs=vmem(),
        scratch_shapes=staged(*operands) + [dma((len(operands),))],
        compiler_params=params(WHOLE),
        cost_estimate=cost(2 * slots * 384 * 128, 300000),
        name="ask",
    )(*operands)
    lanes = ask.shape[1]
    asked = lax.all_to_all(
        ask.reshape(gens, SUB, lanes), "gen", split_axis=0, concat_axis=0, tiled=True
    ).reshape(slots, lanes)

    live = live_state.reshape(live_dev, width, STATE)
    operands = (
        prompt_len,
        pre_raw[0].T,
        decay[None],
        dt_bias[None],
        conv_weight,
        conv_bias[None],
        bct,
        pre_x[0],
    )
    xconv, cum, cumt, dtt, prefix, tail, late, turned = pl.pallas_call(
        state_kernel,
        out_shape=(
            shape((span, width), BF16),
            shape((span, heads), F32),
            shape((heads, span), F32),
            shape((heads, span), F32),
            shape((2 * STATE, width), BF16),
            shape((SUB, width), BF16),
            shape((SUB, width // 4), BF16),
            shape((live_dev * STATE, width), BF16),
        ),
        in_specs=[hbm()] * (len(operands) + 1),
        out_specs=(vmem(),) * 8,
        scratch_shapes=[pltpu.SMEM((1,), jnp.int32)]
        + staged(*operands[1:], live)
        + [dma((len(operands) + CHUNKS,)), pltpu.VMEM((span + SUB, width), F32)],
        compiler_params=params(WHOLE),
        cost_estimate=cost(2 * 10 * span * span * 64, 8000000, span * width * 2),
        name="state",
    )(*operands, live)

    operands = (asked, conv_rows, prefix, tail, late)
    answer = pl.pallas_call(
        answer_kernel,
        out_shape=shape((slots, width + width // 2 + width // 4), BF16),
        in_specs=[pl.BlockSpec(memory_space=pl.ANY)] + [hbm()] * len(operands),
        out_specs=vmem(),
        scratch_shapes=staged(*operands, turned)
        + [
            dma((len(operands) + CHUNKS,)),
            pltpu.VMEM((live_dev * SUB, width), BF16),
        ],
        compiler_params=params(WHOLE),
        cost_estimate=cost(2 * slots * 512 * 1024, 4000000),
        name="answer",
    )(*operands, turned)
    lanes = answer.shape[1]
    got = lax.all_to_all(
        answer.reshape(gens, SUB, lanes), "gen", split_axis=0, concat_axis=0, tiled=True
    ).reshape(slots, lanes)

    pre_gate, pre_ss = pl.pallas_call(
        prompt_kernel,
        out_shape=(
            shape((span, width), F32),
            shape((SUB, span), F32),
        ),
        in_specs=[vmem()] * 7,
        out_specs=(vmem(),) * 2,
        scratch_shapes=[pltpu.VMEM((128, span), F32)],
        compiler_params=params(),
        cost_estimate=cost(2 * heads * span * span * 128, 2500000, heads * span * span),
        name="prompt",
    )(xconv, pre_z[0], bct, cum, cumt, dtt, jnp.repeat(skip, width // heads)[None])

    count = steps * rows
    step_gate, sums = pl.pallas_call(
        lambda *refs: decode_kernel(live_dev, readers, *refs),
        out_shape=(shape((count, width), F32), shape((mp, SUB, 128), F32)),
        in_specs=[vmem()] * 12,
        out_specs=(vmem(), vmem()),
        compiler_params=params(),
        cost_estimate=cost(2 * 384 * 512 * 512, 2500000),
        name="decode",
    )(
        got,
        tgt_l.reshape(-1, 1),
        tgt_r.reshape(-1, 1),
        step_xz,
        step_bc,
        jnp.swapaxes(step_raw, 1, 2).reshape(steps * heads, rows),
        decay[None],
        dt_bias[None],
        skip[None],
        conv_weight,
        conv_bias[None],
        pre_ss,
    )
    sums = lax.all_to_all(sums, "mp", split_axis=0, concat_axis=0, tiled=True)

    prefill_out, decoded = pl.pallas_call(
        lambda *refs: finish_kernel(width_all, *refs),
        out_shape=(shape((span, width), BF16), shape((count, width), BF16)),
        in_specs=[vmem()] * 4,
        out_specs=(vmem(), vmem()),
        compiler_params=params(),
        cost_estimate=cost(1000000, 2500000),
        name="finish",
    )(sums, pre_gate, step_gate, norm_gain[None])
    return (prefill_out[None], decoded.reshape(steps, rows, width))


def solution(mesh):
    placed = (
        P("gen", None, "mp"),
        P("gen", None, "mp"),
        P("gen", None, None, "mp"),
        P("gen", None, "mp"),
        P("gen"),
        P("gen", "mp", None, None),
        P("gen", None, "mp"),
        P("gen"),
        P("gen"),
        P(None, None, "gen", "mp"),
        P(None, None, "gen", "mp"),
        P(None, "gen", "mp"),
        P("mp"),
        P("mp"),
        P(None, "mp"),
        P("mp"),
        P("mp"),
        P("mp"),
    )
    return jax.shard_map(
        per_device,
        mesh=mesh,
        in_specs=placed,
        out_specs=(P("gen", None, "mp"), P(None, "gen", "mp")),
        check_vma=False,
    )
```

```python
import jax
import jax.numpy as jnp
from jax import lax
from jax.experimental import pallas as pl
from jax.experimental.pallas import tpu as pltpu
from jax.sharding import PartitionSpec as P

STATE = 64
EPS = 1e-05
SUB = 8
CHUNKS = 4
GROUP_ROWS = 4
WHOLE = 60 * 1024 * 1024
F32 = jnp.float32
BF16 = jnp.bfloat16
NT = (((1,), (1,)), ((), ()))
TN = (((0,), (0,)), ((), ()))


def iota(shape, dim):
    return lax.broadcasted_iota(jnp.int32, shape, dim)


def mm(a, b):
    return jnp.dot(a, b, preferred_element_type=F32)


def mm_nt(a, b):
    return lax.dot_general(a, b, NT, preferred_element_type=F32)


def onehot(mask):
    return jnp.where(mask, 1.0, 0.0).astype(BF16)


def split2(x):
    hi = x.astype(BF16)
    return hi, (x - hi.astype(F32)).astype(BF16)


def split3(x):
    hi = x.astype(BF16)
    rest = x - hi.astype(F32)
    mid = rest.astype(BF16)
    return hi, mid, (rest - mid.astype(F32)).astype(BF16)


def silu(x):
    return x / (1.0 + jnp.exp(-x))


def softplus(x):
    return jnp.maximum(x, 0.0) + jnp.log1p(jnp.exp(-jnp.abs(x)))


def expander(heads, width):
    return onehot(iota((heads, width), 1) // (width // heads) == iota((heads, width), 0))


def spread(x, expand):
    hi, lo = split2(x)
    return mm(hi, expand) + mm(lo, expand)


def fetch(sources, targets, sems):
    copies = [
        pltpu.make_async_copy(source, target, sems.at[i])
        for i, (source, target) in enumerate(zip(sources, targets))
    ]
    for copy in copies:
        copy.start()
    return copies


def ask_kernel(*refs):
    sources, out_ref, targets, sems = refs[:3], refs[3], refs[4:7], refs[7]
    for copy in fetch(sources, targets, sems):
        copy.wait()
    bc_ref, source_ref, reader_ref = targets
    steps = bc_ref.shape[0]
    slots = out_ref.shape[0]
    live_dev = source_ref.shape[1]
    readers = reader_ref.shape[1]
    zeros_l = jnp.zeros((live_dev, STATE), F32)
    place = (iota((live_dev, STATE), 0) + 1).astype(F32)
    parts = [bc_ref[t, 1, 0:live_dev, :].astype(F32) for t in range(steps)]
    parts += [place] + [zeros_l] * (SUB - steps - 1)
    data_l = jnp.concatenate(parts, 0)
    data_l = jnp.concatenate([data_l, jnp.zeros_like(data_l)], 1).astype(BF16)
    parts = [
        bc_ref[t % steps, 1, live_dev : live_dev + readers, :].astype(F32) for t in range(SUB)
    ]
    data_r = jnp.concatenate(parts, 0)
    data_r = jnp.concatenate([jnp.zeros_like(data_r), data_r], 1).astype(BF16)
    first_l = lax.div(source_ref[...], live_dev) * SUB
    first_r = reader_ref[...] * SUB
    tgt_l = jnp.concatenate([first_l + r for r in range(SUB)], 1)
    tgt_r = jnp.concatenate([first_r + r for r in range(SUB)], 1)
    pick_l = onehot(iota((slots, SUB * live_dev), 0) == tgt_l)
    pick_r = onehot(iota((slots, SUB * readers), 0) == tgt_r)
    out_ref[...] = (mm(pick_l, data_l) + mm(pick_r, data_r)).astype(BF16)


def state_kernel(*refs):
    sources, live_hbm, outs, targets = refs[:8], refs[8], refs[9:17], refs[17:25]
    live_ref, sems, xf = refs[25:]
    xc_ref, cum_ref, cumt_ref, dtt_ref, st_ref, tail_ref, late_ref, turned_ref = outs
    chunk = live_ref.shape[0] // CHUNKS
    chunks = [slice(i * chunk, (i + 1) * chunk) for i in range(CHUNKS)]
    copies = fetch(
        sources + tuple(live_hbm.at[part] for part in chunks),
        targets + tuple(live_ref.at[part] for part in chunks),
        sems,
    )
    for copy in copies[:8]:
        copy.wait()
    len_ref, rawt_ref, decay_ref, bias_ref, cw_ref, cb_ref, bct_ref, x_ref = targets
    span, width = x_ref.shape
    heads = rawt_ref.shape[0]
    taps = cw_ref.shape[0]
    length = len_ref[0]
    xf[0:SUB, :] = jnp.zeros((SUB, width), F32)
    xf[SUB : SUB + span, :] = x_ref[...].astype(F32)
    square = iota((heads, heads), 0) == iota((heads, heads), 1)

    def column(row):
        return jnp.sum(jnp.where(square, row, 0.0), axis=1, keepdims=True)

    dtt = softplus(rawt_ref[...].astype(F32) + column(bias_ref[...]))
    dtt = jnp.where(iota((heads, span), 1) < length, dtt, 0.0)
    dtt_ref[...] = dtt
    tri = onehot(iota((span, span), 0) >= iota((span, span), 1))
    pieces = split3(dtt * -column(decay_ref[...]))
    cum_ref[...] = mm_nt(tri, pieces[0]) + mm_nt(tri, pieces[1]) + mm_nt(tri, pieces[2])
    cumt = mm_nt(pieces[0], tri) + mm_nt(pieces[1], tri) + mm_nt(pieces[2], tri)
    cumt_ref[...] = cumt
    weight = jnp.exp(cumt[:, span - 1 : span] - cumt) * dtt
    weight_hi, weight_lo = split2(weight)
    expand = expander(heads, width)
    weights = [cw_ref[k : k + 1, :].astype(F32) for k in range(taps)]
    block = 128
    total = jnp.zeros((STATE, width), F32)
    for start in range(0, span, block):
        part = slice(start, start + block)
        acc = cb_ref[...]
        for k in range(taps):
            first = SUB - taps + 1 + k + start
            acc = acc + xf[first : first + block, :] * weights[k]
        xc = silu(acc).astype(BF16)
        xc_ref[part, :] = xc
        wide = lax.dot_general(weight_hi[:, part], expand, TN, preferred_element_type=F32)
        wide = wide + lax.dot_general(
            weight_lo[:, part], expand, TN, preferred_element_type=F32
        )
        weighted = (xc.astype(F32) * wide).astype(BF16)
        total = total + mm(bct_ref[0, :, part], weighted)
    st_ref[0:STATE, :] = jnp.zeros((STATE, width), BF16)
    st_ref[STATE : 2 * STATE, :] = total.astype(BF16)
    row, col = iota((SUB, span), 0), iota((SUB, span), 1)
    tail = onehot((col == length - (taps - 1)) & (row == SUB - 1))
    tail_ref[...] = mm(tail, x_ref[...]).astype(BF16)
    row, col = iota((2 * SUB, span), 0), iota((2 * SUB, span), 1)
    both = mm(onehot(col == length - 2 + jnp.where(row < SUB, 0, 1)), x_ref[...])
    part = width // 4
    row = iota((SUB, part), 0)
    late = jnp.zeros((SUB, part), F32)
    for i in range(4):
        lanes = slice(i * part, (i + 1) * part)
        piece = jnp.where(row < 4, both[0:SUB, lanes], both[SUB:, lanes])
        late = jnp.where(jnp.bitwise_and(row, 3) == i, piece, late)
    late_ref[...] = late.astype(BF16)
    unit = onehot(iota((STATE, STATE), 0) == iota((STATE, STATE), 1))
    for k in range(live_ref.shape[0]):
        if k % chunk == 0:
            copies[8 + k // chunk].wait()
        turned_ref[k * STATE : (k + 1) * STATE, :] = mm_nt(unit, live_ref[k]).astype(BF16)


def prompt_kernel(
    xc_ref,
    z_ref,
    bct_ref,
    cum_ref,
    cumt_ref,
    dtt_ref,
    skip_ref,
    g_ref,
    ss_ref,
    scores,
):
    span, width = xc_ref.shape
    heads = cum_ref.shape[1]
    block = 128
    ones = jnp.ones((SUB, block), BF16)
    lanes = iota((block, block), 1)
    causal = iota((block, block), 0) >= lanes
    for start in range(0, span, block):
        stop = start + block
        scores[:, 0:stop] = lax.dot_general(
            bct_ref[1, :, start:stop], bct_ref[0, :, 0:stop], TN, preferred_element_type=F32
        )
        square = jnp.zeros((block, block), F32)
        for lane in range(0, width, block):
            halves = []
            for half in range(2):
                head = lane * heads // width + half
                at = cum_ref[start:stop, head : head + 1]
                gap = jnp.where(causal, at - cumt_ref[head : head + 1, start:stop], -jnp.inf)
                near = scores[:, start:stop] * jnp.exp(gap) * dtt_ref[head : head + 1, start:stop]
                yhead = mm(near.astype(BF16), xc_ref[start:stop, lane : lane + block])
                if start:
                    gap = at - cumt_ref[head : head + 1, 0:start]
                    far = scores[:, 0:start] * jnp.exp(gap) * dtt_ref[head : head + 1, 0:start]
                    yhead = yhead + mm(far.astype(BF16), xc_ref[0:start, lane : lane + block])
                halves.append(yhead)
            y = jnp.where(lanes < block // 2, halves[0], halves[1])
            xin = xc_ref[start:stop, lane : lane + block].astype(F32)
            y = y + skip_ref[:, lane : lane + block] * xin
            gate = y * silu(z_ref[start:stop, lane : lane + block].astype(F32))
            g_ref[start:stop, lane : lane + block] = gate
            square = square + gate * gate
        hi, lo = split2(square)
        ss_ref[:, start:stop] = mm_nt(ones, hi) + mm_nt(ones, lo)


def answer_kernel(*refs):
    ask_ref, conv_ref, prefix_ref, tail_ref, late_ref, state_ref, out_ref, ys = refs
    slots = ask_ref.shape[0]
    count = ys.shape[0]
    live_dev = count // SUB
    width = prefix_ref.shape[1]
    half = width // 2
    ask = ask_ref[...]
    down, lane = iota((slots, 1), 0), iota((1, slots), 1)
    in_slot = jnp.bitwise_and(down, SUB - 1)
    place = ask.astype(F32).reshape(slots // SUB, SUB, 2 * STATE)
    place = jnp.broadcast_to(place[:, 4:5, :], place.shape).reshape(slots, 2 * STATE)
    lane0 = onehot(iota((SUB, 2 * STATE), 1) == 0)
    across = mm_nt(lane0, place.astype(BF16))[0:1, :].astype(jnp.int32)
    back = (across - 1) * SUB + jnp.bitwise_and(lane, SUB - 1)
    got = mm(onehot(iota((count, 1), 0) == back), ask).astype(BF16)
    deep = GROUP_ROWS * STATE
    copy_of = jnp.bitwise_and(iota((1, deep), 1), STATE - 1)
    wide = mm(got, onehot(iota((2 * STATE, 1), 0) == copy_of))
    row, col = iota((count, 1), 0), iota((1, deep), 1)
    wanted = jnp.where(jnp.bitwise_and(row, SUB - 1) < 4, lax.div(row, SUB), -1)
    wanted = jnp.where(wanted >= 0, jnp.bitwise_and(wanted, GROUP_ROWS - 1), -1)
    wide = jnp.where(wanted == lax.div(col, STATE), wide, 0.0).astype(BF16)
    tall = GROUP_ROWS * SUB
    for group in range(live_dev // GROUP_ROWS):
        first = group * deep
        rows = slice(group * tall, (group + 1) * tall)
        ys[rows, :] = mm(wide[rows, :], state_ref[first : first + deep, :]).astype(BF16)
    place = place[:, 0:1].astype(jnp.int32)
    there = onehot(iota((1, count), 1) == (place - 1) * SUB + in_slot)
    live = mm(there, ys[...])
    kept = conv_ref.shape[0]
    conv_row = (in_slot - 4) * live_dev + place - 1
    conv_row = jnp.where((place > 0) & (in_slot >= 4), conv_row, -1)
    there = onehot(iota((1, kept), 1) == conv_row)
    live = (live + mm(there, conv_ref[...])).reshape(slots // SUB, SUB, width)
    live = live + tail_ref[...].astype(F32)[None]
    out_ref[:, 0:width] = live.reshape(slots, width).astype(BF16)
    new = mm(ask, prefix_ref[...])
    new = jnp.where(in_slot < SUB // 2, new[:, 0:half], new[:, half:width])
    out_ref[:, width : width + half] = new.astype(BF16)
    part = late_ref.shape[1]
    late = jnp.broadcast_to(late_ref[...].astype(F32)[None], (slots // SUB, SUB, part))
    out_ref[:, width + half :] = late.reshape(slots, part).astype(BF16)


def decode_kernel(
    live_dev,
    readers,
    got_ref,
    tgt_l_ref,
    tgt_r_ref,
    xz_ref,
    bc_ref,
    raw_ref,
    decay_ref,
    bias_ref,
    skip_ref,
    cw_ref,
    cb_ref,
    pre_ss_ref,
    g_ref,
    ss_ref,
):
    slots = got_ref.shape[0]
    steps, _, rows, width = xz_ref.shape
    heads = raw_ref.shape[0] // steps
    raws = raw_ref[...].astype(F32).T
    span = pre_ss_ref.shape[1]
    taps = cw_ref.shape[0]
    half = width // 2
    pick_l = onehot(iota((SUB * live_dev, slots), 1) == tgt_l_ref[...])
    pick_r = onehot(iota((SUB * readers, slots), 1) == tgt_r_ref[...])
    live = mm(pick_l, got_ref[:, 0:width])
    new = mm(pick_r, got_ref[:, width:])
    old = mm(pick_r[(SUB - 1) * readers :, :], got_ref[:, 0:width])

    def live_row(r):
        return live[r * live_dev : (r + 1) * live_dev, :]

    def new_row(r, first, last):
        return new[r * readers : (r + 1) * readers, first:last]

    def tail_row(r):
        return jnp.concatenate([new_row(r + i, half, half + width // 4) for i in range(4)], 1)

    first = []
    for t in range(steps):
        wide = jnp.concatenate([new_row(t, 0, half), new_row(t + 4, 0, half)], 1)
        first.append(jnp.concatenate([live_row(t), wide], 0))
    inputs = [
        jnp.concatenate([live_row(4), old], 0),
        jnp.concatenate([live_row(5), tail_row(0)], 0),
        jnp.concatenate([live_row(6), tail_row(4)], 0),
    ]
    inputs += [xz_ref[t, 0].astype(F32) for t in range(steps)]
    expand = expander(heads, width)
    weights = [cw_ref[k : k + 1, :].astype(F32) for k in range(taps)]
    dts, logs, bmats, cmats, xcs, gates = [], [], [], [], [], []
    for t in range(steps):
        acc = cb_ref[...]
        for k in range(taps):
            acc = acc + inputs[t + k] * weights[k]
        xcs.append(silu(acc).astype(BF16).astype(F32))
        dt = softplus(raws[:, t * heads : (t + 1) * heads] + bias_ref[...])
        dts.append(dt)
        decayed = -dt * decay_ref[...]
        logs.append(decayed if t == 0 else logs[-1] + decayed)
        bmats.append(bc_ref[t, 0].astype(F32))
        cmats.append(bc_ref[t, 1].astype(F32))
        y = spread(jnp.exp(logs[t]), expand) * first[t]
        for s in range(t + 1):
            score = jnp.sum(bmats[s] * cmats[t], axis=1, keepdims=True)
            factor = dts[s] * score
            if s < t:
                factor = jnp.exp(logs[t] - logs[s]) * factor
            else:
                factor = factor + skip_ref[...]
            y = y + spread(factor, expand) * xcs[s]
        gate = y * silu(xz_ref[t, 1].astype(F32))
        g_ref[t * rows : (t + 1) * rows, :] = gate
        gates.append(gate * gate)
    square = jnp.concatenate(gates, 0)
    hi, lo = split2(square)
    ones = jnp.ones((SUB, width), BF16)
    sums = mm_nt(ones, hi) + mm_nt(ones, lo)
    lanes = ss_ref.shape[2]
    pad = -sums.shape[1] % lanes
    sums = jnp.concatenate([pre_ss_ref[...], sums, jnp.zeros((SUB, pad), F32)], 1)
    parts = [sums[0:1, i : i + lanes] for i in range(0, sums.shape[1], lanes)]
    parts += [jnp.zeros((SUB - len(parts), lanes), F32)]
    ss_ref[...] = jnp.broadcast_to(jnp.concatenate(parts, 0)[None], ss_ref.shape)


def finish_kernel(width_all, ss_ref, pre_ref, step_ref, gain_ref, pre_out_ref, step_out_ref):
    total = ss_ref[0]
    for i in range(1, ss_ref.shape[0]):
        total = total + ss_ref[i]
    scale = lax.rsqrt(total / width_all + EPS)
    gain = gain_ref[...]
    span = pre_ref.shape[0]
    block = 128

    def column(first, rows):
        row = scale[first // block : first // block + 1, :]
        diag = iota((rows, block), 0) == iota((rows, block), 1)
        return jnp.sum(jnp.where(diag, row, 0.0), axis=1, keepdims=True)

    for start in range(0, span, block):
        part = slice(start, start + block)
        pre_out_ref[part, :] = (pre_ref[part, :] * column(start, block) * gain).astype(BF16)
    count = step_ref.shape[0]
    for start in range(0, count, block):
        rows = min(block, count - start)
        part = slice(start, start + rows)
        step_out_ref[part, :] = (step_ref[part, :] * column(span + start, rows) * gain).astype(
            BF16
        )


def params(limit=24 * 1024 * 1024, **more):
    return pltpu.CompilerParams(vmem_limit_bytes=limit, **more)


def cost(flops, moved, special=0):
    return pl.CostEstimate(flops=flops, bytes_accessed=moved, transcendentals=special)


def vmem():
    return pl.BlockSpec(memory_space=pltpu.VMEM)


def hbm():
    return pl.BlockSpec(memory_space=pltpu.HBM)


def shape(dims, kind):
    return jax.ShapeDtypeStruct(dims, kind)


def per_device(
    pre_x,
    pre_z,
    pre_bc,
    pre_raw,
    prompt_len,
    live_state,
    live_conv,
    source,
    reader,
    step_xz,
    step_bc,
    step_raw,
    decay,
    dt_bias,
    conv_weight,
    conv_bias,
    skip,
    norm_gain,
):
    _, span, width = pre_x.shape
    mp = lax.axis_size("mp")
    gens = lax.axis_size("gen")
    width_all = width * mp
    live_dev = source.shape[0]
    readers = reader.shape[0]
    heads = pre_raw.shape[2]
    steps, _, rows, _ = step_xz.shape
    slots = gens * SUB
    offset = jnp.arange(SUB, dtype=jnp.int32)[:, None]
    tgt_l = SUB * (source // live_dev)[None, :] + offset
    tgt_r = SUB * reader[None, :] + offset

    conv_rows = jnp.transpose(live_conv, (1, 0, 2)).reshape(-1, width)
    bct = jnp.swapaxes(pre_bc[0], 1, 2)
    dma = pltpu.SemaphoreType.DMA

    def staged(*arrays):
        return [pltpu.VMEM(array.shape, array.dtype) for array in arrays]

    operands = (step_bc, source[None], reader[None])
    ask = pl.pallas_call(
        ask_kernel,
        out_shape=shape((slots, 2 * STATE), BF16),
        in_specs=[hbm()] * len(operands),
        out_specs=vmem(),
        scratch_shapes=staged(*operands) + [dma((len(operands),))],
        compiler_params=params(WHOLE),
        cost_estimate=cost(2 * slots * 384 * 128, 300000),
        name="ask",
    )(*operands)
    lanes = ask.shape[1]
    asked = lax.all_to_all(
        ask.reshape(gens, SUB, lanes), "gen", split_axis=0, concat_axis=0, tiled=True
    ).reshape(slots, lanes)

    live = live_state.reshape(live_dev, width, STATE)
    operands = (
        prompt_len,
        pre_raw[0].T,
        decay[None],
        dt_bias[None],
        conv_weight,
        conv_bias[None],
        bct,
        pre_x[0],
    )
    xconv, cum, cumt, dtt, prefix, tail, late, turned = pl.pallas_call(
        state_kernel,
        out_shape=(
            shape((span, width), BF16),
            shape((span, heads), F32),
            shape((heads, span), F32),
            shape((heads, span), F32),
            shape((2 * STATE, width), BF16),
            shape((SUB, width), BF16),
            shape((SUB, width // 4), BF16),
            shape((live_dev * STATE, width), BF16),
        ),
        in_specs=[hbm()] * (len(operands) + 1),
        out_specs=(vmem(),) * 8,
        scratch_shapes=[pltpu.SMEM((1,), jnp.int32)]
        + staged(*operands[1:], live)
        + [dma((len(operands) + CHUNKS,)), pltpu.VMEM((span + SUB, width), F32)],
        compiler_params=params(WHOLE),
        cost_estimate=cost(2 * 10 * span * span * 64, 8000000, span * width * 2),
        name="state",
    )(*operands, live)

    operands = (asked, conv_rows, prefix, tail, late)
    answer = pl.pallas_call(
        answer_kernel,
        out_shape=shape((slots, width + width // 2 + width // 4), BF16),
        in_specs=[vmem()] * (len(operands) + 1),
        out_specs=vmem(),
        scratch_shapes=[pltpu.VMEM((live_dev * SUB, width), BF16)],
        compiler_params=params(),
        cost_estimate=cost(2 * slots * 512 * 1024, 4000000),
        name="answer",
    )(*operands, turned)
    lanes = answer.shape[1]
    got = lax.all_to_all(
        answer.reshape(gens, SUB, lanes), "gen", split_axis=0, concat_axis=0, tiled=True
    ).reshape(slots, lanes)

    pre_gate, pre_ss = pl.pallas_call(
        prompt_kernel,
        out_shape=(
            shape((span, width), F32),
            shape((SUB, span), F32),
        ),
        in_specs=[vmem()] * 7,
        out_specs=(vmem(),) * 2,
        scratch_shapes=[pltpu.VMEM((128, span), F32)],
        compiler_params=params(),
        cost_estimate=cost(2 * heads * span * span * 128, 2500000, heads * span * span),
        name="prompt",
    )(xconv, pre_z[0], bct, cum, cumt, dtt, jnp.repeat(skip, width // heads)[None])

    count = steps * rows
    step_gate, sums = pl.pallas_call(
        lambda *refs: decode_kernel(live_dev, readers, *refs),
        out_shape=(shape((count, width), F32), shape((mp, SUB, 128), F32)),
        in_specs=[vmem()] * 12,
        out_specs=(vmem(), vmem()),
        compiler_params=params(),
        cost_estimate=cost(2 * 384 * 512 * 512, 2500000),
        name="decode",
    )(
        got,
        tgt_l.reshape(-1, 1),
        tgt_r.reshape(-1, 1),
        step_xz,
        step_bc,
        jnp.swapaxes(step_raw, 1, 2).reshape(steps * heads, rows),
        decay[None],
        dt_bias[None],
        skip[None],
        conv_weight,
        conv_bias[None],
        pre_ss,
    )
    sums = lax.all_to_all(sums, "mp", split_axis=0, concat_axis=0, tiled=True)

    prefill_out, decoded = pl.pallas_call(
        lambda *refs: finish_kernel(width_all, *refs),
        out_shape=(shape((span, width), BF16), shape((count, width), BF16)),
        in_specs=[vmem()] * 4,
        out_specs=(vmem(), vmem()),
        compiler_params=params(),
        cost_estimate=cost(1000000, 2500000),
        name="finish",
    )(sums, pre_gate, step_gate, norm_gain[None])
    return (prefill_out[None], decoded.reshape(steps, rows, width))


def solution(mesh):
    placed = (
        P("gen", None, "mp"),
        P("gen", None, "mp"),
        P("gen", None, None, "mp"),
        P("gen", None, "mp"),
        P("gen"),
        P("gen", "mp", None, None),
        P("gen", None, "mp"),
        P("gen"),
        P("gen"),
        P(None, None, "gen", "mp"),
        P(None, None, "gen", "mp"),
        P(None, "gen", "mp"),
        P("mp"),
        P("mp"),
        P(None, "mp"),
        P("mp"),
        P("mp"),
        P("mp"),
    )
    return jax.shard_map(
        per_device,
        mesh=mesh,
        in_specs=placed,
        out_specs=(P("gen", None, "mp"), P(None, "gen", "mp")),
        check_vma=False,
    )
```

```python
import jax
import jax.numpy as jnp
from jax import lax
from jax.experimental import pallas as pl
from jax.experimental.pallas import tpu as pltpu
from jax.sharding import PartitionSpec as P

STATE = 64
EPS = 1e-05
SUB = 8
CHUNKS = 4
GROUP_ROWS = 4
WHOLE = 60 * 1024 * 1024
F32 = jnp.float32
BF16 = jnp.bfloat16
NT = (((1,), (1,)), ((), ()))
TN = (((0,), (0,)), ((), ()))


def iota(shape, dim):
    return lax.broadcasted_iota(jnp.int32, shape, dim)


def mm(a, b):
    return jnp.dot(a, b, preferred_element_type=F32)


def mm_nt(a, b):
    return lax.dot_general(a, b, NT, preferred_element_type=F32)


def onehot(mask):
    return jnp.where(mask, 1.0, 0.0).astype(BF16)


def split2(x):
    hi = x.astype(BF16)
    return hi, (x - hi.astype(F32)).astype(BF16)


def split3(x):
    hi = x.astype(BF16)
    rest = x - hi.astype(F32)
    mid = rest.astype(BF16)
    return hi, mid, (rest - mid.astype(F32)).astype(BF16)


def silu(x):
    return x / (1.0 + jnp.exp(-x))


def softplus(x):
    return jnp.maximum(x, 0.0) + jnp.log1p(jnp.exp(-jnp.abs(x)))


def expander(heads, width):
    return onehot(iota((heads, width), 1) // (width // heads) == iota((heads, width), 0))


def spread(x, expand):
    hi, lo = split2(x)
    return mm(hi, expand) + mm(lo, expand)


def fetch(sources, targets, sems):
    copies = [
        pltpu.make_async_copy(source, target, sems.at[i])
        for i, (source, target) in enumerate(zip(sources, targets))
    ]
    for copy in copies:
        copy.start()
    return copies


def ask_kernel(*refs):
    sources, out_ref, targets, sems = refs[:3], refs[3], refs[4:7], refs[7]
    for copy in fetch(sources, targets, sems):
        copy.wait()
    bc_ref, source_ref, reader_ref = targets
    steps = bc_ref.shape[0]
    slots = out_ref.shape[0]
    live_dev = source_ref.shape[1]
    readers = reader_ref.shape[1]
    zeros_l = jnp.zeros((live_dev, STATE), F32)
    place = (iota((live_dev, STATE), 0) + 1).astype(F32)
    parts = [bc_ref[t, 1, 0:live_dev, :].astype(F32) for t in range(steps)]
    parts += [place] + [zeros_l] * (SUB - steps - 1)
    data_l = jnp.concatenate(parts, 0)
    data_l = jnp.concatenate([data_l, jnp.zeros_like(data_l)], 1).astype(BF16)
    parts = [
        bc_ref[t % steps, 1, live_dev : live_dev + readers, :].astype(F32) for t in range(SUB)
    ]
    data_r = jnp.concatenate(parts, 0)
    data_r = jnp.concatenate([jnp.zeros_like(data_r), data_r], 1).astype(BF16)
    first_l = lax.div(source_ref[...], live_dev) * SUB
    first_r = reader_ref[...] * SUB
    tgt_l = jnp.concatenate([first_l + r for r in range(SUB)], 1)
    tgt_r = jnp.concatenate([first_r + r for r in range(SUB)], 1)
    pick_l = onehot(iota((slots, SUB * live_dev), 0) == tgt_l)
    pick_r = onehot(iota((slots, SUB * readers), 0) == tgt_r)
    out_ref[...] = (mm(pick_l, data_l) + mm(pick_r, data_r)).astype(BF16)


def state_kernel(*refs):
    sources, live_hbm, outs, targets = refs[:8], refs[8], refs[9:14], refs[14:22]
    live_ref, sems, xf = refs[22:]
    xc_ref, cum_ref, cumt_ref, dtt_ref, pack_ref = outs
    base = live_ref.shape[0] * STATE
    st_ref = pack_ref.at[base : base + 2 * STATE]
    chunk = live_ref.shape[0] // CHUNKS
    chunks = [slice(i * chunk, (i + 1) * chunk) for i in range(CHUNKS)]
    copies = fetch(
        sources + tuple(live_hbm.at[part] for part in chunks),
        targets + tuple(live_ref.at[part] for part in chunks),
        sems,
    )
    for copy in copies[:8]:
        copy.wait()
    len_ref, rawt_ref, decay_ref, bias_ref, cw_ref, cb_ref, bct_ref, x_ref = targets
    span, width = x_ref.shape
    heads = rawt_ref.shape[0]
    taps = cw_ref.shape[0]
    length = len_ref[0]
    xf[0:SUB, :] = jnp.zeros((SUB, width), F32)
    xf[SUB : SUB + span, :] = x_ref[...].astype(F32)
    square = iota((heads, heads), 0) == iota((heads, heads), 1)

    def column(row):
        return jnp.sum(jnp.where(square, row, 0.0), axis=1, keepdims=True)

    dtt = softplus(rawt_ref[...].astype(F32) + column(bias_ref[...]))
    dtt = jnp.where(iota((heads, span), 1) < length, dtt, 0.0)
    dtt_ref[...] = dtt
    tri = onehot(iota((span, span), 0) >= iota((span, span), 1))
    pieces = split3(dtt * -column(decay_ref[...]))
    cum_ref[...] = mm_nt(tri, pieces[0]) + mm_nt(tri, pieces[1]) + mm_nt(tri, pieces[2])
    cumt = mm_nt(pieces[0], tri) + mm_nt(pieces[1], tri) + mm_nt(pieces[2], tri)
    cumt_ref[...] = cumt
    weight = jnp.exp(cumt[:, span - 1 : span] - cumt) * dtt
    weight_hi, weight_lo = split2(weight)
    expand = expander(heads, width)
    weights = [cw_ref[k : k + 1, :].astype(F32) for k in range(taps)]
    block = 128
    total = jnp.zeros((STATE, width), F32)
    for start in range(0, span, block):
        part = slice(start, start + block)
        acc = cb_ref[...]
        for k in range(taps):
            first = SUB - taps + 1 + k + start
            acc = acc + xf[first : first + block, :] * weights[k]
        xc = silu(acc).astype(BF16)
        xc_ref[part, :] = xc
        wide = lax.dot_general(weight_hi[:, part], expand, TN, preferred_element_type=F32)
        wide = wide + lax.dot_general(
            weight_lo[:, part], expand, TN, preferred_element_type=F32
        )
        weighted = (xc.astype(F32) * wide).astype(BF16)
        total = total + mm(bct_ref[0, :, part], weighted)
    st_ref[0:STATE, :] = jnp.zeros((STATE, width), BF16)
    st_ref[STATE : 2 * STATE, :] = total.astype(BF16)
    row, col = iota((SUB, span), 0), iota((SUB, span), 1)
    tail = onehot((col == length - (taps - 1)) & (row == SUB - 1))
    tail = mm(tail, x_ref[...])
    row, col = iota((2 * SUB, span), 0), iota((2 * SUB, span), 1)
    both = mm(onehot(col == length - 2 + jnp.where(row < SUB, 0, 1)), x_ref[...])
    part = width // 4
    row = iota((SUB, part), 0)
    late = jnp.zeros((SUB, part), F32)
    for i in range(4):
        lanes = slice(i * part, (i + 1) * part)
        piece = jnp.where(row < 4, both[0:SUB, lanes], both[SUB:, lanes])
        late = jnp.where(jnp.bitwise_and(row, 3) == i, piece, late)
    late = jnp.concatenate([late] * 4, 1)
    base = base + 2 * STATE
    pack_ref[base : base + 2 * SUB, :] = jnp.concatenate([tail, late], 0).astype(BF16)
    unit = onehot(iota((STATE, STATE), 0) == iota((STATE, STATE), 1))
    for k in range(live_ref.shape[0]):
        if k % chunk == 0:
            copies[8 + k // chunk].wait()
        pack_ref[k * STATE : (k + 1) * STATE, :] = mm_nt(unit, live_ref[k]).astype(BF16)


def prompt_kernel(
    xc_ref,
    z_ref,
    bct_ref,
    cum_ref,
    cumt_ref,
    dtt_ref,
    skip_ref,
    g_ref,
    ss_ref,
    scores,
):
    span, width = xc_ref.shape
    heads = cum_ref.shape[1]
    block = 128
    ones = jnp.ones((SUB, block), BF16)
    lanes = iota((block, block), 1)
    causal = iota((block, block), 0) >= lanes
    for start in range(0, span, block):
        stop = start + block
        scores[:, 0:stop] = lax.dot_general(
            bct_ref[1, :, start:stop], bct_ref[0, :, 0:stop], TN, preferred_element_type=F32
        )
        square = jnp.zeros((block, block), F32)
        for lane in range(0, width, block):
            halves = []
            for half in range(2):
                head = lane * heads // width + half
                at = cum_ref[start:stop, head : head + 1]
                gap = jnp.where(causal, at - cumt_ref[head : head + 1, start:stop], -jnp.inf)
                near = scores[:, start:stop] * jnp.exp(gap) * dtt_ref[head : head + 1, start:stop]
                yhead = mm(near.astype(BF16), xc_ref[start:stop, lane : lane + block])
                if start:
                    gap = at - cumt_ref[head : head + 1, 0:start]
                    far = scores[:, 0:start] * jnp.exp(gap) * dtt_ref[head : head + 1, 0:start]
                    yhead = yhead + mm(far.astype(BF16), xc_ref[0:start, lane : lane + block])
                halves.append(yhead)
            y = jnp.where(lanes < block // 2, halves[0], halves[1])
            xin = xc_ref[start:stop, lane : lane + block].astype(F32)
            y = y + skip_ref[:, lane : lane + block] * xin
            gate = y * silu(z_ref[start:stop, lane : lane + block].astype(F32))
            g_ref[start:stop, lane : lane + block] = gate
            square = square + gate * gate
        hi, lo = split2(square)
        ss_ref[:, start:stop] = mm_nt(ones, hi) + mm_nt(ones, lo)


def answer_kernel(*refs):
    ask_ref, conv_ref, state_ref, out_ref, ys = refs
    base = ys.shape[0] // SUB * STATE
    width = ys.shape[1]
    prefix = state_ref[base : base + 2 * STATE, :]
    base = base + 2 * STATE
    ends = state_ref[base : base + 2 * SUB, :].astype(F32)
    tail, late = ends[0:SUB, :], ends[SUB:, 0 : width // 4]
    slots = ask_ref.shape[0]
    count = ys.shape[0]
    live_dev = count // SUB
    half = width // 2
    ask = ask_ref[...]
    down, lane = iota((slots, 1), 0), iota((1, slots), 1)
    in_slot = jnp.bitwise_and(down, SUB - 1)
    place = ask.astype(F32).reshape(slots // SUB, SUB, 2 * STATE)
    place = jnp.broadcast_to(place[:, 4:5, :], place.shape).reshape(slots, 2 * STATE)
    lane0 = onehot(iota((SUB, 2 * STATE), 1) == 0)
    across = mm_nt(lane0, place.astype(BF16))[0:1, :].astype(jnp.int32)
    back = (across - 1) * SUB + jnp.bitwise_and(lane, SUB - 1)
    got = mm(onehot(iota((count, 1), 0) == back), ask).astype(BF16)
    deep = GROUP_ROWS * STATE
    copy_of = jnp.bitwise_and(iota((1, deep), 1), STATE - 1)
    wide = mm(got, onehot(iota((2 * STATE, 1), 0) == copy_of))
    row, col = iota((count, 1), 0), iota((1, deep), 1)
    wanted = jnp.where(jnp.bitwise_and(row, SUB - 1) < 4, lax.div(row, SUB), -1)
    wanted = jnp.where(wanted >= 0, jnp.bitwise_and(wanted, GROUP_ROWS - 1), -1)
    wide = jnp.where(wanted == lax.div(col, STATE), wide, 0.0).astype(BF16)
    tall = GROUP_ROWS * SUB
    for group in range(live_dev // GROUP_ROWS):
        first = group * deep
        rows = slice(group * tall, (group + 1) * tall)
        ys[rows, :] = mm(wide[rows, :], state_ref[first : first + deep, :]).astype(BF16)
    place = place[:, 0:1].astype(jnp.int32)
    there = onehot(iota((1, count), 1) == (place - 1) * SUB + in_slot)
    live = mm(there, ys[...])
    kept = conv_ref.shape[0]
    conv_row = (in_slot - 4) * live_dev + place - 1
    conv_row = jnp.where((place > 0) & (in_slot >= 4), conv_row, -1)
    there = onehot(iota((1, kept), 1) == conv_row)
    live = (live + mm(there, conv_ref[...])).reshape(slots // SUB, SUB, width)
    live = live + tail[None]
    out_ref[:, 0:width] = live.reshape(slots, width).astype(BF16)
    new = mm(ask, prefix)
    new = jnp.where(in_slot < SUB // 2, new[:, 0:half], new[:, half:width])
    out_ref[:, width : width + half] = new.astype(BF16)
    part = late.shape[1]
    late = jnp.broadcast_to(late[None], (slots // SUB, SUB, part))
    out_ref[:, width + half :] = late.reshape(slots, part).astype(BF16)


def decode_kernel(
    live_dev,
    readers,
    got_ref,
    tgt_l_ref,
    tgt_r_ref,
    xz_ref,
    bc_ref,
    raw_ref,
    decay_ref,
    bias_ref,
    skip_ref,
    cw_ref,
    cb_ref,
    pre_ss_ref,
    g_ref,
    ss_ref,
):
    slots = got_ref.shape[0]
    steps, _, rows, width = xz_ref.shape
    heads = raw_ref.shape[0] // steps
    raws = raw_ref[...].astype(F32).T
    span = pre_ss_ref.shape[1]
    taps = cw_ref.shape[0]
    half = width // 2
    pick_l = onehot(iota((SUB * live_dev, slots), 1) == tgt_l_ref[...])
    pick_r = onehot(iota((SUB * readers, slots), 1) == tgt_r_ref[...])
    live = mm(pick_l, got_ref[:, 0:width])
    new = mm(pick_r, got_ref[:, width:])
    old = mm(pick_r[(SUB - 1) * readers :, :], got_ref[:, 0:width])

    def live_row(r):
        return live[r * live_dev : (r + 1) * live_dev, :]

    def new_row(r, first, last):
        return new[r * readers : (r + 1) * readers, first:last]

    def tail_row(r):
        return jnp.concatenate([new_row(r + i, half, half + width // 4) for i in range(4)], 1)

    first = []
    for t in range(steps):
        wide = jnp.concatenate([new_row(t, 0, half), new_row(t + 4, 0, half)], 1)
        first.append(jnp.concatenate([live_row(t), wide], 0))
    inputs = [
        jnp.concatenate([live_row(4), old], 0),
        jnp.concatenate([live_row(5), tail_row(0)], 0),
        jnp.concatenate([live_row(6), tail_row(4)], 0),
    ]
    inputs += [xz_ref[t, 0].astype(F32) for t in range(steps)]
    expand = expander(heads, width)
    weights = [cw_ref[k : k + 1, :].astype(F32) for k in range(taps)]
    dts, logs, bmats, cmats, xcs, gates = [], [], [], [], [], []
    for t in range(steps):
        acc = cb_ref[...]
        for k in range(taps):
            acc = acc + inputs[t + k] * weights[k]
        xcs.append(silu(acc).astype(BF16).astype(F32))
        dt = softplus(raws[:, t * heads : (t + 1) * heads] + bias_ref[...])
        dts.append(dt)
        decayed = -dt * decay_ref[...]
        logs.append(decayed if t == 0 else logs[-1] + decayed)
        bmats.append(bc_ref[t, 0].astype(F32))
        cmats.append(bc_ref[t, 1].astype(F32))
        y = spread(jnp.exp(logs[t]), expand) * first[t]
        for s in range(t + 1):
            score = jnp.sum(bmats[s] * cmats[t], axis=1, keepdims=True)
            factor = dts[s] * score
            if s < t:
                factor = jnp.exp(logs[t] - logs[s]) * factor
            else:
                factor = factor + skip_ref[...]
            y = y + spread(factor, expand) * xcs[s]
        gate = y * silu(xz_ref[t, 1].astype(F32))
        g_ref[t * rows : (t + 1) * rows, :] = gate
        gates.append(gate * gate)
    square = jnp.concatenate(gates, 0)
    hi, lo = split2(square)
    ones = jnp.ones((SUB, width), BF16)
    sums = mm_nt(ones, hi) + mm_nt(ones, lo)
    lanes = ss_ref.shape[2]
    pad = -sums.shape[1] % lanes
    sums = jnp.concatenate([pre_ss_ref[...], sums, jnp.zeros((SUB, pad), F32)], 1)
    parts = [sums[0:1, i : i + lanes] for i in range(0, sums.shape[1], lanes)]
    parts += [jnp.zeros((SUB - len(parts), lanes), F32)]
    ss_ref[...] = jnp.broadcast_to(jnp.concatenate(parts, 0)[None], ss_ref.shape)


def finish_kernel(width_all, ss_ref, pre_ref, step_ref, gain_ref, pre_out_ref, step_out_ref):
    total = ss_ref[0]
    for i in range(1, ss_ref.shape[0]):
        total = total + ss_ref[i]
    scale = lax.rsqrt(total / width_all + EPS)
    gain = gain_ref[...]
    span = pre_ref.shape[0]
    block = 128

    def column(first, rows):
        row = scale[first // block : first // block + 1, :]
        diag = iota((rows, block), 0) == iota((rows, block), 1)
        return jnp.sum(jnp.where(diag, row, 0.0), axis=1, keepdims=True)

    for start in range(0, span, block):
        part = slice(start, start + block)
        pre_out_ref[part, :] = (pre_ref[part, :] * column(start, block) * gain).astype(BF16)
    count = step_ref.shape[0]
    for start in range(0, count, block):
        rows = min(block, count - start)
        part = slice(start, start + rows)
        step_out_ref[part, :] = (step_ref[part, :] * column(span + start, rows) * gain).astype(
            BF16
        )


def params(limit=24 * 1024 * 1024, **more):
    return pltpu.CompilerParams(vmem_limit_bytes=limit, **more)


def cost(flops, moved, special=0):
    return pl.CostEstimate(flops=flops, bytes_accessed=moved, transcendentals=special)


def vmem():
    return pl.BlockSpec(memory_space=pltpu.VMEM)


def hbm():
    return pl.BlockSpec(memory_space=pltpu.HBM)


def shape(dims, kind):
    return jax.ShapeDtypeStruct(dims, kind)


def per_device(
    pre_x,
    pre_z,
    pre_bc,
    pre_raw,
    prompt_len,
    live_state,
    live_conv,
    source,
    reader,
    step_xz,
    step_bc,
    step_raw,
    decay,
    dt_bias,
    conv_weight,
    conv_bias,
    skip,
    norm_gain,
):
    _, span, width = pre_x.shape
    mp = lax.axis_size("mp")
    gens = lax.axis_size("gen")
    width_all = width * mp
    live_dev = source.shape[0]
    readers = reader.shape[0]
    heads = pre_raw.shape[2]
    steps, _, rows, _ = step_xz.shape
    slots = gens * SUB
    offset = jnp.arange(SUB, dtype=jnp.int32)[:, None]
    tgt_l = SUB * (source // live_dev)[None, :] + offset
    tgt_r = SUB * reader[None, :] + offset

    conv_rows = jnp.transpose(live_conv, (1, 0, 2)).reshape(-1, width)
    bct = jnp.swapaxes(pre_bc[0], 1, 2)
    dma = pltpu.SemaphoreType.DMA

    def staged(*arrays):
        return [pltpu.VMEM(array.shape, array.dtype) for array in arrays]

    operands = (step_bc, source[None], reader[None])
    ask = pl.pallas_call(
        ask_kernel,
        out_shape=shape((slots, 2 * STATE), BF16),
        in_specs=[hbm()] * len(operands),
        out_specs=vmem(),
        scratch_shapes=staged(*operands) + [dma((len(operands),))],
        compiler_params=params(WHOLE),
        cost_estimate=cost(2 * slots * 384 * 128, 300000),
        name="ask",
    )(*operands)
    lanes = ask.shape[1]
    asked = lax.all_to_all(
        ask.reshape(gens, SUB, lanes), "gen", split_axis=0, concat_axis=0, tiled=True
    ).reshape(slots, lanes)

    live = live_state.reshape(live_dev, width, STATE)
    operands = (
        prompt_len,
        pre_raw[0].T,
        decay[None],
        dt_bias[None],
        conv_weight,
        conv_bias[None],
        bct,
        pre_x[0],
    )
    xconv, cum, cumt, dtt, pack = pl.pallas_call(
        state_kernel,
        out_shape=(
            shape((span, width), BF16),
            shape((span, heads), F32),
            shape((heads, span), F32),
            shape((heads, span), F32),
            shape((live_dev * STATE + 2 * STATE + 2 * SUB, width), BF16),
        ),
        in_specs=[hbm()] * (len(operands) + 1),
        out_specs=(vmem(),) * 5,
        scratch_shapes=[pltpu.SMEM((1,), jnp.int32)]
        + staged(*operands[1:], live)
        + [dma((len(operands) + CHUNKS,)), pltpu.VMEM((span + SUB, width), F32)],
        compiler_params=params(WHOLE),
        cost_estimate=cost(2 * 10 * span * span * 64, 8000000, span * width * 2),
        name="state",
    )(*operands, live)

    operands = (asked, conv_rows)
    answer = pl.pallas_call(
        answer_kernel,
        out_shape=shape((slots, width + width // 2 + width // 4), BF16),
        in_specs=[vmem()] * (len(operands) + 1),
        out_specs=vmem(),
        scratch_shapes=[pltpu.VMEM((live_dev * SUB, width), BF16)],
        compiler_params=params(),
        cost_estimate=cost(2 * slots * 512 * 1024, 4000000),
        name="answer",
    )(*operands, pack)
    lanes = answer.shape[1]
    got = lax.all_to_all(
        answer.reshape(gens, SUB, lanes), "gen", split_axis=0, concat_axis=0, tiled=True
    ).reshape(slots, lanes)

    pre_gate, pre_ss = pl.pallas_call(
        prompt_kernel,
        out_shape=(
            shape((span, width), F32),
            shape((SUB, span), F32),
        ),
        in_specs=[vmem()] * 7,
        out_specs=(vmem(),) * 2,
        scratch_shapes=[pltpu.VMEM((128, span), F32)],
        compiler_params=params(),
        cost_estimate=cost(2 * heads * span * span * 128, 2500000, heads * span * span),
        name="prompt",
    )(xconv, pre_z[0], bct, cum, cumt, dtt, jnp.repeat(skip, width // heads)[None])

    count = steps * rows
    step_gate, sums = pl.pallas_call(
        lambda *refs: decode_kernel(live_dev, readers, *refs),
        out_shape=(shape((count, width), F32), shape((mp, SUB, 128), F32)),
        in_specs=[vmem()] * 12,
        out_specs=(vmem(), vmem()),
        compiler_params=params(),
        cost_estimate=cost(2 * 384 * 512 * 512, 2500000),
        name="decode",
    )(
        got,
        tgt_l.reshape(-1, 1),
        tgt_r.reshape(-1, 1),
        step_xz,
        step_bc,
        jnp.swapaxes(step_raw, 1, 2).reshape(steps * heads, rows),
        decay[None],
        dt_bias[None],
        skip[None],
        conv_weight,
        conv_bias[None],
        pre_ss,
    )
    sums = lax.all_to_all(sums, "mp", split_axis=0, concat_axis=0, tiled=True)

    prefill_out, decoded = pl.pallas_call(
        lambda *refs: finish_kernel(width_all, *refs),
        out_shape=(shape((span, width), BF16), shape((count, width), BF16)),
        in_specs=[vmem()] * 4,
        out_specs=(vmem(), vmem()),
        compiler_params=params(),
        cost_estimate=cost(1000000, 2500000),
        name="finish",
    )(sums, pre_gate, step_gate, norm_gain[None])
    return (prefill_out[None], decoded.reshape(steps, rows, width))


def solution(mesh):
    placed = (
        P("gen", None, "mp"),
        P("gen", None, "mp"),
        P("gen", None, None, "mp"),
        P("gen", None, "mp"),
        P("gen"),
        P("gen", "mp", None, None),
        P("gen", None, "mp"),
        P("gen"),
        P("gen"),
        P(None, None, "gen", "mp"),
        P(None, None, "gen", "mp"),
        P(None, "gen", "mp"),
        P("mp"),
        P("mp"),
        P(None, "mp"),
        P("mp"),
        P("mp"),
        P("mp"),
    )
    return jax.shard_map(
        per_device,
        mesh=mesh,
        in_specs=placed,
        out_specs=(P("gen", None, "mp"), P(None, "gen", "mp")),
        check_vma=False,
    )
```
